256 devices in a mesh: row: 2 (over core), col: 128 (over y, x, z).
Axes of the slice: x: 4, y: 4, z: 8, core: 2. Of those that a mesh axis runs over, the one named last changes fastest.
Arguments:
- observed: bfloat16 [1024, 16, 16384], P(None, 'row', 'col'), may hold values from -40 to 40
- library: bfloat16 [1024, 256], P('col'), may hold values from -0.1875 to 0.1875
Outputs:
- abundance: float32 [256, 16, 16384], P(None, 'row', 'col')
The draws below stay inside these ranges and needn't reach their ends.
All inputs are finite; a program needn't handle non-finite values.
Results may differ from the reference program's by a relative error of at most 0.0024.
Values may be sent and summed in bfloat16 or wider, within the bound.
A program may use at most 128 MiB of HBM per device.

```python
import jax
import jax.numpy as jnp
from jax import lax

CHANNELS = 1024
ENDMEMBERS = 256
ITERS = 3
ROWS = 16
COLS = 16384


def draw_observed(key, part):
    subkeys = jax.random.split(jax.random.fold_in(key, 17), 4)
    shape = (CHANNELS, ROWS, COLS)
    noise_base = jax.random.normal(subkeys[0], shape, jnp.float32)
    region_low, region_high = (jnp.log(1.0 / 3.0), jnp.log(3.0))
    channel_scale = jnp.exp(jax.random.uniform(subkeys[1], (CHANNELS, 1, 1), jnp.float32, jnp.log(0.5), jnp.log(2.0)))
    region_table = jnp.exp(jax.random.uniform(subkeys[2], (COLS // 32,), jnp.float32, region_low, region_high))
    region_scale = jnp.repeat(region_table, 32).reshape(1, 1, COLS)
    pixel_scale = jax.random.uniform(subkeys[3], (1, ROWS, COLS), jnp.float32, 0.5, 1.5)
    return jnp.clip(noise_base * channel_scale * region_scale * pixel_scale, -40.0, 40.0).astype(jnp.bfloat16)


def steps_of(rng, dims, cuts, smallest, high):
    def one(dim, shards_of):
        draws = jax.random.uniform(jax.random.fold_in(jax.random.fold_in(rng, 6), dim), (shards_of,), jnp.float32, smallest / len(cuts), high / len(cuts))
        return jnp.repeat(jnp.exp(draws), dims[dim] // shards_of).reshape((-1,) + (1,) * (len(dims) - dim - 1))

    level = one(*cuts[0])
    for cut in cuts[1:]:
        level = level * one(*cut)
    return level


def noise(rng, extent, deviation, limit, shards=(), held_as=jnp.bfloat16):
    result = deviation * jax.random.normal(rng, extent, jnp.float32)
    if shards:
        result = result * steps_of(rng, extent, shards, -0.22, 0.18)
    return jnp.clip(result, -limit, limit).astype(held_as)


def setup_inputs(seed: int = 0) -> dict:
    splits = jax.random.split(jax.random.key(seed), 3)
    observed = draw_observed(jax.random.fold_in(splits[2], 71), 0)
    library = noise(splits[1], (CHANNELS, ENDMEMBERS), CHANNELS ** -0.5, 0.1875, ((0, 128),))
    return {"observed": observed, "library": library}


prox_tau = 8.0
weight_sparse = 0.3
weight_tv = 1.0

def soften(values_in, threshold):
    return values_in - jnp.clip(values_in, -threshold, threshold)

def gradient(field_in):
    zero_row = jnp.zeros_like(field_in[:, :1, :])
    zero_col = jnp.zeros_like(field_in[:, :, :1])
    down_diff = jnp.concatenate([field_in[:, 1:, :] - field_in[:, :-1, :], zero_row], axis=1)
    right_diff = jnp.concatenate([field_in[:, :, 1:] - field_in[:, :, :-1], zero_col], axis=2)
    return (down_diff, right_diff)

def adjoint(down_arg, right_arg):
    zero_row = jnp.zeros_like(down_arg[:, :1, :])
    zero_col = jnp.zeros_like(right_arg[:, :, :1])
    down_kept = jnp.concatenate([down_arg[:, :-1, :], zero_row], axis=1)
    right_kept = jnp.concatenate([right_arg[:, :, :-1], zero_col], axis=2)
    upper_part = jnp.concatenate([zero_row, down_kept[:, :-1, :]], axis=1)
    side_part = jnp.concatenate([zero_col, right_kept[:, :, :-1]], axis=2)
    return upper_part - down_kept + (side_part - right_kept)

def solve_step(library, inverse, estimate, data_var, data_dual, sparse_var, sparse_dual, diverge):
    packed = (data_var - data_dual).astype(jnp.bfloat16).reshape(CHANNELS, -1)
    projected = jnp.dot(library.T.astype(jnp.float32), packed.astype(jnp.float32), preferred_element_type=jnp.float32).reshape(estimate.shape)
    rhs_field = projected + (sparse_var - sparse_dual) + prox_tau * estimate - diverge
    solved = jnp.dot(inverse, rhs_field.reshape(ENDMEMBERS, -1), precision=lax.Precision.HIGHEST)
    return solved.reshape(estimate.shape)

def reference(observed, library):
    gram_matrix = jnp.dot(library.T.astype(jnp.float32), library.astype(jnp.float32), preferred_element_type=jnp.float32)
    identity = jnp.eye(ENDMEMBERS, dtype=jnp.float32)
    system = gram_matrix + (1.0 + prox_tau) * identity
    factor = jnp.linalg.cholesky(system)
    inverse = jax.scipy.linalg.cho_solve((factor, True), identity)
    observed_wide = observed.astype(jnp.float32)
    data_var = observed_wide
    data_dual = jnp.zeros_like(observed_wide)
    estimate = jnp.zeros((ENDMEMBERS, ROWS, COLS), jnp.float32)
    sparse_var = jnp.zeros_like(estimate)
    sparse_dual = jnp.zeros_like(estimate)
    down_var = jnp.zeros_like(estimate)
    right_var = jnp.zeros_like(estimate)
    down_dual = jnp.zeros_like(estimate)
    right_dual = jnp.zeros_like(estimate)
    diverge = jnp.zeros_like(estimate)
    penalty = jnp.float32(1.0)
    for iteration in range(ITERS):
        estimate = solve_step(library, inverse, estimate, data_var, data_dual, sparse_var, sparse_dual, diverge)
        half_estimate = estimate.astype(jnp.bfloat16).reshape(ENDMEMBERS, -1)
        modelled = jnp.dot(library.astype(jnp.float32), half_estimate.astype(jnp.float32), preferred_element_type=jnp.float32).reshape(observed.shape)
        down_diff, right_diff = gradient(estimate)
        data_var = (observed_wide + penalty * (modelled + data_dual)) / (1.0 + penalty)
        new_sparse = jnp.maximum(estimate + sparse_dual - weight_sparse / penalty, 0.0)
        new_down = soften(down_diff + down_dual, weight_tv / penalty)
        new_right = soften(right_diff + right_dual, weight_tv / penalty)
        data_dual = data_dual + modelled - data_var
        sparse_dual = sparse_dual + estimate - new_sparse
        down_dual = down_dual + down_diff - new_down
        right_dual = right_dual + right_diff - new_right
        primal = jnp.sum((modelled - data_var) ** 2) + jnp.sum((estimate - new_sparse) ** 2) + jnp.sum((down_diff - new_down) ** 2) + jnp.sum((right_diff - new_right) ** 2)
        dual_sum = jnp.sum((new_sparse - sparse_var) ** 2) + jnp.sum((new_down - down_var) ** 2) + jnp.sum((new_right - right_var) ** 2)
        sparse_var, down_var, right_var = (new_sparse, new_down, new_right)
        following = penalty * jnp.sqrt(jnp.sqrt((primal + 1.0) / (penalty * penalty * dual_sum + 1.0)))
        rescale = penalty / following
        data_dual = data_dual * rescale
        sparse_dual = sparse_dual * rescale
        down_dual = down_dual * rescale
        right_dual = right_dual * rescale
        penalty = following
        diverge = adjoint(down_diff - down_var + down_dual, right_diff - right_var + right_dual)
    estimate = solve_step(library, inverse, estimate, data_var, data_dual, sparse_var, sparse_dual, diverge)
    return estimate
```

```python
import functools

import jax
import jax.numpy as jnp
from jax import lax
from jax.experimental import pallas as pl
from jax.experimental.pallas import tpu as pltpu
from jax.sharding import PartitionSpec as P

ITERS = 3
PROX = 8.0
WEIGHT_SPARSE = 0.3
WEIGHT_TV = 1.0
MESH = pl.DeviceIdType.MESH
F32 = jnp.float32
BF16 = jnp.bfloat16
VMEM = pl.BlockSpec(memory_space=pltpu.VMEM)


def depth_of(cols):
    return 8 if cols == 128 else 2


def slot_of(col, depth, cols):
    plane, z = col // depth, col % depth
    half = depth // 2
    return (z % 2) * (cols // 2) + plane * half + z // 2


def gather_kernel(cols, shard_ref, out_ref, packed, send_sem, recv_sem):
    depth = depth_of(cols)
    planes, half = cols // depth, depth // 2
    row, col = lax.axis_index("row"), lax.axis_index("col")
    plane, z = lax.div(col, depth), lax.rem(col, depth)
    parity = lax.rem(z, 2)

    def z_peer(step):
        return (row, plane * depth + lax.rem(z + step, depth))

    def plane_peer(step):
        return (row, lax.rem(plane + step, planes) * depth + z)

    core_peer = (1 - row, col)
    peers = [z_peer(s) for s in range(1, depth)] + [plane_peer(s) for s in range(1, planes)] + [core_peer]
    barrier = pltpu.get_barrier_semaphore()
    for peer in peers:
        pl.semaphore_signal(barrier, inc=1, device_id=peer, device_id_type=MESH)
    shard = shard_ref[...].astype(F32)
    packed[...] = jnp.concatenate([shard[:, :128], shard[:, 128:]], axis=0).astype(BF16)
    mine = parity * (cols // 2) + plane * half + lax.div(z, 2)
    pl.semaphore_wait(barrier, len(peers))

    @pl.when(row == parity)
    def _():
        out_ref[mine] = packed[...]
        for step in range(1, depth):
            pltpu.make_async_remote_copy(
                src_ref=packed,
                dst_ref=out_ref.at[mine],
                send_sem=send_sem.at[0],
                recv_sem=recv_sem.at[0],
                device_id=z_peer(step),
                device_id_type=MESH,
            ).start()
        if half > 1:
            got = out_ref.at[pl.ds(0, half - 1)]
            pltpu.make_async_copy(got, got, recv_sem.at[0]).wait()

    @pl.when(row != parity)
    def _():
        got = out_ref.at[pl.ds(0, half)]
        pltpu.make_async_copy(got, got, recv_sem.at[0]).wait()

    block = out_ref.at[pl.ds(row * (cols // 2) + plane * half, half)]
    for step in range(1, planes):
        pltpu.make_async_remote_copy(
            src_ref=block,
            dst_ref=block,
            send_sem=send_sem.at[1],
            recv_sem=recv_sem.at[1],
            device_id=plane_peer(step),
            device_id_type=MESH,
        ).start()
    got = out_ref.at[pl.ds(0, half * (planes - 1))]
    pltpu.make_async_copy(got, got, recv_sem.at[1]).wait()
    own_half = out_ref.at[pl.ds(row * (cols // 2), cols // 2)]
    swap = pltpu.make_async_remote_copy(
        src_ref=own_half,
        dst_ref=own_half,
        send_sem=send_sem.at[2],
        recv_sem=recv_sem.at[2],
        device_id=core_peer,
        device_id_type=MESH,
    )
    swap.start()

    @pl.when(row == parity)
    def _():
        sent = out_ref.at[pl.ds(0, depth - 1)]
        pltpu.make_async_copy(sent, sent, send_sem.at[0]).wait()

    pltpu.make_async_copy(got, got, send_sem.at[1]).wait()
    swap.wait()


def gather_library(library, cols):
    return pl.pallas_call(
        functools.partial(gather_kernel, cols),
        out_shape=jax.ShapeDtypeStruct((cols, 16, 128), BF16),
        in_specs=[VMEM],
        out_specs=VMEM,
        scratch_shapes=[
            pltpu.VMEM((16, 128), BF16),
            pltpu.SemaphoreType.DMA((3,)),
            pltpu.SemaphoreType.DMA((3,)),
        ],
        compiler_params=pltpu.CompilerParams(collective_id=0, has_side_effects=True),
        name="gather_library",
    )(library)


def small_inverse(m):
    def inv2(q):
        (a, b), (c, d) = q
        scale = 1.0 / (a * d - b * c)
        return [[d * scale, -b * scale], [-c * scale, a * scale]]

    def mul(x, y):
        return [[x[i][0] * y[0][j] + x[i][1] * y[1][j] for j in range(2)] for i in range(2)]

    def sub(x, y):
        return [[x[i][j] - y[i][j] for j in range(2)] for i in range(2)]

    a = [r[:2] for r in m[:2]]
    b = [r[2:] for r in m[:2]]
    c = [r[:2] for r in m[2:]]
    d = [r[2:] for r in m[2:]]
    ai = inv2(a)
    cai = mul(c, ai)
    aib = mul(ai, b)
    si = inv2(sub(d, mul(cai, b)))
    right = mul(aib, si)
    low = mul(si, cai)
    top = [[ai[i][j] + (right[i][0] * cai[0][j] + right[i][1] * cai[1][j]) for j in range(2)] for i in range(2)]
    return [
        top[0] + [-v for v in right[0]],
        top[1] + [-v for v in right[1]],
        [-v for v in low[0]] + si[0],
        [-v for v in low[1]] + si[1],
    ]


def eliminate(matrix):
    size, step = 128, 4
    groups = [matrix[8 * g : 8 * g + 8, :] for g in range(size // 8)]
    lane = lax.broadcasted_iota(jnp.int32, (8, size), 1)
    place = lax.broadcasted_iota(jnp.int32, (8, size), 0)
    full = (8, size)
    for first in range(0, size, step):
        home, shift = first // 8, first % 8
        cols = [
            [jnp.broadcast_to(g[:, first + a : first + a + 1], full) for a in range(step)] for g in groups
        ]
        pivot = [
            [jnp.broadcast_to(cols[home][b][shift + a : shift + a + 1, :], full) for b in range(step)]
            for a in range(step)
        ]
        turned = small_inverse(pivot)
        inside = (lane >= first) & (lane < first + step)
        rows = []
        for a in range(step):
            line = jnp.broadcast_to(groups[home][shift + a : shift + a + 1, :], full)
            line = jnp.where(inside, 0.0, line)
            rows.append(jnp.where(lane == first + a, 1.0, line))
        fresh = []
        for a in range(step):
            total = turned[a][0] * rows[0] + turned[a][1] * rows[1]
            fresh.append(total + (turned[a][2] * rows[2] + turned[a][3] * rows[3]))
        nxt = []
        for g, group in enumerate(groups):
            c = cols[g]
            kept = jnp.where(inside, 0.0, group)
            value = kept - (c[0] * fresh[0] + c[1] * fresh[1]) - (c[2] * fresh[2] + c[3] * fresh[3])
            if g == home:
                for a in range(step):
                    value = jnp.where(place == shift + a, fresh[a], value)
            nxt.append(value)
        groups = nxt
    return jnp.concatenate(groups, axis=0)


def exact_dot(a, b, dims):
    return lax.dot_general(a, b, (dims, ((), ())), precision=lax.Precision.HIGHEST, preferred_element_type=F32)


def split2(x):
    high = x.astype(BF16)
    return high, (x - high.astype(F32)).astype(BF16)


def setup_kernel(cols, obs_ref, lib_ref, inv_ref, gram_ref, proj_ref, square_ref, lib, wide):
    depth = depth_of(cols)
    channels = 8 * cols
    for pair in range(cols // 2):
        one = lib_ref[slot_of(2 * pair, depth, cols)].astype(F32)
        two = lib_ref[slot_of(2 * pair + 1, depth, cols)].astype(F32)
        lib[16 * pair : 16 * pair + 16, 0:128] = jnp.concatenate([one[0:8], two[0:8]], axis=0).astype(BF16)
        lib[16 * pair : 16 * pair + 16, 128:256] = jnp.concatenate([one[8:16], two[8:16]], axis=0).astype(BF16)
    library = lib[...]
    gram = lax.dot_general(library, library, (((0,), (0,)), ((), ())), preferred_element_type=F32)
    high, low = split2(gram)
    gram_ref[0:256, :] = high
    gram_ref[256:512, :] = low
    same = lax.broadcasted_iota(jnp.int32, (256, 256), 0) == lax.broadcasted_iota(jnp.int32, (256, 256), 1)
    system = gram + jnp.where(same, 1.0 + PROX, 0.0)

    a11, a12 = system[:128, :128], system[:128, 128:]
    a21, a22 = system[128:, :128], system[128:, 128:]
    x = eliminate(a11)
    y = exact_dot(x, a12, ((1,), (0,)))
    z = eliminate(a22 - exact_dot(a21, y, ((1,), (0,))))
    b12 = -exact_dot(y, z, ((1,), (0,)))
    b11 = x - exact_dot(b12, y, ((1,), (1,)))
    b21 = -exact_dot(z, y, ((1,), (1,)))
    inv_ref[0:128, 0:128] = b11
    inv_ref[0:128, 128:256] = b12
    inv_ref[128:256, 0:128] = b21
    inv_ref[128:256, 128:256] = z

    def widen(k, total):
        base = pl.multiple_of(k * 16, 16)
        part = obs_ref[pl.ds(base, 16)].astype(F32)
        wide[pl.ds(pl.multiple_of(base * 8, 128), 128), :] = part.reshape(128, 128)
        return total + jnp.sum(part * part, axis=0)

    square_ref[...] = lax.fori_loop(0, channels // 16, widen, jnp.zeros((8, 128), F32))
    flip = lax.axis_index("row") == 1

    def project(i, carry):
        source = jnp.where(flip, 7 - i, i)
        part = wide[pl.ds(source, channels, stride=8), :].astype(BF16)
        proj_ref[pl.ds(pl.multiple_of(i * 128, 128), 128), :] = lax.dot_general(
            part, lib[...], (((0,), (0,)), ((), ())), preferred_element_type=F32
        )
        return carry

    lax.fori_loop(0, 8, project, 0)


def set_up(observed, gathered, cols):
    channels = 8 * cols
    return pl.pallas_call(
        functools.partial(setup_kernel, cols),
        out_shape=[
            jax.ShapeDtypeStruct((256, 256), F32),
            jax.ShapeDtypeStruct((512, 256), BF16),
            jax.ShapeDtypeStruct((1024, 256), F32),
            jax.ShapeDtypeStruct((8, 128), F32),
        ],
        in_specs=[VMEM, VMEM],
        out_specs=[VMEM] * 4,
        scratch_shapes=[pltpu.VMEM((channels, 256), BF16), pltpu.VMEM((channels * 8, 128), F32)],
        compiler_params=pltpu.CompilerParams(vmem_limit_bytes=24 * 2**20),
        name="set_up",
    )(observed, gathered)


CHUNK = 32
PAD = 136


def fold(x):
    total = None
    for k in range(x.shape[0] // 8):
        for half in range(2):
            part = x[8 * k : 8 * k + 8, 128 * half : 128 * half + 128]
            total = part if total is None else total + part
    return total


def iterate_kernel(
    cols,
    inv_ref,
    gram_ref,
    proj_ref,
    square_ref,
    out_ref,
    est,
    part_a,
    part_b,
    rim_send,
    rim_left,
    rim_right,
    halo,
    ghost,
    sparse_var,
    sparse_dual,
    down_var,
    down_dual,
    down_arg,
    right_var,
    right_dual,
    right_arg,
    mix,
    gram_mix,
    inv3,
    sums,
    near,
    far,
    halo_sem,
    rim_sem,
    sum_sem,
):
    depth = depth_of(cols)
    planes = cols // depth
    row, col = lax.axis_index("row"), lax.axis_index("col")
    plane, z = lax.div(col, depth), lax.rem(col, depth)
    core_peer = (1 - row, col)
    left = (row, lax.rem(col + cols - 1, cols))
    right = (row, lax.rem(col + 1, cols))
    here = z * 2 + row
    pack = 2 * depth

    def near_peer(step):
        other = lax.rem(here + step, pack)
        return (lax.rem(other, 2), plane * depth + lax.div(other, 2))

    def far_peer(step):
        return (row, lax.rem(plane + step, planes) * depth + z)

    peers = (
        [near_peer(s) for s in range(1, pack)] + [far_peer(s) for s in range(1, planes)] + [left, right, core_peer]
    )
    barrier = pltpu.get_barrier_semaphore()
    for peer in peers:
        pl.semaphore_signal(barrier, inc=1, device_id=peer, device_id_type=MESH)

    high, low = split2(inv_ref[...])
    inv3[0:256, :] = high
    inv3[256:512, :] = low
    inv3[512:768, :] = high

    def rows_of(x):
        return pl.ds(pl.multiple_of(x * 128, 128), 128)

    def stacked(x):
        one, two = split2(x)
        return jnp.concatenate([one, one, two], axis=1)

    def solve(x):
        return jnp.dot(stacked(x), inv3[...], preferred_element_type=F32)

    def solve_turned(x):
        one, two = split2(x)
        dims = (((1,), (1,)), ((), ()))
        total = lax.dot_general(inv3[0:256, :], one, dims, preferred_element_type=F32)
        total = total + lax.dot_general(inv3[256:512, :], one, dims, preferred_element_type=F32)
        return total + lax.dot_general(inv3[0:256, :], two, dims, preferred_element_type=F32)

    def send_halo(turn, slot, field):
        copy = pltpu.make_async_remote_copy(
            src_ref=field.at[rows_of(7)],
            dst_ref=halo.at[turn, slot],
            send_sem=halo_sem.at[0, turn, slot],
            recv_sem=halo_sem.at[1, turn, slot],
            device_id=core_peer,
            device_id_type=MESH,
        )
        copy.start()
        return copy

    def send_rims(turn):
        used = 8 if turn == 0 else 16
        to_left = pltpu.make_async_remote_copy(
            src_ref=rim_send.at[turn, 0, pl.ds(0, used)],
            dst_ref=rim_right.at[turn, pl.ds(0, used)],
            send_sem=rim_sem.at[0, turn, 0],
            recv_sem=rim_sem.at[1, turn, 0],
            device_id=left,
            device_id_type=MESH,
        )
        to_right = pltpu.make_async_remote_copy(
            src_ref=rim_send.at[turn, 1, pl.ds(0, used)],
            dst_ref=rim_left.at[turn, pl.ds(0, used)],
            send_sem=rim_sem.at[0, turn, 1],
            recv_sem=rim_sem.at[1, turn, 1],
            device_id=right,
            device_id_type=MESH,
        )
        to_left.start()
        to_right.start()
        return [to_left, to_right]

    def put_rims(turn, i, slot, value):
        rim_send[turn, 0, pl.ds(8 * slot + i, 1), :] = value[0:1, :]
        rim_send[turn, 1, pl.ds(8 * slot + i, 1), :] = value[127:128, :]

    for i in range(8):
        value = solve(proj_ref[128 * i : 128 * i + 128, :])
        part_a[128 * i : 128 * i + 128, :] = value
        put_rims(0, i, 0, value)

    pl.semaphore_wait(barrier, len(peers))
    rim_copies = send_rims(0)
    halo_copies = [send_halo(0, 0, part_a)]

    def start_sums(turn, stage):
        buffer = (near, far)[stage]
        peer_of, count = ((near_peer, pack), (far_peer, planes))[stage]
        index = (here, plane)[stage]
        for step in range(1, count):
            pltpu.make_async_remote_copy(
                src_ref=sums.at[turn, stage],
                dst_ref=buffer.at[turn, pl.ds(index, 1)],
                send_sem=sum_sem.at[0, turn, stage],
                recv_sem=sum_sem.at[1, turn, stage],
                device_id=peer_of(step),
                device_id_type=MESH,
            ).start()

    def wait_sums(turn, stage, which):
        buffer = (near, far)[stage]
        count = (pack, planes)[stage]
        got = buffer.at[turn, pl.ds(0, count - 1)]
        pltpu.make_async_copy(got, got, sum_sem.at[which, turn, stage]).wait()

    first_col = jnp.where(col == 0, 1.0, 0.0).astype(F32)
    last_col = jnp.where(col == cols - 1, 1.0, 0.0).astype(F32)
    lanes = lax.broadcasted_iota(jnp.int32, (1, 128), 1)
    penalty, rescale, carry_c, carry_s = 1.0, 0.0, 0.0, 0.0

    def scalar(x):
        return x if isinstance(x, float) else x[0, 0]

    for turn in range(ITERS):
        start = turn == 0
        old_c, old_s = carry_c, carry_s
        pc_v = penalty * old_c
        sigma_v = 1.0 - pc_v * old_s
        share_v = 1.0 / (1.0 + penalty)
        carry_s = 1.0 + old_c * old_s
        bound, cut = scalar(WEIGHT_TV / penalty), scalar(WEIGHT_SPARSE / penalty)
        pc, sigma, scale_c = scalar(pc_v), scalar(sigma_v), scalar(old_c)
        share, ratio, scale_s = scalar(share_v), scalar(penalty * share_v), scalar(carry_s)
        factor = scalar(rescale)
        for copy in rim_copies + halo_copies:
            copy.wait()

        def combined(a, b):
            return a if start else a + factor * b

        def place(i, carry):
            value = combined(part_a[rows_of(i), :], part_b[rows_of(i), :])
            est[i, 0:128, :] = value
            return carry

        lax.fori_loop(0, 8, place, 0)
        est[8, 0:128, :] = combined(halo[turn, 0], halo[turn, 1])
        own_first = combined(rim_send[turn, 0, 0:8, :], rim_send[turn, 0, 8:16, :])
        own_last = combined(rim_send[turn, 1, 0:8, :], rim_send[turn, 1, 8:16, :])
        from_right = combined(rim_right[turn, 0:8, :], rim_right[turn, 8:16, :])
        from_left = combined(rim_left[turn, 0:8, :], rim_left[turn, 8:16, :])
        from_right = jnp.where(last_col > 0.0, own_last, from_right)
        from_left = jnp.where(first_col > 0.0, own_first, from_left)
        for i in range(8):
            est[i, 128:129, :] = from_right[i : i + 1, :]

        g_diff = own_first - from_left
        g_sum = g_diff if start else g_diff + factor * ghost[...]
        g_dual = jnp.clip(g_sum, -bound, bound)
        g_arg = g_diff - (g_sum - g_dual)
        ghost[...] = g_dual
        for i in range(8):
            right_arg[i, 7:8, :] = g_arg[i : i + 1, :]
            right_dual[i, 7:8, :] = g_dual[i : i + 1, :]

        def update(i, off, totals):
            at = pl.ds(off, CHUNK)
            shifted = pl.ds(off + 8, CHUNK)
            flat = pl.ds(pl.multiple_of(i * 128 + off, CHUNK), CHUNK)
            primal, dual, data = totals
            e = est[i, at, :]
            half = e.astype(BF16)
            gh = jnp.dot(jnp.concatenate([half, half], axis=1), gram_ref[...], preferred_element_type=F32)
            h = half.astype(F32)
            w = proj_ref[flat, :]
            if start:
                data = data + fold(h * (gh - 2.0 * w))
                mix[flat, :] = h
                gram_mix[flat, :] = gh
            else:
                y, gy = mix[flat, :], gram_mix[flat, :]
                data = data + fold((h - pc * y) * (gh - pc * gy - (2.0 * sigma) * w))
                mix[flat, :] = h + scale_c * y
                gram_mix[flat, :] = gh + scale_c * gy
            t = e if start else e + factor * sparse_dual[flat, :]
            fresh = jnp.maximum(t - cut, 0.0)
            gap = e - fresh
            primal = primal + fold(gap * gap)
            move = fresh if start else fresh - sparse_var[flat, :]
            dual = dual + fold(move * move)
            sparse_var[flat, :] = fresh
            sparse_dual[flat, :] = t - fresh
            d = est[i + 1, at, :] - e
            t = d if start else d + factor * down_dual[flat, :]
            clipped = jnp.clip(t, -bound, bound)
            fresh = t - clipped
            gap = d - fresh
            move = fresh if start else fresh - down_var[flat, :]
            weight = jnp.where((i == 7) & (row == 1), 0.0, 1.0).astype(F32)
            primal = primal + weight * fold(gap * gap)
            dual = dual + weight * fold(move * move)
            down_var[flat, :] = fresh
            down_dual[flat, :] = clipped
            down_arg[flat, :] = gap
            d = est[i, pl.ds(off + 1, CHUNK), :] - e
            t = d if start else d + factor * right_dual[i, shifted, :]
            clipped = jnp.clip(t, -bound, bound)
            fresh = t - clipped
            gap = d - fresh
            primal = primal + fold(gap * gap)
            move = fresh if start else fresh - right_var[flat, :]
            dual = dual + fold(move * move)
            right_var[flat, :] = fresh
            right_dual[i, shifted, :] = clipped
            right_arg[i, shifted, :] = gap
            return primal, dual, data

        def update_row(i, totals):
            for off in range(0, 128, CHUNK):
                totals = update(i, off, totals)
            return totals

        zero = jnp.zeros((8, 128), F32)
        primal, dual, data = lax.fori_loop(0, 8, update_row, (zero, zero, zero))
        data = (data + (sigma * sigma) * square_ref[...]) * (share * share)
        line_p = jnp.sum(primal + data, axis=0, keepdims=True)
        line_d = jnp.sum(dual, axis=0, keepdims=True)
        line_p = line_p + pltpu.roll(line_p, 64, 1)
        line_d = line_d + pltpu.roll(line_d, 64, 1)
        line = jnp.where(lanes < 64, line_p, line_d)
        sums[turn, 0] = line
        near[turn, pl.ds(here, 1), :] = line
        start_sums(turn, 0)

        final = turn == ITERS - 1

        def rhs(i):
            flat = rows_of(i)
            above = rows_of(jnp.maximum(i - 1, 0))
            has_above = jnp.where(i > 0, 1.0, 0.0).astype(F32)
            w = proj_ref[flat, :]
            we = gram_mix[flat, :] - scale_s * w
            at = pl.ds(8, 128)
            before = pl.ds(7, 128)
            adj_a = (has_above * down_arg[above, :] - down_arg[flat, :]) + (
                right_arg[i, before, :] - right_arg[i, at, :]
            )
            adj_b = (has_above * down_dual[above, :] - down_dual[flat, :]) + (
                right_dual[i, before, :] - right_dual[i, at, :]
            )
            a = w + ratio * we + sparse_var[flat, :] + PROX * est[i, 0:128, :] - adj_a
            b = -(share * we + sparse_dual[flat, :] + adj_b)
            return a, b

        def prepare(i, carry):
            a, b = rhs(i)
            a, b = solve(a), solve(b)
            part_a[rows_of(i), :] = a
            part_b[rows_of(i), :] = b
            put_rims(turn + 1, i, 0, a)
            put_rims(turn + 1, i, 1, b)
            return carry

        def prepare_final(i, carry):
            a, b = rhs(i)
            out_ref[jnp.where(row == 1, 7 - i, i)] = solve_turned(a)
            turned = solve_turned(b)
            part_b[rows_of(i), 0:128] = turned[0:128, :]
            part_b[rows_of(i), 128:256] = turned[128:256, :]
            return carry

        work = prepare_final if final else prepare
        lax.fori_loop(0, 4, work, 0)
        wait_sums(turn, 0, 1)
        line = jnp.sum(near[turn], axis=0, keepdims=True)
        sums[turn, 1] = line
        far[turn, pl.ds(plane, 1), :] = line
        start_sums(turn, 1)
        lax.fori_loop(4, 8, work, 0)
        if not final:
            rim_copies = send_rims(turn + 1)
            halo_copies = [send_halo(turn + 1, 0, part_a), send_halo(turn + 1, 1, part_b)]
        wait_sums(turn, 1, 1)
        line = jnp.sum(far[turn], axis=0, keepdims=True)
        total_p = jnp.sum(jnp.where(lanes < 64, line, 0.0), axis=1, keepdims=True)
        total_d = jnp.sum(jnp.where(lanes < 64, 0.0, line), axis=1, keepdims=True)
        root = jnp.sqrt(jnp.sqrt((total_p + 1.0) / (penalty * penalty * total_d + 1.0)))
        following = penalty * root
        rescale = penalty / following
        carry_c = rescale * share_v
        penalty = following

    factor = scalar(rescale)

    def finish(i, carry):
        at = jnp.where(row == 1, 7 - i, i)
        out_ref[at, 0:128, :] = out_ref[at, 0:128, :] + factor * part_b[rows_of(i), 0:128]
        out_ref[at, 128:256, :] = out_ref[at, 128:256, :] + factor * part_b[rows_of(i), 128:256]
        return carry

    lax.fori_loop(0, 8, finish, 0)
    for turn in range(ITERS):
        for stage in range(2):
            wait_sums(turn, stage, 0)


def iterate(inverse, gram, proj, square, cols):
    depth = depth_of(cols)
    field = pltpu.VMEM((1024, 256), F32)
    padded = pltpu.VMEM((8, PAD, 256), F32)
    rims = pltpu.VMEM((ITERS, 16, 256), F32)
    return pl.pallas_call(
        functools.partial(iterate_kernel, cols),
        out_shape=jax.ShapeDtypeStruct((8, 256, 128), F32),
        in_specs=[VMEM] * 4,
        out_specs=VMEM,
        scratch_shapes=[
            pltpu.VMEM((9, PAD, 256), F32),
            field,
            field,
            pltpu.VMEM((ITERS, 2, 16, 256), F32),
            rims,
            rims,
            pltpu.VMEM((ITERS, 2, 128, 256), F32),
            pltpu.VMEM((8, 256), F32),
            field,
            field,
            field,
            field,
            field,
            field,
            padded,
            padded,
            field,
            field,
            pltpu.VMEM((768, 256), BF16),
            pltpu.VMEM((ITERS, 2, 1, 128), F32),
            pltpu.VMEM((ITERS, 2 * depth, 128), F32),
            pltpu.VMEM((ITERS, cols // depth, 128), F32),
            pltpu.SemaphoreType.DMA((2, ITERS, 2)),
            pltpu.SemaphoreType.DMA((2, ITERS, 2)),
            pltpu.SemaphoreType.DMA((2, ITERS, 2)),
        ],
        compiler_params=pltpu.CompilerParams(
            collective_id=1, has_side_effects=True, vmem_limit_bytes=32 * 2**20
        ),
        name="iterate",
    )(inverse, gram, proj, square)


def on_device(cols, observed, library):
    gathered = gather_library(library, cols)
    inverse, gram, proj, square = set_up(observed, gathered, cols)
    return iterate(inverse, gram, proj, square, cols).transpose(1, 0, 2)


def solution(mesh):
    return jax.shard_map(
        functools.partial(on_device, mesh.shape["col"]),
        mesh=mesh,
        in_specs=(P(None, "row", "col"), P("col", None)),
        out_specs=P(None, "row", "col"),
        check_vma=False,
    )
```

```python
import functools

import jax
import jax.numpy as jnp
from jax import lax
from jax.experimental import pallas as pl
from jax.experimental.pallas import tpu as pltpu
from jax.sharding import PartitionSpec as P

ITERS = 3
PROX = 8.0
WEIGHT_SPARSE = 0.3
WEIGHT_TV = 1.0
MESH = pl.DeviceIdType.MESH
F32 = jnp.float32
BF16 = jnp.bfloat16
VMEM = pl.BlockSpec(memory_space=pltpu.VMEM)


def slot_of(col, depth, cols):
    plane, z = col // depth, col % depth
    half = depth // 2
    return (z % 2) * (cols // 2) + plane * half + z // 2


def dot_of(x, y):
    t = [a * b for a, b in zip(x, y)]
    while len(t) > 1:
        t = [t[i] + t[i + 1] if i + 1 < len(t) else t[i] for i in range(0, len(t), 2)]
    return t[0]

def symmetric_inverse(m):
    n = len(m)
    if n == 1:
        return [[1.0 / m[0][0]]]
    if n == 2:
        scale = 1.0 / (m[0][0] * m[1][1] - m[0][1] * m[0][1])
        off = -m[0][1] * scale
        return [[m[1][1] * scale, off], [off, m[0][0] * scale]]
    h = n // 2
    a = symmetric_inverse([r[:h] for r in m[:h]])
    b = [r[h:] for r in m[:h]]
    bt = [list(c) for c in zip(*b)]
    t = [[dot_of(a[i], bt[j]) for j in range(h)] for i in range(h)]
    tt = [list(c) for c in zip(*t)]
    s = [[None] * h for _ in range(h)]
    for i in range(h):
        for j in range(i, h):
            s[i][j] = s[j][i] = m[h + i][h + j] - dot_of(bt[i], tt[j])
    s = symmetric_inverse(s)
    u = [[dot_of(t[i], s[j]) for j in range(h)] for i in range(h)]
    top = [[None] * h for _ in range(h)]
    for i in range(h):
        for j in range(i, h):
            top[i][j] = top[j][i] = a[i][j] + dot_of(u[i], t[j])
    out = [[None] * n for _ in range(n)]
    for i in range(h):
        for j in range(h):
            out[i][j] = top[i][j]
            out[h + i][h + j] = s[i][j]
            out[i][h + j] = -u[i][j]
            out[h + j][i] = -u[i][j]
    return out

def eliminate(matrix, ref):
    size, step = 128, 8
    groups = [matrix[8 * g : 8 * g + 8, :] for g in range(size // 8)]
    lane = lax.broadcasted_iota(jnp.int32, (8, size), 1)
    place = lax.broadcasted_iota(jnp.int32, (8, size), 0)
    full = (8, size)
    for home, first in enumerate(range(0, size, step)):

        def cols_of(g):
            return [jnp.broadcast_to(g[:, first + a : first + a + 1], full) for a in range(step)]

        home_cols = cols_of(groups[home])
        ref[0:8, :] = groups[home]
        for b in range(step):
            ref[8 + 8 * b : 16 + 8 * b, :] = home_cols[b]
        line = [jnp.broadcast_to(ref[a : a + 1, :], full) for a in range(step)]
        pivot = [[None] * step for _ in range(step)]
        for a in range(step):
            for b in range(a, step):
                spot = 8 + 8 * b + a
                pivot[a][b] = pivot[b][a] = jnp.broadcast_to(ref[spot : spot + 1, :], full)
        turned = symmetric_inverse(pivot)
        inside = (lane >= first) & (lane < first + step)
        rows = [jnp.where(lane == first + a, 1.0, jnp.where(inside, 0.0, line[a])) for a in range(step)]
        fresh = [dot_of(turned[a], rows) for a in range(step)]
        nxt = []
        for g, group in enumerate(groups):
            if g == home:
                value = fresh[0]
                for a in range(1, step):
                    value = jnp.where(place == a, fresh[a], value)
            else:
                value = jnp.where(inside, 0.0, group) - dot_of(cols_of(group), fresh)
            nxt.append(value)
        groups = nxt
    return jnp.concatenate(groups, axis=0)


def exact_dot(a, b, dims):
    return lax.dot_general(a, b, (dims, ((), ())), precision=lax.Precision.HIGHEST, preferred_element_type=F32)


def split2(x):
    high = x.astype(BF16)
    return high, (x - high.astype(F32)).astype(BF16)


CHUNK = 32
PAD = 136


def fold(x):
    total = None
    for k in range(x.shape[0] // 8):
        for half in range(2):
            part = x[8 * k : 8 * k + 8, 128 * half : 128 * half + 128]
            total = part if total is None else total + part
    return total


def kernel(
    sizes,
    obs_ref,
    shard_ref,
    out_ref,
    obs,
    wide,
    turned_obs,
    packed,
    shards,
    lib,
    work_rows,
    inverse,
    gram2,
    inv3,
    proj,
    own_rims,
    est,
    part_a,
    part_b,
    rim_send,
    rim_left,
    rim_right,
    halo,
    ghost,
    sparse_var,
    sparse_dual,
    down_var,
    down_dual,
    down_arg,
    right_var,
    right_dual,
    right_arg,
    mix,
    gram_mix,
    sums,
    pair,
    far,
    obs_sem,
    gather_sem,
    halo_sem,
    rim_sem,
    sum_sem,
):
    ys, xs, depth = sizes
    planes, half = ys * xs, depth // 2
    cols = planes * depth
    channels = 8 * cols
    row, col = lax.axis_index("row"), lax.axis_index("col")
    plane, z = lax.div(col, depth), lax.rem(col, depth)
    y, x = lax.div(plane, xs), lax.rem(plane, xs)
    parity = lax.rem(z, 2)
    flip = row == 1
    core_peer = (1 - row, col)
    left = (row, lax.rem(col + cols - 1, cols))
    right = (row, lax.rem(col + 1, cols))

    def peer_at(dy, dx, dz):
        return (row, (lax.rem(y + dy, ys) * xs + lax.rem(x + dx, xs)) * depth + lax.rem(z + dz, depth))

    def z_peer(step):
        return peer_at(0, 0, step)

    def plane_peer(step):
        return peer_at(step // xs, step % xs, 0)

    obs_copy = pltpu.make_async_copy(obs_ref, obs, obs_sem)
    obs_copy.start()
    barrier = pltpu.get_barrier_semaphore()
    for dz in range(depth):
        for dy in range(ys):
            for dx in range(xs):
                if dy or dx or dz:
                    pl.semaphore_signal(barrier, inc=1, device_id=peer_at(dy, dx, dz), device_id_type=MESH)
    pl.semaphore_signal(barrier, inc=1, device_id=core_peer, device_id_type=MESH)
    shard = shard_ref[...].astype(F32)
    packed[...] = jnp.concatenate([shard[:, :128], shard[:, 128:]], axis=0).astype(BF16)
    mine = parity * (cols // 2) + plane * half + lax.div(z, 2)
    obs_copy.wait()

    def widen(k, total):
        base = pl.multiple_of(k * 16, 16)
        part = obs[pl.ds(base, 16)].astype(F32)
        wide[pl.ds(pl.multiple_of(base * 8, 128), 128), :] = part.reshape(128, 128)
        return total + jnp.sum(part * part, axis=0)

    square = lax.fori_loop(0, channels // 16, widen, jnp.zeros((8, 128), F32))
    pl.semaphore_wait(barrier, cols)

    @pl.when(row == parity)
    def _():
        for step in range(1, depth):
            pltpu.make_async_remote_copy(
                src_ref=packed,
                dst_ref=shards.at[mine],
                send_sem=gather_sem.at[0],
                recv_sem=gather_sem.at[1],
                device_id=z_peer(step),
                device_id_type=MESH,
            ).start()
        shards[mine] = packed[...]

    def turn_rows(i, carry):
        source = jnp.where(flip, 7 - i, i)
        part = wide[pl.ds(source, channels, stride=8), :]
        turned_obs[pl.ds(pl.multiple_of(i * 128, 128), 128), :] = part.T.astype(BF16)
        return carry

    lax.fori_loop(0, 4, turn_rows, 0)

    @pl.when(row == parity)
    def _():
        if half > 1:
            got = shards.at[pl.ds(0, half - 1)]
            pltpu.make_async_copy(got, got, gather_sem.at[1]).wait()

    @pl.when(row != parity)
    def _():
        got = shards.at[pl.ds(0, half)]
        pltpu.make_async_copy(got, got, gather_sem.at[1]).wait()

    block = shards.at[pl.ds(row * (cols // 2) + plane * half, half)]
    for step in range(1, planes):
        pltpu.make_async_remote_copy(
            src_ref=block,
            dst_ref=block,
            send_sem=gather_sem.at[2],
            recv_sem=gather_sem.at[3],
            device_id=plane_peer(step),
            device_id_type=MESH,
        ).start()
    lax.fori_loop(4, 8, turn_rows, 0)
    got = shards.at[pl.ds(0, half * (planes - 1))]
    pltpu.make_async_copy(got, got, gather_sem.at[3]).wait()
    own_half = shards.at[pl.ds(row * (cols // 2), cols // 2)]
    swap = pltpu.make_async_remote_copy(
        src_ref=own_half,
        dst_ref=own_half,
        send_sem=gather_sem.at[4],
        recv_sem=gather_sem.at[5],
        device_id=core_peer,
        device_id_type=MESH,
    )
    swap.start()

    @pl.when(row == parity)
    def _():
        sent = shards.at[pl.ds(0, depth - 1)]
        pltpu.make_async_copy(sent, sent, gather_sem.at[0]).wait()

    pltpu.make_async_copy(got, got, gather_sem.at[2]).wait()
    swap.wait()

    for two in range(cols // 2):
        one = shards[slot_of(2 * two, depth, cols)].astype(F32)
        other = shards[slot_of(2 * two + 1, depth, cols)].astype(F32)
        lib[16 * two : 16 * two + 16, 0:128] = jnp.concatenate([one[0:8], other[0:8]], axis=0).astype(BF16)
        lib[16 * two : 16 * two + 16, 128:256] = jnp.concatenate([one[8:16], other[8:16]], axis=0).astype(BF16)

    def rows_of(x):
        return pl.ds(pl.multiple_of(x * 128, 128), 128)

    for i in range(8):
        value = jnp.dot(turned_obs[128 * i : 128 * i + 128, :], lib[...], preferred_element_type=F32)
        proj[128 * i : 128 * i + 128, :] = value
        rim_send[0, 0, i : i + 1, :] = value[0:1, :]
        rim_send[0, 1, i : i + 1, :] = value[127:128, :]

    def send_halo(turn, slot, field):
        copy = pltpu.make_async_remote_copy(
            src_ref=field.at[rows_of(7)],
            dst_ref=halo.at[turn, slot],
            send_sem=halo_sem.at[0, turn, slot],
            recv_sem=halo_sem.at[1, turn, slot],
            device_id=core_peer,
            device_id_type=MESH,
        )
        copy.start()
        return copy

    def send_rims(turn):
        used = 8 if turn == 0 else 16
        to_left = pltpu.make_async_remote_copy(
            src_ref=rim_send.at[turn, 0, pl.ds(0, used)],
            dst_ref=rim_right.at[turn, pl.ds(0, used)],
            send_sem=rim_sem.at[0, turn, 0],
            recv_sem=rim_sem.at[1, turn, 0],
            device_id=left,
            device_id_type=MESH,
        )
        to_right = pltpu.make_async_remote_copy(
            src_ref=rim_send.at[turn, 1, pl.ds(0, used)],
            dst_ref=rim_left.at[turn, pl.ds(0, used)],
            send_sem=rim_sem.at[0, turn, 1],
            recv_sem=rim_sem.at[1, turn, 1],
            device_id=right,
            device_id_type=MESH,
        )
        to_left.start()
        to_right.start()
        return [to_left, to_right]

    rim_copies = send_rims(0)
    halo_copies = [send_halo(0, 0, proj)]

    library = lib[...]
    gram = lax.dot_general(library, library, (((0,), (0,)), ((), ())), preferred_element_type=F32)
    high, low = split2(gram)
    gram2[0:256, :] = high
    gram2[256:512, :] = low
    same = lax.broadcasted_iota(jnp.int32, (256, 256), 0) == lax.broadcasted_iota(jnp.int32, (256, 256), 1)
    system = gram + jnp.where(same, 1.0 + PROX, 0.0)
    first_inverse = eliminate(system[:128, :128], work_rows)
    lead = exact_dot(first_inverse, system[:128, 128:], ((1,), (0,)))
    last_inverse = eliminate(
        system[128:, 128:] - exact_dot(system[128:, :128], lead, ((1,), (0,))), work_rows
    )
    corner = -exact_dot(lead, last_inverse, ((1,), (0,)))
    inverse[0:128, 0:128] = first_inverse - exact_dot(corner, lead, ((1,), (1,)))
    inverse[0:128, 128:256] = corner
    inverse[128:256, 0:128] = -exact_dot(last_inverse, lead, ((1,), (1,)))
    inverse[128:256, 128:256] = last_inverse
    high, low = split2(inverse[...])
    inv3[0:256, :] = high
    inv3[256:512, :] = low
    inv3[512:768, :] = high

    def stacked(x):
        one, two = split2(x)
        return jnp.concatenate([one, one, two], axis=1)

    def solve(x):
        return jnp.dot(stacked(x), inv3[...], preferred_element_type=F32)

    def solve_turned(x):
        one, two = split2(x)
        dims = (((1,), (1,)), ((), ()))
        total = lax.dot_general(inv3[0:256, :], one, dims, preferred_element_type=F32)
        total = total + lax.dot_general(inv3[256:512, :], one, dims, preferred_element_type=F32)
        return total + lax.dot_general(inv3[0:256, :], two, dims, preferred_element_type=F32)

    def put_rims(turn, i, slot, value):
        rim_send[turn, 0, pl.ds(8 * slot + i, 1), :] = value[0:1, :]
        rim_send[turn, 1, pl.ds(8 * slot + i, 1), :] = value[127:128, :]

    for i in range(8):
        value = solve(proj[128 * i : 128 * i + 128, :])
        part_a[128 * i : 128 * i + 128, :] = value
        own_rims[0, i : i + 1, :] = value[0:1, :]
        own_rims[1, i : i + 1, :] = value[127:128, :]

    def send_pair(turn):
        pltpu.make_async_remote_copy(
            src_ref=sums.at[turn, 0],
            dst_ref=pair.at[turn],
            send_sem=sum_sem.at[0, turn, 0],
            recv_sem=sum_sem.at[1, turn, 0],
            device_id=core_peer,
            device_id_type=MESH,
        ).start()

    def send_sums(turn, dz, alone):
        for dy in range(ys):
            for dx in range(xs):
                copy = pltpu.make_async_remote_copy(
                    src_ref=sums.at[turn, 1],
                    dst_ref=far.at[turn, pl.ds(col, 1)],
                    send_sem=sum_sem.at[0, turn, 1],
                    recv_sem=sum_sem.at[1, turn, 1],
                    device_id=peer_at(dy, dx, dz),
                    device_id_type=MESH,
                )
                if dy or dx:
                    copy.start()
                else:
                    pl.when(jnp.logical_not(alone))(copy.start)

    def wait_pair(turn, which):
        pltpu.make_async_copy(pair.at[turn], pair.at[turn], sum_sem.at[which, turn, 0]).wait()

    def wait_far(turn, which):
        got = far.at[turn, pl.ds(0, cols - 1)]
        pltpu.make_async_copy(got, got, sum_sem.at[which, turn, 1]).wait()

    first_col = jnp.where(col == 0, 1.0, 0.0).astype(F32)
    last_col = jnp.where(col == cols - 1, 1.0, 0.0).astype(F32)
    lanes = lax.broadcasted_iota(jnp.int32, (1, 128), 1)
    penalty, rescale, carry_c, carry_s = 1.0, 0.0, 0.0, 0.0

    def scalar(x):
        return x if isinstance(x, float) else x[0, 0]

    for turn in range(ITERS):
        start = turn == 0
        old_c, old_s = carry_c, carry_s
        pc_v = penalty * old_c
        sigma_v = 1.0 - pc_v * old_s
        share_v = 1.0 / (1.0 + penalty)
        carry_s = 1.0 + old_c * old_s
        bound, cut = scalar(WEIGHT_TV / penalty), scalar(WEIGHT_SPARSE / penalty)
        pc, sigma, scale_c = scalar(pc_v), scalar(sigma_v), scalar(old_c)
        share, ratio, scale_s = scalar(share_v), scalar(penalty * share_v), scalar(carry_s)
        factor = scalar(rescale)
        for copy in rim_copies + halo_copies:
            copy.wait()

        def combined(a, b):
            return a if start else a + factor * b

        def place(i, carry):
            value = combined(part_a[rows_of(i), :], part_b[rows_of(i), :])
            est[i, 0:128, :] = value
            return carry

        lax.fori_loop(0, 8, place, 0)
        if start:
            est[8, 0:128, :] = solve(halo[0, 0])
            rims = solve(jnp.concatenate([rim_left[0, 0:8, :], rim_right[0, 0:8, :]], axis=0))
            from_left, from_right = rims[0:8], rims[8:16]
            own_first, own_last = own_rims[0], own_rims[1]
        else:
            est[8, 0:128, :] = combined(halo[turn, 0], halo[turn, 1])
            own_first = combined(rim_send[turn, 0, 0:8, :], rim_send[turn, 0, 8:16, :])
            own_last = combined(rim_send[turn, 1, 0:8, :], rim_send[turn, 1, 8:16, :])
            from_right = combined(rim_right[turn, 0:8, :], rim_right[turn, 8:16, :])
            from_left = combined(rim_left[turn, 0:8, :], rim_left[turn, 8:16, :])
        from_right = jnp.where(last_col > 0.0, own_last, from_right)
        from_left = jnp.where(first_col > 0.0, own_first, from_left)
        for i in range(8):
            est[i, 128:129, :] = from_right[i : i + 1, :]

        g_diff = own_first - from_left
        g_sum = g_diff if start else g_diff + factor * ghost[...]
        g_dual = jnp.clip(g_sum, -bound, bound)
        g_arg = g_diff - (g_sum - g_dual)
        ghost[...] = g_dual
        for i in range(8):
            right_arg[i, 7:8, :] = g_arg[i : i + 1, :]
            right_dual[i, 7:8, :] = g_dual[i : i + 1, :]

        def update(i, off, totals):
            at = pl.ds(off, CHUNK)
            shifted = pl.ds(off + 8, CHUNK)
            flat = pl.ds(pl.multiple_of(i * 128 + off, CHUNK), CHUNK)
            primal, dual, data = totals
            e = est[i, at, :]
            half = e.astype(BF16)
            gh = jnp.dot(jnp.concatenate([half, half], axis=1), gram2[...], preferred_element_type=F32)
            h = half.astype(F32)
            w = proj[flat, :]
            if start:
                data = data + fold(h * (gh - 2.0 * w))
                mix[flat, :] = h
                gram_mix[flat, :] = gh
            else:
                y, gy = mix[flat, :], gram_mix[flat, :]
                data = data + fold((h - pc * y) * (gh - pc * gy - (2.0 * sigma) * w))
                mix[flat, :] = h + scale_c * y
                gram_mix[flat, :] = gh + scale_c * gy
            t = e if start else e + factor * sparse_dual[flat, :]
            fresh = jnp.maximum(t - cut, 0.0)
            gap = e - fresh
            primal = primal + fold(gap * gap)
            move = fresh if start else fresh - sparse_var[flat, :]
            dual = dual + fold(move * move)
            sparse_var[flat, :] = fresh
            sparse_dual[flat, :] = t - fresh
            d = est[i + 1, at, :] - e
            t = d if start else d + factor * down_dual[flat, :]
            clipped = jnp.clip(t, -bound, bound)
            fresh = t - clipped
            gap = d - fresh
            move = fresh if start else fresh - down_var[flat, :]
            weight = jnp.where((i == 7) & (row == 1), 0.0, 1.0).astype(F32)
            primal = primal + weight * fold(gap * gap)
            dual = dual + weight * fold(move * move)
            down_var[flat, :] = fresh
            down_dual[flat, :] = clipped
            down_arg[flat, :] = gap
            d = est[i, pl.ds(off + 1, CHUNK), :] - e
            t = d if start else d + factor * right_dual[i, shifted, :]
            clipped = jnp.clip(t, -bound, bound)
            fresh = t - clipped
            gap = d - fresh
            primal = primal + fold(gap * gap)
            move = fresh if start else fresh - right_var[flat, :]
            dual = dual + fold(move * move)
            right_var[flat, :] = fresh
            right_dual[i, shifted, :] = clipped
            right_arg[i, shifted, :] = gap
            return primal, dual, data

        def update_row(i, totals):
            for off in range(0, 128, CHUNK):
                totals = update(i, off, totals)
            return totals

        zero = jnp.zeros((8, 128), F32)
        primal, dual, data = lax.fori_loop(0, 8, update_row, (zero, zero, zero))
        data = (data + (sigma * sigma) * square) * (share * share)
        line_p = jnp.sum(primal + data, axis=0, keepdims=True)
        line_d = jnp.sum(dual, axis=0, keepdims=True)
        line_p = line_p + pltpu.roll(line_p, 64, 1)
        line_d = line_d + pltpu.roll(line_d, 64, 1)
        line = jnp.where(lanes < 64, line_p, line_d)
        sums[turn, 0] = line
        send_pair(turn)

        final = turn == ITERS - 1

        def rhs(i):
            flat = rows_of(i)
            above = rows_of(jnp.maximum(i - 1, 0))
            has_above = jnp.where(i > 0, 1.0, 0.0).astype(F32)
            w = proj[flat, :]
            we = gram_mix[flat, :] - scale_s * w
            at = pl.ds(8, 128)
            before = pl.ds(7, 128)
            adj_a = (has_above * down_arg[above, :] - down_arg[flat, :]) + (
                right_arg[i, before, :] - right_arg[i, at, :]
            )
            adj_b = (has_above * down_dual[above, :] - down_dual[flat, :]) + (
                right_dual[i, before, :] - right_dual[i, at, :]
            )
            a = w + ratio * we + sparse_var[flat, :] + PROX * est[i, 0:128, :] - adj_a
            b = -(share * we + sparse_dual[flat, :] + adj_b)
            return a, b

        def prepare(i, carry):
            a, b = rhs(i)
            a, b = solve(a), solve(b)
            part_a[rows_of(i), :] = a
            part_b[rows_of(i), :] = b
            put_rims(turn + 1, i, 0, a)
            put_rims(turn + 1, i, 1, b)
            return carry

        def prepare_final(i, carry):
            a, b = rhs(i)
            out_ref[jnp.where(row == 1, 7 - i, i)] = solve_turned(a)
            turned = solve_turned(b)
            part_b[rows_of(i), 0:128] = turned[0:128, :]
            part_b[rows_of(i), 128:256] = turned[128:256, :]
            return carry

        work = prepare_final if final else prepare
        lax.fori_loop(0, 2, work, 0)
        wait_pair(turn, 1)
        line = line + pair[turn]
        sums[turn, 1] = line
        far[turn, pl.ds(col, 1), :] = line

        def send_and_work(n, carry):
            for one in (2 * n, 2 * n + 1):
                away = lax.div(one + 1, 2)
                dz = jnp.where(lax.rem(one, 2) == 1, half - away, half + away)
                send_sums(turn, dz, one == depth - 1)
            return work(n + 2, carry)

        lax.fori_loop(0, half, send_and_work, 0)
        lax.fori_loop(half + 2, 8, work, 0)
        if not final:
            rim_copies = send_rims(turn + 1)
            halo_copies = [send_halo(turn + 1, 0, part_a), send_halo(turn + 1, 1, part_b)]
        wait_far(turn, 1)
        line = jnp.sum(far[turn], axis=0, keepdims=True)
        total_p = jnp.sum(jnp.where(lanes < 64, line, 0.0), axis=1, keepdims=True)
        total_d = jnp.sum(jnp.where(lanes < 64, 0.0, line), axis=1, keepdims=True)
        root = jnp.sqrt(jnp.sqrt((total_p + 1.0) / (penalty * penalty * total_d + 1.0)))
        following = penalty * root
        rescale = penalty / following
        carry_c = rescale * share_v
        penalty = following

    factor = scalar(rescale)

    def finish(i, carry):
        at = jnp.where(row == 1, 7 - i, i)
        out_ref[at, 0:128, :] = out_ref[at, 0:128, :] + factor * part_b[rows_of(i), 0:128]
        out_ref[at, 128:256, :] = out_ref[at, 128:256, :] + factor * part_b[rows_of(i), 128:256]
        return carry

    lax.fori_loop(0, 8, finish, 0)
    for turn in range(ITERS):
        wait_pair(turn, 0)
        wait_far(turn, 0)


def run(sizes, observed, shard):
    ys, xs, depth = sizes
    cols = ys * xs * depth
    channels = 8 * cols
    field = pltpu.VMEM((1024, 256), F32)
    padded = pltpu.VMEM((8, PAD, 256), F32)
    rims = pltpu.VMEM((ITERS, 16, 256), F32)
    return pl.pallas_call(
        functools.partial(kernel, sizes),
        out_shape=jax.ShapeDtypeStruct((8, 256, 128), F32),
        in_specs=[pl.BlockSpec(memory_space=pl.ANY), VMEM],
        out_specs=VMEM,
        scratch_shapes=[
            pltpu.VMEM((channels, 8, 128), BF16),
            pltpu.VMEM((channels * 8, 128), F32),
            pltpu.VMEM((1024, channels), BF16),
            pltpu.VMEM((16, 128), BF16),
            pltpu.VMEM((cols, 16, 128), BF16),
            pltpu.VMEM((channels, 256), BF16),
            pltpu.VMEM((72, 128), F32),
            pltpu.VMEM((256, 256), F32),
            pltpu.VMEM((512, 256), BF16),
            pltpu.VMEM((768, 256), BF16),
            field,
            pltpu.VMEM((2, 8, 256), F32),
            pltpu.VMEM((9, PAD, 256), F32),
            field,
            field,
            pltpu.VMEM((ITERS, 2, 16, 256), F32),
            rims,
            rims,
            pltpu.VMEM((ITERS, 2, 128, 256), F32),
            pltpu.VMEM((8, 256), F32),
            field,
            field,
            field,
            field,
            field,
            field,
            padded,
            padded,
            field,
            field,
            pltpu.VMEM((ITERS, 2, 1, 128), F32),
            pltpu.VMEM((ITERS, 1, 128), F32),
            pltpu.VMEM((ITERS, cols, 128), F32),
            pltpu.SemaphoreType.DMA(()),
            pltpu.SemaphoreType.DMA((6,)),
            pltpu.SemaphoreType.DMA((2, ITERS, 2)),
            pltpu.SemaphoreType.DMA((2, ITERS, 2)),
            pltpu.SemaphoreType.DMA((2, ITERS, 2)),
        ],
        compiler_params=pltpu.CompilerParams(
            collective_id=0, has_side_effects=True, vmem_limit_bytes=48 * 2**20
        ),
        name="unmix",
    )(observed, shard)


def on_device(sizes, observed, library):
    return run(sizes, observed, library).transpose(1, 0, 2)


def solution(mesh):
    sizes = (4, 4, 8) if mesh.shape["col"] == 128 else (2, 2, 2)
    return jax.shard_map(
        functools.partial(on_device, sizes),
        mesh=mesh,
        in_specs=(P(None, "row", "col"), P("col", None)),
        out_specs=P(None, "row", "col"),
        check_vma=False,
    )
```

```python
import functools

import jax
import jax.numpy as jnp
from jax import lax
from jax.experimental import pallas as pl
from jax.experimental.pallas import tpu as pltpu
from jax.sharding import PartitionSpec as P

ITERS = 3
PROX = 8.0
WEIGHT_SPARSE = 0.3
WEIGHT_TV = 1.0
MESH = pl.DeviceIdType.MESH
F32 = jnp.float32
BF16 = jnp.bfloat16
VMEM = pl.BlockSpec(memory_space=pltpu.VMEM)


def slot_of(col, depth, cols):
    plane, z = col // depth, col % depth
    half = depth // 2
    return (z % 2) * (cols // 2) + plane * half + z // 2


def dot_of(x, y):
    t = [a * b for a, b in zip(x, y)]
    while len(t) > 1:
        t = [t[i] + t[i + 1] if i + 1 < len(t) else t[i] for i in range(0, len(t), 2)]
    return t[0]

def symmetric_inverse(m):
    n = len(m)
    if n == 1:
        return [[1.0 / m[0][0]]]
    if n == 2:
        scale = 1.0 / (m[0][0] * m[1][1] - m[0][1] * m[0][1])
        off = -m[0][1] * scale
        return [[m[1][1] * scale, off], [off, m[0][0] * scale]]
    h = n // 2
    a = symmetric_inverse([r[:h] for r in m[:h]])
    b = [r[h:] for r in m[:h]]
    bt = [list(c) for c in zip(*b)]
    t = [[dot_of(a[i], bt[j]) for j in range(h)] for i in range(h)]
    tt = [list(c) for c in zip(*t)]
    s = [[None] * h for _ in range(h)]
    for i in range(h):
        for j in range(i, h):
            s[i][j] = s[j][i] = m[h + i][h + j] - dot_of(bt[i], tt[j])
    s = symmetric_inverse(s)
    u = [[dot_of(t[i], s[j]) for j in range(h)] for i in range(h)]
    top = [[None] * h for _ in range(h)]
    for i in range(h):
        for j in range(i, h):
            top[i][j] = top[j][i] = a[i][j] + dot_of(u[i], t[j])
    out = [[None] * n for _ in range(n)]
    for i in range(h):
        for j in range(h):
            out[i][j] = top[i][j]
            out[h + i][h + j] = s[i][j]
            out[i][h + j] = -u[i][j]
            out[h + j][i] = -u[i][j]
    return out

def eliminate(matrix, ref):
    size, step = 128, 8
    groups = [matrix[8 * g : 8 * g + 8, :] for g in range(size // 8)]
    lane = lax.broadcasted_iota(jnp.int32, (8, size), 1)
    place = lax.broadcasted_iota(jnp.int32, (8, size), 0)
    full = (8, size)
    for home, first in enumerate(range(0, size, step)):

        def cols_of(g):
            return [jnp.broadcast_to(g[:, first + a : first + a + 1], full) for a in range(step)]

        home_cols = cols_of(groups[home])
        ref[0:8, :] = groups[home]
        for b in range(step):
            ref[8 + 8 * b : 16 + 8 * b, :] = home_cols[b]
        line = [jnp.broadcast_to(ref[a : a + 1, :], full) for a in range(step)]
        pivot = [[None] * step for _ in range(step)]
        for a in range(step):
            for b in range(a, step):
                spot = 8 + 8 * b + a
                pivot[a][b] = pivot[b][a] = jnp.broadcast_to(ref[spot : spot + 1, :], full)
        turned = symmetric_inverse(pivot)
        inside = (lane >= first) & (lane < first + step)
        rows = [jnp.where(lane == first + a, 1.0, jnp.where(inside, 0.0, line[a])) for a in range(step)]
        fresh = [dot_of(turned[a], rows) for a in range(step)]
        nxt = []
        for g, group in enumerate(groups):
            if g == home:
                value = fresh[0]
                for a in range(1, step):
                    value = jnp.where(place == a, fresh[a], value)
            else:
                value = jnp.where(inside, 0.0, group) - dot_of(cols_of(group), fresh)
            nxt.append(value)
        groups = nxt
    return jnp.concatenate(groups, axis=0)


def exact_dot(a, b, dims):
    return lax.dot_general(a, b, (dims, ((), ())), precision=lax.Precision.HIGHEST, preferred_element_type=F32)


def split2(x):
    high = x.astype(BF16)
    return high, (x - high.astype(F32)).astype(BF16)


CHUNK = 32
PAD = 136


def fold(x):
    total = None
    for k in range(x.shape[0] // 8):
        for half in range(2):
            part = x[8 * k : 8 * k + 8, 128 * half : 128 * half + 128]
            total = part if total is None else total + part
    return total


def kernel(
    sizes,
    obs_ref,
    shard_ref,
    out_ref,
    obs,
    own_shard,
    wide,
    turned_obs,
    packed,
    shards,
    lib,
    work_rows,
    inverse,
    gram2,
    inv3,
    proj,
    own_rims,
    est,
    part_a,
    part_b,
    rim_send,
    rim_left,
    rim_right,
    halo,
    ghost,
    sparse_var,
    sparse_dual,
    down_var,
    down_dual,
    down_arg,
    right_var,
    right_dual,
    right_arg,
    mix,
    gram_mix,
    sums,
    pair,
    far,
    obs_sem,
    shard_sem,
    gather_sem,
    plane_sem,
    halo_sem,
    rim_sem,
    sum_sem,
):
    ys, xs, depth = sizes
    planes, half = ys * xs, depth // 2
    cols = planes * depth
    channels = 8 * cols
    row, col = lax.axis_index("row"), lax.axis_index("col")
    plane, z = lax.div(col, depth), lax.rem(col, depth)
    y, x = lax.div(plane, xs), lax.rem(plane, xs)
    parity = lax.rem(z, 2)
    flip = row == 1
    core_peer = (1 - row, col)
    left = (row, lax.rem(col + cols - 1, cols))
    right = (row, lax.rem(col + 1, cols))

    def peer_at(dy, dx, dz):
        return (row, (lax.rem(y + dy, ys) * xs + lax.rem(x + dx, xs)) * depth + lax.rem(z + dz, depth))

    def z_peer(step):
        return peer_at(0, 0, step)

    def plane_peer(step):
        return peer_at(step // xs, step % xs, 0)

    obs_copy = pltpu.make_async_copy(obs_ref, obs, obs_sem)
    obs_copy.start()
    shard_copy = pltpu.make_async_copy(shard_ref, own_shard, shard_sem)
    shard_copy.start()
    barrier = pltpu.get_barrier_semaphore()
    peers = [z_peer(n) for n in range(1, depth)] + [plane_peer(n) for n in range(1, planes)] + [core_peer]
    for peer in peers:
        pl.semaphore_signal(barrier, inc=1, device_id=peer, device_id_type=MESH)
    shard_copy.wait()
    shard = own_shard[...].astype(F32)
    packed[...] = jnp.concatenate([shard[:, :128], shard[:, 128:]], axis=0).astype(BF16)
    mine = parity * (cols // 2) + plane * half + lax.div(z, 2)
    obs_copy.wait()

    def widen(k, total):
        base = pl.multiple_of(k * 16, 16)
        part = obs[pl.ds(base, 16)].astype(F32)
        wide[pl.ds(pl.multiple_of(base * 8, 128), 128), :] = part.reshape(128, 128)
        return total + jnp.sum(part * part, axis=0)

    square = lax.fori_loop(0, channels // 16, widen, jnp.zeros((8, 128), F32))
    pl.semaphore_wait(barrier, len(peers))

    @pl.when(row == parity)
    def _():
        for step in range(1, depth):
            pltpu.make_async_remote_copy(
                src_ref=packed,
                dst_ref=shards.at[mine],
                send_sem=gather_sem.at[0],
                recv_sem=gather_sem.at[1],
                device_id=z_peer(step),
                device_id_type=MESH,
            ).start()
        shards[mine] = packed[...]

    def turn_rows(i, carry):
        source = jnp.where(flip, 7 - i, i)
        part = wide[pl.ds(source, channels, stride=8), :]
        turned_obs[pl.ds(pl.multiple_of(i * 128, 128), 128), :] = part.T.astype(BF16)
        return carry

    lax.fori_loop(0, 4, turn_rows, 0)

    @pl.when(row == parity)
    def _():
        if half > 1:
            got = shards.at[pl.ds(0, half - 1)]
            pltpu.make_async_copy(got, got, gather_sem.at[1]).wait()

    @pl.when(row != parity)
    def _():
        got = shards.at[pl.ds(0, half)]
        pltpu.make_async_copy(got, got, gather_sem.at[1]).wait()

    def block_of(dy, dx):
        other = lax.rem(y + ys - dy, ys) * xs + lax.rem(x + xs - dx, xs)
        return shards.at[pl.ds(row * (cols // 2) + other * half, half)]

    def pass_over(block):
        pltpu.make_async_remote_copy(
            src_ref=block,
            dst_ref=block,
            send_sem=gather_sem.at[3],
            recv_sem=gather_sem.at[4],
            device_id=core_peer,
            device_id_type=MESH,
        ).start()

    block = block_of(0, 0)
    for step in range(1, planes):
        pltpu.make_async_remote_copy(
            src_ref=block,
            dst_ref=block,
            send_sem=gather_sem.at[2],
            recv_sem=plane_sem.at[step],
            device_id=plane_peer(step),
            device_id_type=MESH,
        ).start()
    pass_over(block)
    lax.fori_loop(4, 8, turn_rows, 0)
    nearest = sorted(range(1, planes), key=lambda n: min(n // xs, ys - n // xs) + min(n % xs, xs - n % xs))
    for step in nearest:
        got = block_of(step // xs, step % xs)
        pltpu.make_async_copy(got, got, plane_sem.at[step]).wait()
        pass_over(got)
    other_half = shards.at[pl.ds((1 - row) * (cols // 2), cols // 2)]
    pltpu.make_async_copy(other_half, other_half, gather_sem.at[4]).wait()

    @pl.when(row == parity)
    def _():
        sent = shards.at[pl.ds(0, depth - 1)]
        pltpu.make_async_copy(sent, sent, gather_sem.at[0]).wait()

    sent = shards.at[pl.ds(0, half * (planes - 1))]
    pltpu.make_async_copy(sent, sent, gather_sem.at[2]).wait()
    pltpu.make_async_copy(other_half, other_half, gather_sem.at[3]).wait()

    for two in range(cols // 2):
        one = shards[slot_of(2 * two, depth, cols)].astype(F32)
        other = shards[slot_of(2 * two + 1, depth, cols)].astype(F32)
        lib[16 * two : 16 * two + 16, 0:128] = jnp.concatenate([one[0:8], other[0:8]], axis=0).astype(BF16)
        lib[16 * two : 16 * two + 16, 128:256] = jnp.concatenate([one[8:16], other[8:16]], axis=0).astype(BF16)

    def rows_of(x):
        return pl.ds(pl.multiple_of(x * 128, 128), 128)

    def send_halo(turn, slot, field):
        copy = pltpu.make_async_remote_copy(
            src_ref=field.at[rows_of(7)],
            dst_ref=halo.at[turn, slot],
            send_sem=halo_sem.at[0, turn, slot],
            recv_sem=halo_sem.at[1, turn, slot],
            device_id=core_peer,
            device_id_type=MESH,
        )
        copy.start()
        return copy

    def send_rims(turn):
        used = 8 if turn == 0 else 16
        to_left = pltpu.make_async_remote_copy(
            src_ref=rim_send.at[turn, 0, pl.ds(0, used)],
            dst_ref=rim_right.at[turn, pl.ds(0, used)],
            send_sem=rim_sem.at[0, turn, 0],
            recv_sem=rim_sem.at[1, turn, 0],
            device_id=left,
            device_id_type=MESH,
        )
        to_right = pltpu.make_async_remote_copy(
            src_ref=rim_send.at[turn, 1, pl.ds(0, used)],
            dst_ref=rim_left.at[turn, pl.ds(0, used)],
            send_sem=rim_sem.at[0, turn, 1],
            recv_sem=rim_sem.at[1, turn, 1],
            device_id=right,
            device_id_type=MESH,
        )
        to_left.start()
        to_right.start()
        return [to_left, to_right]

    library = lib[...]
    gram = lax.dot_general(library, library, (((0,), (0,)), ((), ())), preferred_element_type=F32)
    high, low = split2(gram)
    gram2[0:256, :] = high
    gram2[256:512, :] = low
    same = lax.broadcasted_iota(jnp.int32, (256, 256), 0) == lax.broadcasted_iota(jnp.int32, (256, 256), 1)
    system = gram + jnp.where(same, 1.0 + PROX, 0.0)
    for i in range(8):
        value = jnp.dot(turned_obs[128 * i : 128 * i + 128, :], lib[...], preferred_element_type=F32)
        proj[128 * i : 128 * i + 128, :] = value
        rim_send[0, 0, i : i + 1, :] = value[0:1, :]
        rim_send[0, 1, i : i + 1, :] = value[127:128, :]

    first_inverse = eliminate(system[:128, :128], work_rows)
    rim_copies = send_rims(0)
    halo_copies = [send_halo(0, 0, proj)]
    lead = exact_dot(first_inverse, system[:128, 128:], ((1,), (0,)))
    last_inverse = eliminate(
        system[128:, 128:] - exact_dot(system[128:, :128], lead, ((1,), (0,))), work_rows
    )
    corner = -exact_dot(lead, last_inverse, ((1,), (0,)))
    inverse[0:128, 0:128] = first_inverse - exact_dot(corner, lead, ((1,), (1,)))
    inverse[0:128, 128:256] = corner
    inverse[128:256, 0:128] = -exact_dot(last_inverse, lead, ((1,), (1,)))
    inverse[128:256, 128:256] = last_inverse
    high, low = split2(inverse[...])
    inv3[0:256, :] = high
    inv3[256:512, :] = low
    inv3[512:768, :] = high

    def stacked(x):
        one, two = split2(x)
        return jnp.concatenate([one, one, two], axis=1)

    def solve(x):
        return jnp.dot(stacked(x), inv3[...], preferred_element_type=F32)

    def solve_turned(x):
        one, two = split2(x)
        dims = (((1,), (1,)), ((), ()))
        total = lax.dot_general(inv3[0:256, :], one, dims, preferred_element_type=F32)
        total = total + lax.dot_general(inv3[256:512, :], one, dims, preferred_element_type=F32)
        return total + lax.dot_general(inv3[0:256, :], two, dims, preferred_element_type=F32)

    def put_rims(turn, i, slot, value):
        rim_send[turn, 0, pl.ds(8 * slot + i, 1), :] = value[0:1, :]
        rim_send[turn, 1, pl.ds(8 * slot + i, 1), :] = value[127:128, :]

    for i in range(8):
        value = solve(proj[128 * i : 128 * i + 128, :])
        part_a[128 * i : 128 * i + 128, :] = value
        own_rims[0, i : i + 1, :] = value[0:1, :]
        own_rims[1, i : i + 1, :] = value[127:128, :]

    def send_pair(turn):
        pltpu.make_async_remote_copy(
            src_ref=sums.at[turn, 0],
            dst_ref=pair.at[turn],
            send_sem=sum_sem.at[0, turn, 0],
            recv_sem=sum_sem.at[1, turn, 0],
            device_id=core_peer,
            device_id_type=MESH,
        ).start()

    def send_sums(turn, dz, alone):
        for dy in range(ys):
            for dx in range(xs):
                copy = pltpu.make_async_remote_copy(
                    src_ref=sums.at[turn, 1],
                    dst_ref=far.at[turn, pl.ds(col, 1)],
                    send_sem=sum_sem.at[0, turn, 1],
                    recv_sem=sum_sem.at[1, turn, 1],
                    device_id=peer_at(dy, dx, dz),
                    device_id_type=MESH,
                )
                if dy or dx:
                    copy.start()
                else:
                    pl.when(jnp.logical_not(alone))(copy.start)

    def wait_pair(turn, which):
        pltpu.make_async_copy(pair.at[turn], pair.at[turn], sum_sem.at[which, turn, 0]).wait()

    def wait_far(turn, which):
        got = far.at[turn, pl.ds(0, cols - 1)]
        pltpu.make_async_copy(got, got, sum_sem.at[which, turn, 1]).wait()

    first_col = jnp.where(col == 0, 1.0, 0.0).astype(F32)
    last_col = jnp.where(col == cols - 1, 1.0, 0.0).astype(F32)
    lanes = lax.broadcasted_iota(jnp.int32, (1, 128), 1)
    penalty, rescale, carry_c, carry_s = 1.0, 0.0, 0.0, 0.0

    def scalar(x):
        return x if isinstance(x, float) else x[0, 0]

    for turn in range(ITERS):
        start = turn == 0
        old_c, old_s = carry_c, carry_s
        pc_v = penalty * old_c
        sigma_v = 1.0 - pc_v * old_s
        share_v = 1.0 / (1.0 + penalty)
        carry_s = 1.0 + old_c * old_s
        bound, cut = scalar(WEIGHT_TV / penalty), scalar(WEIGHT_SPARSE / penalty)
        pc, sigma, scale_c = scalar(pc_v), scalar(sigma_v), scalar(old_c)
        share, ratio, scale_s = scalar(share_v), scalar(penalty * share_v), scalar(carry_s)
        factor = scalar(rescale)
        for copy in rim_copies + halo_copies:
            copy.wait()

        def combined(a, b):
            return a if start else a + factor * b

        def place(i, carry):
            value = combined(part_a[rows_of(i), :], part_b[rows_of(i), :])
            est[i, 0:128, :] = value
            return carry

        lax.fori_loop(0, 8, place, 0)
        if start:
            est[8, 0:128, :] = solve(halo[0, 0])
            rims = solve(jnp.concatenate([rim_left[0, 0:8, :], rim_right[0, 0:8, :]], axis=0))
            from_left, from_right = rims[0:8], rims[8:16]
            own_first, own_last = own_rims[0], own_rims[1]
        else:
            est[8, 0:128, :] = combined(halo[turn, 0], halo[turn, 1])
            own_first = combined(rim_send[turn, 0, 0:8, :], rim_send[turn, 0, 8:16, :])
            own_last = combined(rim_send[turn, 1, 0:8, :], rim_send[turn, 1, 8:16, :])
            from_right = combined(rim_right[turn, 0:8, :], rim_right[turn, 8:16, :])
            from_left = combined(rim_left[turn, 0:8, :], rim_left[turn, 8:16, :])
        from_right = jnp.where(last_col > 0.0, own_last, from_right)
        from_left = jnp.where(first_col > 0.0, own_first, from_left)
        for i in range(8):
            est[i, 128:129, :] = from_right[i : i + 1, :]

        g_diff = own_first - from_left
        g_sum = g_diff if start else g_diff + factor * ghost[...]
        g_dual = jnp.clip(g_sum, -bound, bound)
        g_arg = g_diff - (g_sum - g_dual)
        ghost[...] = g_dual
        for i in range(8):
            right_arg[i, 7:8, :] = g_arg[i : i + 1, :]
            right_dual[i, 7:8, :] = g_dual[i : i + 1, :]

        def update(i, off, totals):
            at = pl.ds(off, CHUNK)
            shifted = pl.ds(off + 8, CHUNK)
            flat = pl.ds(pl.multiple_of(i * 128 + off, CHUNK), CHUNK)
            primal, dual, data = totals
            e = est[i, at, :]
            half = e.astype(BF16)
            gh = jnp.dot(jnp.concatenate([half, half], axis=1), gram2[...], preferred_element_type=F32)
            h = half.astype(F32)
            w = proj[flat, :]
            if start:
                data = data + fold(h * (gh - 2.0 * w))
                mix[flat, :] = h
                gram_mix[flat, :] = gh
            else:
                y, gy = mix[flat, :], gram_mix[flat, :]
                data = data + fold((h - pc * y) * (gh - pc * gy - (2.0 * sigma) * w))
                mix[flat, :] = h + scale_c * y
                gram_mix[flat, :] = gh + scale_c * gy
            t = e if start else e + factor * sparse_dual[flat, :]
            fresh = jnp.maximum(t - cut, 0.0)
            gap = e - fresh
            primal = primal + fold(gap * gap)
            move = fresh if start else fresh - sparse_var[flat, :]
            dual = dual + fold(move * move)
            sparse_var[flat, :] = fresh
            sparse_dual[flat, :] = t - fresh
            d = est[i + 1, at, :] - e
            t = d if start else d + factor * down_dual[flat, :]
            clipped = jnp.clip(t, -bound, bound)
            fresh = t - clipped
            gap = d - fresh
            move = fresh if start else fresh - down_var[flat, :]
            weight = jnp.where((i == 7) & (row == 1), 0.0, 1.0).astype(F32)
            primal = primal + weight * fold(gap * gap)
            dual = dual + weight * fold(move * move)
            down_var[flat, :] = fresh
            down_dual[flat, :] = clipped
            down_arg[flat, :] = gap
            d = est[i, pl.ds(off + 1, CHUNK), :] - e
            t = d if start else d + factor * right_dual[i, shifted, :]
            clipped = jnp.clip(t, -bound, bound)
            fresh = t - clipped
            gap = d - fresh
            primal = primal + fold(gap * gap)
            move = fresh if start else fresh - right_var[flat, :]
            dual = dual + fold(move * move)
            right_var[flat, :] = fresh
            right_dual[i, shifted, :] = clipped
            right_arg[i, shifted, :] = gap
            return primal, dual, data

        def update_row(i, totals):
            for off in range(0, 128, CHUNK):
                totals = update(i, off, totals)
            return totals

        zero = jnp.zeros((8, 128), F32)
        primal, dual, data = lax.fori_loop(0, 8, update_row, (zero, zero, zero))
        data = (data + (sigma * sigma) * square) * (share * share)
        line_p = jnp.sum(primal + data, axis=0, keepdims=True)
        line_d = jnp.sum(dual, axis=0, keepdims=True)
        line_p = line_p + pltpu.roll(line_p, 64, 1)
        line_d = line_d + pltpu.roll(line_d, 64, 1)
        line = jnp.where(lanes < 64, line_p, line_d)
        sums[turn, 0] = line
        send_pair(turn)

        final = turn == ITERS - 1

        def rhs(i):
            flat = rows_of(i)
            above = rows_of(jnp.maximum(i - 1, 0))
            has_above = jnp.where(i > 0, 1.0, 0.0).astype(F32)
            w = proj[flat, :]
            we = gram_mix[flat, :] - scale_s * w
            at = pl.ds(8, 128)
            before = pl.ds(7, 128)
            adj_a = (has_above * down_arg[above, :] - down_arg[flat, :]) + (
                right_arg[i, before, :] - right_arg[i, at, :]
            )
            adj_b = (has_above * down_dual[above, :] - down_dual[flat, :]) + (
                right_dual[i, before, :] - right_dual[i, at, :]
            )
            a = w + ratio * we + sparse_var[flat, :] + PROX * est[i, 0:128, :] - adj_a
            b = -(share * we + sparse_dual[flat, :] + adj_b)
            return a, b

        def prepare(i, carry):
            a, b = rhs(i)
            a, b = solve(a), solve(b)
            part_a[rows_of(i), :] = a
            part_b[rows_of(i), :] = b
            put_rims(turn + 1, i, 0, a)
            put_rims(turn + 1, i, 1, b)
            return carry

        def prepare_final(i, carry):
            a, b = rhs(i)
            out_ref[jnp.where(row == 1, 7 - i, i)] = solve_turned(a)
            turned = solve_turned(b)
            part_b[rows_of(i), 0:128] = turned[0:128, :]
            part_b[rows_of(i), 128:256] = turned[128:256, :]
            return carry

        work = prepare_final if final else prepare
        lax.fori_loop(0, 2, work, 0)
        wait_pair(turn, 1)
        line = line + pair[turn]
        sums[turn, 1] = line
        far[turn, pl.ds(col, 1), :] = line

        def send_all(n, carry):
            away = lax.div(n + 1, 2)
            send_sums(turn, jnp.where(lax.rem(n, 2) == 1, half - away, half + away), n == depth - 1)
            return carry

        lax.fori_loop(0, depth, send_all, 0)
        lax.fori_loop(2, 8, work, 0)
        if not final:
            rim_copies = send_rims(turn + 1)
            halo_copies = [send_halo(turn + 1, 0, part_a), send_halo(turn + 1, 1, part_b)]
        wait_far(turn, 1)
        line = jnp.sum(far[turn], axis=0, keepdims=True)
        total_p = jnp.sum(jnp.where(lanes < 64, line, 0.0), axis=1, keepdims=True)
        total_d = jnp.sum(jnp.where(lanes < 64, 0.0, line), axis=1, keepdims=True)
        root = jnp.sqrt(jnp.sqrt((total_p + 1.0) / (penalty * penalty * total_d + 1.0)))
        following = penalty * root
        rescale = penalty / following
        carry_c = rescale * share_v
        penalty = following

    factor = scalar(rescale)

    def finish(i, carry):
        at = jnp.where(row == 1, 7 - i, i)
        out_ref[at, 0:128, :] = out_ref[at, 0:128, :] + factor * part_b[rows_of(i), 0:128]
        out_ref[at, 128:256, :] = out_ref[at, 128:256, :] + factor * part_b[rows_of(i), 128:256]
        return carry

    lax.fori_loop(0, 8, finish, 0)
    for turn in range(ITERS):
        wait_pair(turn, 0)
        wait_far(turn, 0)


def run(sizes, observed, shard):
    ys, xs, depth = sizes
    cols = ys * xs * depth
    planes = ys * xs
    channels = 8 * cols
    field = pltpu.VMEM((1024, 256), F32)
    padded = pltpu.VMEM((8, PAD, 256), F32)
    rims = pltpu.VMEM((ITERS, 16, 256), F32)
    return pl.pallas_call(
        functools.partial(kernel, sizes),
        out_shape=jax.ShapeDtypeStruct((8, 256, 128), F32),
        in_specs=[pl.BlockSpec(memory_space=pl.ANY)] * 2,
        out_specs=VMEM,
        scratch_shapes=[
            pltpu.VMEM((channels, 8, 128), BF16),
            pltpu.VMEM((8, 256), BF16),
            pltpu.VMEM((channels * 8, 128), F32),
            pltpu.VMEM((1024, channels), BF16),
            pltpu.VMEM((16, 128), BF16),
            pltpu.VMEM((cols, 16, 128), BF16),
            pltpu.VMEM((channels, 256), BF16),
            pltpu.VMEM((72, 128), F32),
            pltpu.VMEM((256, 256), F32),
            pltpu.VMEM((512, 256), BF16),
            pltpu.VMEM((768, 256), BF16),
            field,
            pltpu.VMEM((2, 8, 256), F32),
            pltpu.VMEM((9, PAD, 256), F32),
            field,
            field,
            pltpu.VMEM((ITERS, 2, 16, 256), F32),
            rims,
            rims,
            pltpu.VMEM((ITERS, 2, 128, 256), F32),
            pltpu.VMEM((8, 256), F32),
            field,
            field,
            field,
            field,
            field,
            field,
            padded,
            padded,
            field,
            field,
            pltpu.VMEM((ITERS, 2, 1, 128), F32),
            pltpu.VMEM((ITERS, 1, 128), F32),
            pltpu.VMEM((ITERS, cols, 128), F32),
            pltpu.SemaphoreType.DMA(()),
            pltpu.SemaphoreType.DMA(()),
            pltpu.SemaphoreType.DMA((5,)),
            pltpu.SemaphoreType.DMA((planes,)),
            pltpu.SemaphoreType.DMA((2, ITERS, 2)),
            pltpu.SemaphoreType.DMA((2, ITERS, 2)),
            pltpu.SemaphoreType.DMA((2, ITERS, 2)),
        ],
        compiler_params=pltpu.CompilerParams(
            collective_id=0, has_side_effects=True, vmem_limit_bytes=125 * 2**19
        ),
        name="unmix",
    )(observed, shard)


def on_device(sizes, observed, library):
    return run(sizes, observed, library).transpose(1, 0, 2)


def solution(mesh):
    sizes = (4, 4, 8) if mesh.shape["col"] == 128 else (2, 2, 2)
    return jax.shard_map(
        functools.partial(on_device, sizes),
        mesh=mesh,
        in_specs=(P(None, "row", "col"), P("col", None)),
        out_specs=P(None, "row", "col"),
        check_vma=False,
    )
```

```python
import functools

import jax
import jax.numpy as jnp
from jax import lax
from jax.experimental import pallas as pl
from jax.experimental.pallas import tpu as pltpu
from jax.sharding import PartitionSpec as P

ITERS = 3
PROX = 8.0
WEIGHT_SPARSE = 0.3
WEIGHT_TV = 1.0
MESH = pl.DeviceIdType.MESH
F32 = jnp.float32
BF16 = jnp.bfloat16
VMEM = pl.BlockSpec(memory_space=pltpu.VMEM)


def slot_of(col, depth, cols):
    plane, z = col // depth, col % depth
    half = depth // 2
    return (z % 2) * (cols // 2) + plane * half + z // 2


def dot_of(x, y):
    t = [a * b for a, b in zip(x, y)]
    while len(t) > 1:
        t = [t[i] + t[i + 1] if i + 1 < len(t) else t[i] for i in range(0, len(t), 2)]
    return t[0]

def symmetric_inverse(m):
    n = len(m)
    if n == 1:
        return [[1.0 / m[0][0]]]
    if n == 2:
        scale = 1.0 / (m[0][0] * m[1][1] - m[0][1] * m[0][1])
        off = -m[0][1] * scale
        return [[m[1][1] * scale, off], [off, m[0][0] * scale]]
    h = n // 2
    a = symmetric_inverse([r[:h] for r in m[:h]])
    b = [r[h:] for r in m[:h]]
    bt = [list(c) for c in zip(*b)]
    t = [[dot_of(a[i], bt[j]) for j in range(h)] for i in range(h)]
    tt = [list(c) for c in zip(*t)]
    s = [[None] * h for _ in range(h)]
    for i in range(h):
        for j in range(i, h):
            s[i][j] = s[j][i] = m[h + i][h + j] - dot_of(bt[i], tt[j])
    s = symmetric_inverse(s)
    u = [[dot_of(t[i], s[j]) for j in range(h)] for i in range(h)]
    top = [[None] * h for _ in range(h)]
    for i in range(h):
        for j in range(i, h):
            top[i][j] = top[j][i] = a[i][j] + dot_of(u[i], t[j])
    out = [[None] * n for _ in range(n)]
    for i in range(h):
        for j in range(h):
            out[i][j] = top[i][j]
            out[h + i][h + j] = s[i][j]
            out[i][h + j] = -u[i][j]
            out[h + j][i] = -u[i][j]
    return out

def eliminate(matrix, ref):
    size, step = 128, 8
    groups = [matrix[8 * g : 8 * g + 8, :] for g in range(size // 8)]
    lane = lax.broadcasted_iota(jnp.int32, (8, size), 1)
    place = lax.broadcasted_iota(jnp.int32, (8, size), 0)
    full = (8, size)
    for home, first in enumerate(range(0, size, step)):

        def cols_of(g):
            return [jnp.broadcast_to(g[:, first + a : first + a + 1], full) for a in range(step)]

        home_cols = cols_of(groups[home])
        ref[0:8, :] = groups[home]
        for b in range(step):
            ref[8 + 8 * b : 16 + 8 * b, :] = home_cols[b]
        line = [jnp.broadcast_to(ref[a : a + 1, :], full) for a in range(step)]
        pivot = [[None] * step for _ in range(step)]
        for a in range(step):
            for b in range(a, step):
                spot = 8 + 8 * b + a
                pivot[a][b] = pivot[b][a] = jnp.broadcast_to(ref[spot : spot + 1, :], full)
        turned = symmetric_inverse(pivot)
        inside = (lane >= first) & (lane < first + step)
        rows = [jnp.where(lane == first + a, 1.0, jnp.where(inside, 0.0, line[a])) for a in range(step)]
        fresh = [dot_of(turned[a], rows) for a in range(step)]
        nxt = []
        for g, group in enumerate(groups):
            if g == home:
                value = fresh[0]
                for a in range(1, step):
                    value = jnp.where(place == a, fresh[a], value)
            else:
                value = jnp.where(inside, 0.0, group) - dot_of(cols_of(group), fresh)
            nxt.append(value)
        groups = nxt
    return jnp.concatenate(groups, axis=0)


def exact_dot(a, b, dims):
    return lax.dot_general(a, b, (dims, ((), ())), precision=lax.Precision.HIGHEST, preferred_element_type=F32)


def split2(x):
    high = x.astype(BF16)
    return high, (x - high.astype(F32)).astype(BF16)


CHUNK = 32
PAD = 136


def fold(x):
    total = None
    for k in range(x.shape[0] // 8):
        for half in range(2):
            part = x[8 * k : 8 * k + 8, 128 * half : 128 * half + 128]
            total = part if total is None else total + part
    return total


def kernel(
    sizes,
    obs_ref,
    shard_ref,
    out_a,
    out_b,
    out_r,
    obs,
    own_shard,
    wide,
    turned_obs,
    packed,
    shards,
    lib,
    work_rows,
    inverse,
    gram2,
    inv3,
    proj,
    own_rims,
    est,
    part_a,
    part_b,
    rim_send,
    rim_left,
    rim_right,
    halo,
    ghost,
    sparse_var,
    sparse_dual,
    down_var,
    down_dual,
    down_arg,
    right_var,
    right_dual,
    right_arg,
    gram_mix,
    sums,
    pair,
    far,
    obs_sem,
    shard_sem,
    gather_sem,
    plane_sem,
    halo_sem,
    rim_sem,
    sum_sem,
    result_sem,
):
    ys, xs, depth = sizes
    planes, half = ys * xs, depth // 2
    cols = planes * depth
    channels = 8 * cols
    row, col = lax.axis_index("row"), lax.axis_index("col")
    plane, z = lax.div(col, depth), lax.rem(col, depth)
    y, x = lax.div(plane, xs), lax.rem(plane, xs)
    parity = lax.rem(z, 2)
    flip = row == 1
    core_peer = (1 - row, col)
    left = (row, lax.rem(col + cols - 1, cols))
    right = (row, lax.rem(col + 1, cols))

    def peer_at(dy, dx, dz):
        return (row, (lax.rem(y + dy, ys) * xs + lax.rem(x + dx, xs)) * depth + lax.rem(z + dz, depth))

    def z_peer(step):
        return peer_at(0, 0, step)

    def plane_peer(step):
        return peer_at(step // xs, step % xs, 0)

    obs_copy = pltpu.make_async_copy(obs_ref, obs, obs_sem)
    obs_copy.start()
    shard_copy = pltpu.make_async_copy(shard_ref, own_shard, shard_sem)
    shard_copy.start()
    barrier = pltpu.get_barrier_semaphore()
    peers = [z_peer(n) for n in range(1, depth)] + [plane_peer(n) for n in range(1, planes)] + [core_peer]
    for peer in peers:
        pl.semaphore_signal(barrier, inc=1, device_id=peer, device_id_type=MESH)
    shard_copy.wait()
    shard = own_shard[...].astype(F32)
    packed[...] = jnp.concatenate([shard[:, :128], shard[:, 128:]], axis=0).astype(BF16)
    mine = parity * (cols // 2) + plane * half + lax.div(z, 2)
    obs_copy.wait()

    def widen(k, total):
        base = pl.multiple_of(k * 16, 16)
        part = obs[pl.ds(base, 16)].astype(F32)
        wide[pl.ds(pl.multiple_of(base * 8, 128), 128), :] = part.reshape(128, 128)
        return total + jnp.sum(part * part, axis=0)

    square = lax.fori_loop(0, channels // 16, widen, jnp.zeros((8, 128), F32))
    pl.semaphore_wait(barrier, len(peers))

    @pl.when(row == parity)
    def _():
        for step in range(1, depth):
            pltpu.make_async_remote_copy(
                src_ref=packed,
                dst_ref=shards.at[mine],
                send_sem=gather_sem.at[0],
                recv_sem=gather_sem.at[1],
                device_id=z_peer(step),
                device_id_type=MESH,
            ).start()
        shards[mine] = packed[...]

    def turn_rows(i, carry):
        source = jnp.where(flip, 7 - i, i)
        part = wide[pl.ds(source, channels, stride=8), :]
        turned_obs[pl.ds(pl.multiple_of(i * 128, 128), 128), :] = part.T.astype(BF16)
        return carry

    lax.fori_loop(0, 4, turn_rows, 0)

    @pl.when(row == parity)
    def _():
        if half > 1:
            got = shards.at[pl.ds(0, half - 1)]
            pltpu.make_async_copy(got, got, gather_sem.at[1]).wait()

    @pl.when(row != parity)
    def _():
        got = shards.at[pl.ds(0, half)]
        pltpu.make_async_copy(got, got, gather_sem.at[1]).wait()

    def block_of(dy, dx):
        other = lax.rem(y + ys - dy, ys) * xs + lax.rem(x + xs - dx, xs)
        return shards.at[pl.ds(row * (cols // 2) + other * half, half)]

    def pass_over(block):
        pltpu.make_async_remote_copy(
            src_ref=block,
            dst_ref=block,
            send_sem=gather_sem.at[3],
            recv_sem=gather_sem.at[4],
            device_id=core_peer,
            device_id_type=MESH,
        ).start()

    block = block_of(0, 0)
    for step in range(1, planes):
        pltpu.make_async_remote_copy(
            src_ref=block,
            dst_ref=block,
            send_sem=gather_sem.at[2],
            recv_sem=plane_sem.at[step],
            device_id=plane_peer(step),
            device_id_type=MESH,
        ).start()
    pass_over(block)
    lax.fori_loop(4, 8, turn_rows, 0)
    nearest = sorted(range(1, planes), key=lambda n: min(n // xs, ys - n // xs) + min(n % xs, xs - n % xs))
    for step in nearest:
        got = block_of(step // xs, step % xs)
        pltpu.make_async_copy(got, got, plane_sem.at[step]).wait()
        pass_over(got)
    other_half = shards.at[pl.ds((1 - row) * (cols // 2), cols // 2)]
    pltpu.make_async_copy(other_half, other_half, gather_sem.at[4]).wait()

    @pl.when(row == parity)
    def _():
        sent = shards.at[pl.ds(0, depth - 1)]
        pltpu.make_async_copy(sent, sent, gather_sem.at[0]).wait()

    sent = shards.at[pl.ds(0, half * (planes - 1))]
    pltpu.make_async_copy(sent, sent, gather_sem.at[2]).wait()
    pltpu.make_async_copy(other_half, other_half, gather_sem.at[3]).wait()

    for two in range(cols // 2):
        one = shards[slot_of(2 * two, depth, cols)].astype(F32)
        other = shards[slot_of(2 * two + 1, depth, cols)].astype(F32)
        lib[16 * two : 16 * two + 16, 0:128] = jnp.concatenate([one[0:8], other[0:8]], axis=0).astype(BF16)
        lib[16 * two : 16 * two + 16, 128:256] = jnp.concatenate([one[8:16], other[8:16]], axis=0).astype(BF16)

    def rows_of(x):
        return pl.ds(pl.multiple_of(x * 128, 128), 128)

    def send_halo(turn, slot, field):
        copy = pltpu.make_async_remote_copy(
            src_ref=field.at[rows_of(7)],
            dst_ref=halo.at[turn, slot],
            send_sem=halo_sem.at[0, turn, slot],
            recv_sem=halo_sem.at[1, turn, slot],
            device_id=core_peer,
            device_id_type=MESH,
        )
        copy.start()
        return copy

    def send_rims(turn):
        used = 8 if turn == 0 else 16
        to_left = pltpu.make_async_remote_copy(
            src_ref=rim_send.at[turn, 0, pl.ds(0, used)],
            dst_ref=rim_right.at[turn, pl.ds(0, used)],
            send_sem=rim_sem.at[0, turn, 0],
            recv_sem=rim_sem.at[1, turn, 0],
            device_id=left,
            device_id_type=MESH,
        )
        to_right = pltpu.make_async_remote_copy(
            src_ref=rim_send.at[turn, 1, pl.ds(0, used)],
            dst_ref=rim_left.at[turn, pl.ds(0, used)],
            send_sem=rim_sem.at[0, turn, 1],
            recv_sem=rim_sem.at[1, turn, 1],
            device_id=right,
            device_id_type=MESH,
        )
        to_left.start()
        to_right.start()
        return [to_left, to_right]

    library = lib[...]
    gram = lax.dot_general(library, library, (((0,), (0,)), ((), ())), preferred_element_type=F32)
    high, low = split2(gram)
    gram2[0:256, :] = high
    gram2[256:512, :] = low
    same = lax.broadcasted_iota(jnp.int32, (256, 256), 0) == lax.broadcasted_iota(jnp.int32, (256, 256), 1)
    system = gram + jnp.where(same, 1.0 + PROX, 0.0)
    for i in range(8):
        value = jnp.dot(turned_obs[128 * i : 128 * i + 128, :], lib[...], preferred_element_type=F32)
        proj[128 * i : 128 * i + 128, :] = value
        rim_send[0, 0, i : i + 1, :] = value[0:1, :]
        rim_send[0, 1, i : i + 1, :] = value[127:128, :]

    first_inverse = eliminate(system[:128, :128], work_rows)
    rim_copies = send_rims(0)
    halo_copies = [send_halo(0, 0, proj)]
    lead = exact_dot(first_inverse, system[:128, 128:], ((1,), (0,)))
    last_inverse = eliminate(
        system[128:, 128:] - exact_dot(system[128:, :128], lead, ((1,), (0,))), work_rows
    )
    corner = -exact_dot(lead, last_inverse, ((1,), (0,)))
    inverse[0:128, 0:128] = first_inverse - exact_dot(corner, lead, ((1,), (1,)))
    inverse[0:128, 128:256] = corner
    inverse[128:256, 0:128] = -exact_dot(last_inverse, lead, ((1,), (1,)))
    inverse[128:256, 128:256] = last_inverse
    high, low = split2(inverse[...])
    inv3[0:256, :] = high
    inv3[256:512, :] = low
    inv3[512:768, :] = high

    def stacked(x):
        one, two = split2(x)
        return jnp.concatenate([one, one, two], axis=1)

    def solve(x):
        return jnp.dot(stacked(x), inv3[...], preferred_element_type=F32)

    def solve_turned(x):
        one, two = split2(x)
        dims = (((1,), (1,)), ((), ()))
        total = lax.dot_general(inv3[0:256, :], one, dims, preferred_element_type=F32)
        total = total + lax.dot_general(inv3[256:512, :], one, dims, preferred_element_type=F32)
        return total + lax.dot_general(inv3[0:256, :], two, dims, preferred_element_type=F32)

    def put_rims(turn, i, slot, value):
        rim_send[turn, 0, pl.ds(8 * slot + i, 1), :] = value[0:1, :]
        rim_send[turn, 1, pl.ds(8 * slot + i, 1), :] = value[127:128, :]

    for i in range(8):
        value = solve(proj[128 * i : 128 * i + 128, :])
        part_a[128 * i : 128 * i + 128, :] = value
        own_rims[0, i : i + 1, :] = value[0:1, :]
        own_rims[1, i : i + 1, :] = value[127:128, :]

    def send_pair(turn):
        pltpu.make_async_remote_copy(
            src_ref=sums.at[turn, 0],
            dst_ref=pair.at[turn],
            send_sem=sum_sem.at[0, turn, 0],
            recv_sem=sum_sem.at[1, turn, 0],
            device_id=core_peer,
            device_id_type=MESH,
        ).start()

    def send_sums(turn, dz, alone):
        for dy in range(ys):
            for dx in range(xs):
                copy = pltpu.make_async_remote_copy(
                    src_ref=sums.at[turn, 1],
                    dst_ref=far.at[turn, pl.ds(col, 1)],
                    send_sem=sum_sem.at[0, turn, 1],
                    recv_sem=sum_sem.at[1, turn, 1],
                    device_id=peer_at(dy, dx, dz),
                    device_id_type=MESH,
                )
                if dy or dx:
                    copy.start()
                else:
                    pl.when(jnp.logical_not(alone))(copy.start)

    def wait_pair(turn, which):
        pltpu.make_async_copy(pair.at[turn], pair.at[turn], sum_sem.at[which, turn, 0]).wait()

    def wait_far(turn, which):
        got = far.at[turn, pl.ds(0, cols - 1)]
        pltpu.make_async_copy(got, got, sum_sem.at[which, turn, 1]).wait()

    first_col = jnp.where(col == 0, 1.0, 0.0).astype(F32)
    last_col = jnp.where(col == cols - 1, 1.0, 0.0).astype(F32)
    lanes = lax.broadcasted_iota(jnp.int32, (1, 128), 1)
    penalty, rescale, carry_c, carry_s = 1.0, 0.0, 0.0, 0.0

    def scalar(x):
        return x if isinstance(x, float) else x[0, 0]

    for turn in range(ITERS):
        start = turn == 0
        old_c, old_s = carry_c, carry_s
        pc_v = penalty * old_c
        sigma_v = 1.0 - pc_v * old_s
        share_v = 1.0 / (1.0 + penalty)
        carry_s = 1.0 + old_c * old_s
        bound, cut = scalar(WEIGHT_TV / penalty), scalar(WEIGHT_SPARSE / penalty)
        pc, sigma, scale_c = scalar(pc_v), scalar(sigma_v), scalar(old_c)
        share, ratio, scale_s = scalar(share_v), scalar(penalty * share_v), scalar(carry_s)
        factor = scalar(rescale)
        for copy in rim_copies + halo_copies:
            copy.wait()

        def combined(a, b):
            return a if start else a + factor * b

        def place(i, carry):
            value = combined(part_a[rows_of(i), :], part_b[rows_of(i), :])
            est[i, 0:128, :] = value
            return carry

        lax.fori_loop(0, 8, place, 0)
        if start:
            est[8, 0:128, :] = solve(halo[0, 0])
            rims = solve(jnp.concatenate([rim_left[0, 0:8, :], rim_right[0, 0:8, :]], axis=0))
            from_left, from_right = rims[0:8], rims[8:16]
            own_first, own_last = own_rims[0], own_rims[1]
        else:
            est[8, 0:128, :] = combined(halo[turn, 0], halo[turn, 1])
            own_first = combined(rim_send[turn, 0, 0:8, :], rim_send[turn, 0, 8:16, :])
            own_last = combined(rim_send[turn, 1, 0:8, :], rim_send[turn, 1, 8:16, :])
            from_right = combined(rim_right[turn, 0:8, :], rim_right[turn, 8:16, :])
            from_left = combined(rim_left[turn, 0:8, :], rim_left[turn, 8:16, :])
        from_right = jnp.where(last_col > 0.0, own_last, from_right)
        from_left = jnp.where(first_col > 0.0, own_first, from_left)
        for i in range(8):
            est[i, 128:129, :] = from_right[i : i + 1, :]

        g_diff = own_first - from_left
        g_sum = g_diff if start else g_diff + factor * ghost[...]
        g_dual = jnp.clip(g_sum, -bound, bound)
        g_arg = g_diff - (g_sum - g_dual)
        ghost[...] = g_dual
        for i in range(8):
            right_arg[i, 7:8, :] = g_arg[i : i + 1, :]
            right_dual[i, 7:8, :] = g_dual[i : i + 1, :]

        def update(i, off, totals):
            at = pl.ds(off, CHUNK)
            shifted = pl.ds(off + 8, CHUNK)
            flat = pl.ds(pl.multiple_of(i * 128 + off, CHUNK), CHUNK)
            primal, dual, quad, cross, along = totals
            e = est[i, at, :]
            half = e.astype(BF16)
            gh = jnp.dot(jnp.concatenate([half, half], axis=1), gram2[...], preferred_element_type=F32)
            h = half.astype(F32)
            w = proj[flat, :]
            quad = quad + fold(h * gh)
            along = along + fold(h * w)
            if start:
                gram_mix[flat, :] = gh
            else:
                gy = gram_mix[flat, :]
                cross = cross + fold(h * gy)
                gram_mix[flat, :] = gh + scale_c * gy
            t = e if start else e + factor * sparse_dual[flat, :]
            fresh = jnp.maximum(t - cut, 0.0)
            gap = e - fresh
            primal = primal + fold(gap * gap)
            move = fresh if start else fresh - sparse_var[flat, :]
            dual = dual + fold(move * move)
            sparse_var[flat, :] = fresh
            sparse_dual[flat, :] = t - fresh
            d = est[i + 1, at, :] - e
            t = d if start else d + factor * down_dual[flat, :]
            clipped = jnp.clip(t, -bound, bound)
            fresh = t - clipped
            gap = d - fresh
            move = fresh if start else fresh - down_var[flat, :]
            weight = jnp.where((i == 7) & (row == 1), 0.0, 1.0).astype(F32)
            primal = primal + weight * fold(gap * gap)
            dual = dual + weight * fold(move * move)
            down_var[flat, :] = fresh
            down_dual[flat, :] = clipped
            down_arg[flat, :] = gap
            d = est[i, pl.ds(off + 1, CHUNK), :] - e
            t = d if start else d + factor * right_dual[i, shifted, :]
            clipped = jnp.clip(t, -bound, bound)
            fresh = t - clipped
            gap = d - fresh
            primal = primal + fold(gap * gap)
            move = fresh if start else fresh - right_var[flat, :]
            dual = dual + fold(move * move)
            right_var[flat, :] = fresh
            right_dual[i, shifted, :] = clipped
            right_arg[i, shifted, :] = gap
            return primal, dual, quad, cross, along

        def update_row(i, totals):
            for off in range(0, 128, CHUNK):
                totals = update(i, off, totals)
            return totals

        zero = jnp.zeros((8, 128), F32)
        primal, dual, quad, cross, along = lax.fori_loop(0, 8, update_row, (zero,) * 5)
        data = quad - 2.0 * along + square
        if not start:
            data = (quad - (2.0 * pc) * cross + (pc * pc) * old_quad) - (2.0 * sigma) * (along - pc * old_along)
            data = data + (sigma * sigma) * square
            quad = quad + (2.0 * scale_c) * cross + (scale_c * scale_c) * old_quad
            along = along + scale_c * old_along
        data = data * (share * share)
        old_quad, old_along = quad, along
        line_p = jnp.sum(primal + data, axis=0, keepdims=True)
        line_d = jnp.sum(dual, axis=0, keepdims=True)
        line_p = line_p + pltpu.roll(line_p, 64, 1)
        line_d = line_d + pltpu.roll(line_d, 64, 1)
        line = jnp.where(lanes < 64, line_p, line_d)
        sums[turn, 0] = line
        send_pair(turn)

        final = turn == ITERS - 1

        def rhs(i):
            flat = rows_of(i)
            above = rows_of(jnp.maximum(i - 1, 0))
            has_above = jnp.where(i > 0, 1.0, 0.0).astype(F32)
            w = proj[flat, :]
            we = gram_mix[flat, :] - scale_s * w
            at = pl.ds(8, 128)
            before = pl.ds(7, 128)
            adj_a = (has_above * down_arg[above, :] - down_arg[flat, :]) + (
                right_arg[i, before, :] - right_arg[i, at, :]
            )
            adj_b = (has_above * down_dual[above, :] - down_dual[flat, :]) + (
                right_dual[i, before, :] - right_dual[i, at, :]
            )
            a = w + ratio * we + sparse_var[flat, :] + PROX * est[i, 0:128, :] - adj_a
            b = -(share * we + sparse_dual[flat, :] + adj_b)
            return a, b

        def prepare(i, carry):
            a, b = rhs(i)
            a, b = solve(a), solve(b)
            part_a[rows_of(i), :] = a
            part_b[rows_of(i), :] = b
            put_rims(turn + 1, i, 0, a)
            put_rims(turn + 1, i, 1, b)
            return carry

        def prepare_final(i, carry):
            a, b = rhs(i)
            spot = jnp.where(flip, 7 - i, i)
            wide[pl.ds(spot, 256, stride=8), :] = solve_turned(a)
            wide[pl.ds(2048 + spot, 256, stride=8), :] = solve_turned(b)
            return carry

        work = prepare_final if final else prepare
        lax.fori_loop(0, 2, work, 0)
        wait_pair(turn, 1)
        line = line + pair[turn]
        sums[turn, 1] = line
        far[turn, pl.ds(col, 1), :] = line

        def send_all(n, carry):
            away = lax.div(n + 1, 2)
            send_sums(turn, jnp.where(lax.rem(n, 2) == 1, half - away, half + away), n == depth - 1)
            return carry

        lax.fori_loop(0, depth, send_all, 0)
        lax.fori_loop(2, 8, work, 0)
        if not final:
            rim_copies = send_rims(turn + 1)
            halo_copies = [send_halo(turn + 1, 0, part_a), send_halo(turn + 1, 1, part_b)]
        else:
            results = [
                pltpu.make_async_copy(wide.at[pl.ds(2048 * n, 2048)], ref, result_sem.at[n])
                for n, ref in enumerate((out_a, out_b))
            ]
            for copy in results:
                copy.start()
        wait_far(turn, 1)
        line = jnp.sum(far[turn], axis=0, keepdims=True)
        total_p = jnp.sum(jnp.where(lanes < 64, line, 0.0), axis=1, keepdims=True)
        total_d = jnp.sum(jnp.where(lanes < 64, 0.0, line), axis=1, keepdims=True)
        root = jnp.sqrt(jnp.sqrt((total_p + 1.0) / (penalty * penalty * total_d + 1.0)))
        following = penalty * root
        rescale = penalty / following
        carry_c = rescale * share_v
        penalty = following

    out_r[...] = jnp.broadcast_to(rescale, (8, 128))
    for copy in results:
        copy.wait()
    for turn in range(ITERS):
        wait_pair(turn, 0)
        wait_far(turn, 0)


def run(sizes, observed, shard):
    ys, xs, depth = sizes
    cols = ys * xs * depth
    planes = ys * xs
    channels = 8 * cols
    field = pltpu.VMEM((1024, 256), F32)
    padded = pltpu.VMEM((8, PAD, 256), F32)
    rims = pltpu.VMEM((ITERS, 16, 256), F32)
    return pl.pallas_call(
        functools.partial(kernel, sizes),
        out_shape=[
            jax.ShapeDtypeStruct((2048, 128), F32),
            jax.ShapeDtypeStruct((2048, 128), F32),
            jax.ShapeDtypeStruct((8, 128), F32),
        ],
        in_specs=[pl.BlockSpec(memory_space=pl.ANY)] * 2,
        out_specs=[pl.BlockSpec(memory_space=pl.ANY)] * 2 + [VMEM],
        scratch_shapes=[
            pltpu.VMEM((channels, 8, 128), BF16),
            pltpu.VMEM((8, 256), BF16),
            pltpu.VMEM((max(channels * 8, 4096), 128), F32),
            pltpu.VMEM((1024, channels), BF16),
            pltpu.VMEM((16, 128), BF16),
            pltpu.VMEM((cols, 16, 128), BF16),
            pltpu.VMEM((channels, 256), BF16),
            pltpu.VMEM((72, 128), F32),
            pltpu.VMEM((256, 256), F32),
            pltpu.VMEM((512, 256), BF16),
            pltpu.VMEM((768, 256), BF16),
            field,
            pltpu.VMEM((2, 8, 256), F32),
            pltpu.VMEM((9, PAD, 256), F32),
            field,
            field,
            pltpu.VMEM((ITERS, 2, 16, 256), F32),
            rims,
            rims,
            pltpu.VMEM((ITERS, 2, 128, 256), F32),
            pltpu.VMEM((8, 256), F32),
            field,
            field,
            field,
            field,
            field,
            field,
            padded,
            padded,
            field,
            pltpu.VMEM((ITERS, 2, 1, 128), F32),
            pltpu.VMEM((ITERS, 1, 128), F32),
            pltpu.VMEM((ITERS, cols, 128), F32),
            pltpu.SemaphoreType.DMA(()),
            pltpu.SemaphoreType.DMA(()),
            pltpu.SemaphoreType.DMA((5,)),
            pltpu.SemaphoreType.DMA((planes,)),
            pltpu.SemaphoreType.DMA((2, ITERS, 2)),
            pltpu.SemaphoreType.DMA((2, ITERS, 2)),
            pltpu.SemaphoreType.DMA((2, ITERS, 2)),
            pltpu.SemaphoreType.DMA((2,)),
        ],
        compiler_params=pltpu.CompilerParams(
            collective_id=0, has_side_effects=True, vmem_limit_bytes=125 * 2**19
        ),
        name="unmix",
    )(observed, shard)


def on_device(sizes, observed, library):
    a, b, rescale = run(sizes, observed, library)
    return (a + rescale[0, 0] * b).reshape(256, 8, 128)


def solution(mesh):
    sizes = (4, 4, 8) if mesh.shape["col"] == 128 else (2, 2, 2)
    return jax.shard_map(
        functools.partial(on_device, sizes),
        mesh=mesh,
        in_specs=(P(None, "row", "col"), P("col", None)),
        out_specs=P(None, "row", "col"),
        check_vma=False,
    )
```

```python
import functools

import jax
import jax.numpy as jnp
from jax import lax
from jax.experimental import pallas as pl
from jax.experimental.pallas import tpu as pltpu
from jax.sharding import PartitionSpec as P

ITERS = 3
PROX = 8.0
WEIGHT_SPARSE = 0.3
WEIGHT_TV = 1.0
MESH = pl.DeviceIdType.MESH
F32 = jnp.float32
BF16 = jnp.bfloat16
VMEM = pl.BlockSpec(memory_space=pltpu.VMEM)


def slot_of(col, depth, cols):
    plane, z = col // depth, col % depth
    half = depth // 2
    return (z % 2) * (cols // 2) + plane * half + z // 2


def dot_of(x, y):
    t = [a * b for a, b in zip(x, y)]
    while len(t) > 1:
        t = [t[i] + t[i + 1] if i + 1 < len(t) else t[i] for i in range(0, len(t), 2)]
    return t[0]

def symmetric_inverse(m):
    n = len(m)
    if n == 1:
        return [[1.0 / m[0][0]]]
    if n == 2:
        scale = 1.0 / (m[0][0] * m[1][1] - m[0][1] * m[0][1])
        off = -m[0][1] * scale
        return [[m[1][1] * scale, off], [off, m[0][0] * scale]]
    h = n // 2
    a = symmetric_inverse([r[:h] for r in m[:h]])
    b = [r[h:] for r in m[:h]]
    bt = [list(c) for c in zip(*b)]
    t = [[dot_of(a[i], bt[j]) for j in range(h)] for i in range(h)]
    tt = [list(c) for c in zip(*t)]
    s = [[None] * h for _ in range(h)]
    for i in range(h):
        for j in range(i, h):
            s[i][j] = s[j][i] = m[h + i][h + j] - dot_of(bt[i], tt[j])
    s = symmetric_inverse(s)
    u = [[dot_of(t[i], s[j]) for j in range(h)] for i in range(h)]
    top = [[None] * h for _ in range(h)]
    for i in range(h):
        for j in range(i, h):
            top[i][j] = top[j][i] = a[i][j] + dot_of(u[i], t[j])
    out = [[None] * n for _ in range(n)]
    for i in range(h):
        for j in range(h):
            out[i][j] = top[i][j]
            out[h + i][h + j] = s[i][j]
            out[i][h + j] = -u[i][j]
            out[h + j][i] = -u[i][j]
    return out

def eliminate(matrix, ref):
    size, step = 128, 8
    groups = [matrix[8 * g : 8 * g + 8, :] for g in range(size // 8)]
    lane = lax.broadcasted_iota(jnp.int32, (8, size), 1)
    place = lax.broadcasted_iota(jnp.int32, (8, size), 0)
    full = (8, size)
    for home, first in enumerate(range(0, size, step)):

        def cols_of(g):
            return [jnp.broadcast_to(g[:, first + a : first + a + 1], full) for a in range(step)]

        home_cols = cols_of(groups[home])
        ref[0:8, :] = groups[home]
        for b in range(step):
            ref[8 + 8 * b : 16 + 8 * b, :] = home_cols[b]
        line = [jnp.broadcast_to(ref[a : a + 1, :], full) for a in range(step)]
        pivot = [[None] * step for _ in range(step)]
        for a in range(step):
            for b in range(a, step):
                spot = 8 + 8 * b + a
                pivot[a][b] = pivot[b][a] = jnp.broadcast_to(ref[spot : spot + 1, :], full)
        turned = symmetric_inverse(pivot)
        inside = (lane >= first) & (lane < first + step)
        rows = [jnp.where(lane == first + a, 1.0, jnp.where(inside, 0.0, line[a])) for a in range(step)]
        fresh = [dot_of(turned[a], rows) for a in range(step)]
        nxt = []
        for g, group in enumerate(groups):
            if g == home:
                value = fresh[0]
                for a in range(1, step):
                    value = jnp.where(place == a, fresh[a], value)
            else:
                value = jnp.where(inside, 0.0, group) - dot_of(cols_of(group), fresh)
            nxt.append(value)
        groups = nxt
    return jnp.concatenate(groups, axis=0)


def exact_dot(a, b, dims):
    return lax.dot_general(a, b, (dims, ((), ())), precision=lax.Precision.HIGHEST, preferred_element_type=F32)


def split2(x):
    high = x.astype(BF16)
    return high, (x - high.astype(F32)).astype(BF16)


CHUNK = 32
PAD = 136


def fold(x):
    total = None
    for k in range(x.shape[0] // 8):
        for half in range(2):
            part = x[8 * k : 8 * k + 8, 128 * half : 128 * half + 128]
            total = part if total is None else total + part
    return total


def kernel(
    sizes,
    obs_ref,
    shard_ref,
    out_ref,
    obs,
    own_shard,
    wide,
    turned_obs,
    packed,
    shards,
    lib,
    work_rows,
    inverse,
    gram2,
    inv3,
    proj,
    own_rims,
    est,
    part_a,
    part_b,
    rim_send,
    rim_left,
    rim_right,
    halo,
    ghost,
    sparse_var,
    sparse_dual,
    down_var,
    down_dual,
    down_arg,
    right_var,
    right_dual,
    right_arg,
    gram_mix,
    sums,
    pair,
    far,
    obs_sem,
    shard_sem,
    gather_sem,
    plane_sem,
    halo_sem,
    rim_sem,
    sum_sem,
):
    ys, xs, depth = sizes
    planes, half = ys * xs, depth // 2
    cols = planes * depth
    channels = 8 * cols
    row, col = lax.axis_index("row"), lax.axis_index("col")
    plane, z = lax.div(col, depth), lax.rem(col, depth)
    y, x = lax.div(plane, xs), lax.rem(plane, xs)
    parity = lax.rem(z, 2)
    flip = row == 1
    core_peer = (1 - row, col)
    left = (row, lax.rem(col + cols - 1, cols))
    right = (row, lax.rem(col + 1, cols))

    def peer_at(dy, dx, dz):
        return (row, (lax.rem(y + dy, ys) * xs + lax.rem(x + dx, xs)) * depth + lax.rem(z + dz, depth))

    def z_peer(step):
        return peer_at(0, 0, step)

    def plane_peer(step):
        return peer_at(step // xs, step % xs, 0)

    obs_copy = pltpu.make_async_copy(obs_ref, obs, obs_sem)
    obs_copy.start()
    shard_copy = pltpu.make_async_copy(shard_ref, own_shard, shard_sem)
    shard_copy.start()
    barrier = pltpu.get_barrier_semaphore()
    peers = [z_peer(n) for n in range(1, depth)] + [plane_peer(n) for n in range(1, planes)] + [core_peer]
    for peer in peers:
        pl.semaphore_signal(barrier, inc=1, device_id=peer, device_id_type=MESH)
    shard_copy.wait()
    shard = own_shard[...].astype(F32)
    packed[...] = jnp.concatenate([shard[:, :128], shard[:, 128:]], axis=0).astype(BF16)
    mine = parity * (cols // 2) + plane * half + lax.div(z, 2)
    obs_copy.wait()

    def widen(k, total):
        base = pl.multiple_of(k * 16, 16)
        part = obs[pl.ds(base, 16)].astype(F32)
        wide[pl.ds(pl.multiple_of(base * 8, 128), 128), :] = part.reshape(128, 128)
        return total + jnp.sum(part * part, axis=0)

    square = lax.fori_loop(0, channels // 16, widen, jnp.zeros((8, 128), F32))
    pl.semaphore_wait(barrier, len(peers))

    @pl.when(row == parity)
    def _():
        for step in range(1, depth):
            pltpu.make_async_remote_copy(
                src_ref=packed,
                dst_ref=shards.at[mine],
                send_sem=gather_sem.at[0],
                recv_sem=gather_sem.at[1],
                device_id=z_peer(step),
                device_id_type=MESH,
            ).start()
        shards[mine] = packed[...]

    def turn_rows(i, carry):
        source = jnp.where(flip, 7 - i, i)
        part = wide[pl.ds(source, channels, stride=8), :]
        turned_obs[pl.ds(pl.multiple_of(i * 128, 128), 128), :] = part.T.astype(BF16)
        return carry

    lax.fori_loop(0, 4, turn_rows, 0)

    @pl.when(row == parity)
    def _():
        if half > 1:
            got = shards.at[pl.ds(0, half - 1)]
            pltpu.make_async_copy(got, got, gather_sem.at[1]).wait()

    @pl.when(row != parity)
    def _():
        got = shards.at[pl.ds(0, half)]
        pltpu.make_async_copy(got, got, gather_sem.at[1]).wait()

    def block_of(dy, dx):
        other = lax.rem(y + ys - dy, ys) * xs + lax.rem(x + xs - dx, xs)
        return shards.at[pl.ds(row * (cols // 2) + other * half, half)]

    def pass_over(block):
        pltpu.make_async_remote_copy(
            src_ref=block,
            dst_ref=block,
            send_sem=gather_sem.at[3],
            recv_sem=gather_sem.at[4],
            device_id=core_peer,
            device_id_type=MESH,
        ).start()

    block = block_of(0, 0)
    for step in range(1, planes):
        pltpu.make_async_remote_copy(
            src_ref=block,
            dst_ref=block,
            send_sem=gather_sem.at[2],
            recv_sem=plane_sem.at[step],
            device_id=plane_peer(step),
            device_id_type=MESH,
        ).start()
    pass_over(block)
    lax.fori_loop(4, 8, turn_rows, 0)
    nearest = sorted(range(1, planes), key=lambda n: min(n // xs, ys - n // xs) + min(n % xs, xs - n % xs))
    for step in nearest:
        got = block_of(step // xs, step % xs)
        pltpu.make_async_copy(got, got, plane_sem.at[step]).wait()
        pass_over(got)
    other_half = shards.at[pl.ds((1 - row) * (cols // 2), cols // 2)]
    pltpu.make_async_copy(other_half, other_half, gather_sem.at[4]).wait()

    @pl.when(row == parity)
    def _():
        sent = shards.at[pl.ds(0, depth - 1)]
        pltpu.make_async_copy(sent, sent, gather_sem.at[0]).wait()

    sent = shards.at[pl.ds(0, half * (planes - 1))]
    pltpu.make_async_copy(sent, sent, gather_sem.at[2]).wait()
    pltpu.make_async_copy(other_half, other_half, gather_sem.at[3]).wait()

    for two in range(cols // 2):
        one = shards[slot_of(2 * two, depth, cols)].astype(F32)
        other = shards[slot_of(2 * two + 1, depth, cols)].astype(F32)
        lib[16 * two : 16 * two + 16, 0:128] = jnp.concatenate([one[0:8], other[0:8]], axis=0).astype(BF16)
        lib[16 * two : 16 * two + 16, 128:256] = jnp.concatenate([one[8:16], other[8:16]], axis=0).astype(BF16)

    def rows_of(x):
        return pl.ds(pl.multiple_of(x * 128, 128), 128)

    def send_halo(turn, slot, field):
        copy = pltpu.make_async_remote_copy(
            src_ref=field.at[rows_of(7)],
            dst_ref=halo.at[turn, slot],
            send_sem=halo_sem.at[0, turn, slot],
            recv_sem=halo_sem.at[1, turn, slot],
            device_id=core_peer,
            device_id_type=MESH,
        )
        copy.start()
        return copy

    def send_rims(turn):
        used = 8 if turn == 0 else 16
        to_left = pltpu.make_async_remote_copy(
            src_ref=rim_send.at[turn, 0, pl.ds(0, used)],
            dst_ref=rim_right.at[turn, pl.ds(0, used)],
            send_sem=rim_sem.at[0, turn, 0],
            recv_sem=rim_sem.at[1, turn, 0],
            device_id=left,
            device_id_type=MESH,
        )
        to_right = pltpu.make_async_remote_copy(
            src_ref=rim_send.at[turn, 1, pl.ds(0, used)],
            dst_ref=rim_left.at[turn, pl.ds(0, used)],
            send_sem=rim_sem.at[0, turn, 1],
            recv_sem=rim_sem.at[1, turn, 1],
            device_id=right,
            device_id_type=MESH,
        )
        to_left.start()
        to_right.start()
        return [to_left, to_right]

    library = lib[...]
    gram = lax.dot_general(library, library, (((0,), (0,)), ((), ())), preferred_element_type=F32)
    high, low = split2(gram)
    gram2[0:256, :] = high
    gram2[256:512, :] = low
    same = lax.broadcasted_iota(jnp.int32, (256, 256), 0) == lax.broadcasted_iota(jnp.int32, (256, 256), 1)
    system = gram + jnp.where(same, 1.0 + PROX, 0.0)
    for i in range(8):
        value = jnp.dot(turned_obs[128 * i : 128 * i + 128, :], lib[...], preferred_element_type=F32)
        proj[128 * i : 128 * i + 128, :] = value
        rim_send[0, 0, i : i + 1, :] = value[0:1, :]
        rim_send[0, 1, i : i + 1, :] = value[127:128, :]

    first_inverse = eliminate(system[:128, :128], work_rows)
    rim_copies = send_rims(0)
    halo_copies = [send_halo(0, 0, proj)]
    lead = exact_dot(first_inverse, system[:128, 128:], ((1,), (0,)))
    last_inverse = eliminate(
        system[128:, 128:] - exact_dot(system[128:, :128], lead, ((1,), (0,))), work_rows
    )
    corner = -exact_dot(lead, last_inverse, ((1,), (0,)))
    inverse[0:128, 0:128] = first_inverse - exact_dot(corner, lead, ((1,), (1,)))
    inverse[0:128, 128:256] = corner
    inverse[128:256, 0:128] = -exact_dot(last_inverse, lead, ((1,), (1,)))
    inverse[128:256, 128:256] = last_inverse
    high, low = split2(inverse[...])
    inv3[0:256, :] = high
    inv3[256:512, :] = low
    inv3[512:768, :] = high

    def stacked(x):
        one, two = split2(x)
        return jnp.concatenate([one, one, two], axis=1)

    def solve(x):
        return jnp.dot(stacked(x), inv3[...], preferred_element_type=F32)

    def solve_turned(x):
        one, two = split2(x)
        dims = (((1,), (1,)), ((), ()))
        total = lax.dot_general(inv3[0:256, :], one, dims, preferred_element_type=F32)
        total = total + lax.dot_general(inv3[256:512, :], one, dims, preferred_element_type=F32)
        return total + lax.dot_general(inv3[0:256, :], two, dims, preferred_element_type=F32)

    def put_rims(turn, i, slot, value):
        rim_send[turn, 0, pl.ds(8 * slot + i, 1), :] = value[0:1, :]
        rim_send[turn, 1, pl.ds(8 * slot + i, 1), :] = value[127:128, :]

    for i in range(8):
        value = solve(proj[128 * i : 128 * i + 128, :])
        part_a[128 * i : 128 * i + 128, :] = value
        own_rims[0, i : i + 1, :] = value[0:1, :]
        own_rims[1, i : i + 1, :] = value[127:128, :]

    def send_pair(turn):
        pltpu.make_async_remote_copy(
            src_ref=sums.at[turn, 0],
            dst_ref=pair.at[turn],
            send_sem=sum_sem.at[0, turn, 0],
            recv_sem=sum_sem.at[1, turn, 0],
            device_id=core_peer,
            device_id_type=MESH,
        ).start()

    def send_sums(turn, dz, alone):
        for dy in range(ys):
            for dx in range(xs):
                copy = pltpu.make_async_remote_copy(
                    src_ref=sums.at[turn, 1],
                    dst_ref=far.at[turn, pl.ds(col, 1)],
                    send_sem=sum_sem.at[0, turn, 1],
                    recv_sem=sum_sem.at[1, turn, 1],
                    device_id=peer_at(dy, dx, dz),
                    device_id_type=MESH,
                )
                if dy or dx:
                    copy.start()
                else:
                    pl.when(jnp.logical_not(alone))(copy.start)

    def wait_pair(turn, which):
        pltpu.make_async_copy(pair.at[turn], pair.at[turn], sum_sem.at[which, turn, 0]).wait()

    def wait_far(turn, which):
        got = far.at[turn, pl.ds(0, cols - 1)]
        pltpu.make_async_copy(got, got, sum_sem.at[which, turn, 1]).wait()

    first_col = jnp.where(col == 0, 1.0, 0.0).astype(F32)
    last_col = jnp.where(col == cols - 1, 1.0, 0.0).astype(F32)
    lanes = lax.broadcasted_iota(jnp.int32, (1, 128), 1)
    penalty, rescale, carry_c, carry_s = 1.0, 0.0, 0.0, 0.0

    def scalar(x):
        return x if isinstance(x, float) else x[0, 0]

    for turn in range(ITERS):
        start = turn == 0
        old_c, old_s = carry_c, carry_s
        pc_v = penalty * old_c
        sigma_v = 1.0 - pc_v * old_s
        share_v = 1.0 / (1.0 + penalty)
        carry_s = 1.0 + old_c * old_s
        bound, cut = scalar(WEIGHT_TV / penalty), scalar(WEIGHT_SPARSE / penalty)
        pc, sigma, scale_c = scalar(pc_v), scalar(sigma_v), scalar(old_c)
        share, ratio, scale_s = scalar(share_v), scalar(penalty * share_v), scalar(carry_s)
        factor = scalar(rescale)
        for copy in rim_copies + halo_copies:
            copy.wait()

        def combined(a, b):
            return a if start else a + factor * b

        def place(i, carry):
            value = combined(part_a[rows_of(i), :], part_b[rows_of(i), :])
            est[i, 0:128, :] = value
            return carry

        lax.fori_loop(0, 8, place, 0)
        if start:
            est[8, 0:128, :] = solve(halo[0, 0])
            rims = solve(jnp.concatenate([rim_left[0, 0:8, :], rim_right[0, 0:8, :]], axis=0))
            from_left, from_right = rims[0:8], rims[8:16]
            own_first, own_last = own_rims[0], own_rims[1]
        else:
            est[8, 0:128, :] = combined(halo[turn, 0], halo[turn, 1])
            own_first = combined(rim_send[turn, 0, 0:8, :], rim_send[turn, 0, 8:16, :])
            own_last = combined(rim_send[turn, 1, 0:8, :], rim_send[turn, 1, 8:16, :])
            from_right = combined(rim_right[turn, 0:8, :], rim_right[turn, 8:16, :])
            from_left = combined(rim_left[turn, 0:8, :], rim_left[turn, 8:16, :])
        from_right = jnp.where(last_col > 0.0, own_last, from_right)
        from_left = jnp.where(first_col > 0.0, own_first, from_left)
        for i in range(8):
            est[i, 128:129, :] = from_right[i : i + 1, :]

        g_diff = own_first - from_left
        g_sum = g_diff if start else g_diff + factor * ghost[...]
        g_dual = jnp.clip(g_sum, -bound, bound)
        g_arg = g_diff - (g_sum - g_dual)
        ghost[...] = g_dual
        for i in range(8):
            right_arg[i, 7:8, :] = g_arg[i : i + 1, :]
            right_dual[i, 7:8, :] = g_dual[i : i + 1, :]

        def update(i, off, totals):
            at = pl.ds(off, CHUNK)
            shifted = pl.ds(off + 8, CHUNK)
            flat = pl.ds(pl.multiple_of(i * 128 + off, CHUNK), CHUNK)
            primal, dual, quad, cross, along = totals
            e = est[i, at, :]
            half = e.astype(BF16)
            gh = jnp.dot(jnp.concatenate([half, half], axis=1), gram2[...], preferred_element_type=F32)
            h = half.astype(F32)
            w = proj[flat, :]
            quad = quad + fold(h * gh)
            along = along + fold(h * w)
            if start:
                gram_mix[flat, :] = gh
            else:
                gy = gram_mix[flat, :]
                cross = cross + fold(h * gy)
                gram_mix[flat, :] = gh + scale_c * gy
            t = e if start else e + factor * sparse_dual[flat, :]
            fresh = jnp.maximum(t - cut, 0.0)
            gap = e - fresh
            primal = primal + fold(gap * gap)
            move = fresh if start else fresh - sparse_var[flat, :]
            dual = dual + fold(move * move)
            sparse_var[flat, :] = fresh
            sparse_dual[flat, :] = t - fresh
            d = est[i + 1, at, :] - e
            t = d if start else d + factor * down_dual[flat, :]
            clipped = jnp.clip(t, -bound, bound)
            fresh = t - clipped
            gap = d - fresh
            move = fresh if start else fresh - down_var[flat, :]
            weight = jnp.where((i == 7) & (row == 1), 0.0, 1.0).astype(F32)
            primal = primal + weight * fold(gap * gap)
            dual = dual + weight * fold(move * move)
            down_var[flat, :] = fresh
            down_dual[flat, :] = clipped
            down_arg[flat, :] = gap
            d = est[i, pl.ds(off + 1, CHUNK), :] - e
            t = d if start else d + factor * right_dual[i, shifted, :]
            clipped = jnp.clip(t, -bound, bound)
            fresh = t - clipped
            gap = d - fresh
            primal = primal + fold(gap * gap)
            move = fresh if start else fresh - right_var[flat, :]
            dual = dual + fold(move * move)
            right_var[flat, :] = fresh
            right_dual[i, shifted, :] = clipped
            right_arg[i, shifted, :] = gap
            return primal, dual, quad, cross, along

        def update_row(i, totals):
            for off in range(0, 128, CHUNK):
                totals = update(i, off, totals)
            return totals

        zero = jnp.zeros((8, 128), F32)
        primal, dual, quad, cross, along = lax.fori_loop(0, 8, update_row, (zero,) * 5)
        data = quad - 2.0 * along + square
        if not start:
            data = (quad - (2.0 * pc) * cross + (pc * pc) * old_quad) - (2.0 * sigma) * (along - pc * old_along)
            data = data + (sigma * sigma) * square
            quad = quad + (2.0 * scale_c) * cross + (scale_c * scale_c) * old_quad
            along = along + scale_c * old_along
        data = data * (share * share)
        old_quad, old_along = quad, along
        line_p = jnp.sum(primal + data, axis=0, keepdims=True)
        line_d = jnp.sum(dual, axis=0, keepdims=True)
        line_p = line_p + pltpu.roll(line_p, 64, 1)
        line_d = line_d + pltpu.roll(line_d, 64, 1)
        line = jnp.where(lanes < 64, line_p, line_d)
        sums[turn, 0] = line
        send_pair(turn)

        final = turn == ITERS - 1

        def rhs(i):
            flat = rows_of(i)
            above = rows_of(jnp.maximum(i - 1, 0))
            has_above = jnp.where(i > 0, 1.0, 0.0).astype(F32)
            w = proj[flat, :]
            we = gram_mix[flat, :] - scale_s * w
            at = pl.ds(8, 128)
            before = pl.ds(7, 128)
            adj_a = (has_above * down_arg[above, :] - down_arg[flat, :]) + (
                right_arg[i, before, :] - right_arg[i, at, :]
            )
            adj_b = (has_above * down_dual[above, :] - down_dual[flat, :]) + (
                right_dual[i, before, :] - right_dual[i, at, :]
            )
            a = w + ratio * we + sparse_var[flat, :] + PROX * est[i, 0:128, :] - adj_a
            b = -(share * we + sparse_dual[flat, :] + adj_b)
            return a, b

        def prepare(i, carry):
            a, b = rhs(i)
            a, b = solve(a), solve(b)
            part_a[rows_of(i), :] = a
            part_b[rows_of(i), :] = b
            put_rims(turn + 1, i, 0, a)
            put_rims(turn + 1, i, 1, b)
            return carry

        def prepare_final(i, carry):
            a, b = rhs(i)
            spot = jnp.where(flip, 7 - i, i)
            out_ref[pl.ds(spot, 256, stride=8), :] = solve_turned(a)
            wide[pl.ds(spot, 256, stride=8), :] = solve_turned(b)
            return carry

        work = prepare_final if final else prepare
        lax.fori_loop(0, 2, work, 0)
        wait_pair(turn, 1)
        line = line + pair[turn]
        sums[turn, 1] = line
        far[turn, pl.ds(col, 1), :] = line

        def send_all(n, carry):
            away = lax.div(n + 1, 2)
            send_sums(turn, jnp.where(lax.rem(n, 2) == 1, half - away, half + away), n == depth - 1)
            return carry

        lax.fori_loop(0, depth, send_all, 0)
        lax.fori_loop(2, 8, work, 0)
        if not final:
            rim_copies = send_rims(turn + 1)
            halo_copies = [send_halo(turn + 1, 0, part_a), send_halo(turn + 1, 1, part_b)]
        wait_far(turn, 1)
        line = jnp.sum(far[turn], axis=0, keepdims=True)
        total_p = jnp.sum(jnp.where(lanes < 64, line, 0.0), axis=1, keepdims=True)
        total_d = jnp.sum(jnp.where(lanes < 64, 0.0, line), axis=1, keepdims=True)
        root = jnp.sqrt(jnp.sqrt((total_p + 1.0) / (penalty * penalty * total_d + 1.0)))
        following = penalty * root
        rescale = penalty / following
        carry_c = rescale * share_v
        penalty = following

    factor = scalar(rescale)

    def finish(i, carry):
        at = pl.ds(pl.multiple_of(i * 256, 256), 256)
        out_ref[at, :] = out_ref[at, :] + factor * wide[at, :]
        return carry

    lax.fori_loop(0, 8, finish, 0)
    for turn in range(ITERS):
        wait_pair(turn, 0)
        wait_far(turn, 0)


def run(sizes, observed, shard):
    ys, xs, depth = sizes
    cols = ys * xs * depth
    planes = ys * xs
    channels = 8 * cols
    field = pltpu.VMEM((1024, 256), F32)
    padded = pltpu.VMEM((8, PAD, 256), F32)
    rims = pltpu.VMEM((ITERS, 16, 256), F32)
    return pl.pallas_call(
        functools.partial(kernel, sizes),
        out_shape=jax.ShapeDtypeStruct((2048, 128), F32),
        in_specs=[pl.BlockSpec(memory_space=pltpu.HBM)] * 2,
        out_specs=VMEM,
        scratch_shapes=[
            pltpu.VMEM((channels, 8, 128), BF16),
            pltpu.VMEM((8, 256), BF16),
            pltpu.VMEM((max(channels * 8, 2048), 128), F32),
            pltpu.VMEM((1024, channels), BF16),
            pltpu.VMEM((16, 128), BF16),
            pltpu.VMEM((cols, 16, 128), BF16),
            pltpu.VMEM((channels, 256), BF16),
            pltpu.VMEM((72, 128), F32),
            pltpu.VMEM((256, 256), F32),
            pltpu.VMEM((512, 256), BF16),
            pltpu.VMEM((768, 256), BF16),
            field,
            pltpu.VMEM((2, 8, 256), F32),
            pltpu.VMEM((9, PAD, 256), F32),
            field,
            field,
            pltpu.VMEM((ITERS, 2, 16, 256), F32),
            rims,
            rims,
            pltpu.VMEM((ITERS, 2, 128, 256), F32),
            pltpu.VMEM((8, 256), F32),
            field,
            field,
            field,
            field,
            field,
            field,
            padded,
            padded,
            field,
            pltpu.VMEM((ITERS, 2, 1, 128), F32),
            pltpu.VMEM((ITERS, 1, 128), F32),
            pltpu.VMEM((ITERS, cols, 128), F32),
            pltpu.SemaphoreType.DMA(()),
            pltpu.SemaphoreType.DMA(()),
            pltpu.SemaphoreType.DMA((5,)),
            pltpu.SemaphoreType.DMA((planes,)),
            pltpu.SemaphoreType.DMA((2, ITERS, 2)),
            pltpu.SemaphoreType.DMA((2, ITERS, 2)),
            pltpu.SemaphoreType.DMA((2, ITERS, 2)),
        ],
        compiler_params=pltpu.CompilerParams(
            collective_id=0, has_side_effects=True, vmem_limit_bytes=52 * 2**20
        ),
        name="unmix",
    )(observed, shard)


def on_device(sizes, observed, library):
    return run(sizes, observed, library).reshape(256, 8, 128)


def solution(mesh):
    sizes = (4, 4, 8) if mesh.shape["col"] == 128 else (2, 2, 2)
    return jax.shard_map(
        functools.partial(on_device, sizes),
        mesh=mesh,
        in_specs=(P(None, "row", "col"), P("col", None)),
        out_specs=P(None, "row", "col"),
        check_vma=False,
    )
```

```python
import functools

import jax
import jax.numpy as jnp
from jax import lax
from jax.experimental import pallas as pl
from jax.experimental.pallas import tpu as pltpu
from jax.sharding import PartitionSpec as P

ITERS = 3
PROX = 8.0
WEIGHT_SPARSE = 0.3
WEIGHT_TV = 1.0
MESH = pl.DeviceIdType.MESH
F32 = jnp.float32
BF16 = jnp.bfloat16
VMEM = pl.BlockSpec(memory_space=pltpu.VMEM)


def slot_of(col, depth, cols):
    plane, z = col // depth, col % depth
    half = depth // 2
    return (z % 2) * (cols // 2) + plane * half + z // 2


def dot_of(x, y):
    t = [a * b for a, b in zip(x, y)]
    while len(t) > 1:
        t = [t[i] + t[i + 1] if i + 1 < len(t) else t[i] for i in range(0, len(t), 2)]
    return t[0]

def symmetric_inverse(m):
    n = len(m)
    if n == 1:
        return [[1.0 / m[0][0]]]
    if n == 2:
        scale = 1.0 / (m[0][0] * m[1][1] - m[0][1] * m[0][1])
        off = -m[0][1] * scale
        return [[m[1][1] * scale, off], [off, m[0][0] * scale]]
    h = n // 2
    a = symmetric_inverse([r[:h] for r in m[:h]])
    b = [r[h:] for r in m[:h]]
    bt = [list(c) for c in zip(*b)]
    t = [[dot_of(a[i], bt[j]) for j in range(h)] for i in range(h)]
    tt = [list(c) for c in zip(*t)]
    s = [[None] * h for _ in range(h)]
    for i in range(h):
        for j in range(i, h):
            s[i][j] = s[j][i] = m[h + i][h + j] - dot_of(bt[i], tt[j])
    s = symmetric_inverse(s)
    u = [[dot_of(t[i], s[j]) for j in range(h)] for i in range(h)]
    top = [[None] * h for _ in range(h)]
    for i in range(h):
        for j in range(i, h):
            top[i][j] = top[j][i] = a[i][j] + dot_of(u[i], t[j])
    out = [[None] * n for _ in range(n)]
    for i in range(h):
        for j in range(h):
            out[i][j] = top[i][j]
            out[h + i][h + j] = s[i][j]
            out[i][h + j] = -u[i][j]
            out[h + j][i] = -u[i][j]
    return out

def eliminate(matrix, ref):
    size, step = 128, 8
    groups = [matrix[8 * g : 8 * g + 8, :] for g in range(size // 8)]
    lane = lax.broadcasted_iota(jnp.int32, (8, size), 1)
    place = lax.broadcasted_iota(jnp.int32, (8, size), 0)
    full = (8, size)
    for home, first in enumerate(range(0, size, step)):

        def cols_of(g):
            return [jnp.broadcast_to(g[:, first + a : first + a + 1], full) for a in range(step)]

        home_cols = cols_of(groups[home])
        ref[0:8, :] = groups[home]
        for b in range(step):
            ref[8 + 8 * b : 16 + 8 * b, :] = home_cols[b]
        line = [jnp.broadcast_to(ref[a : a + 1, :], full) for a in range(step)]
        pivot = [[None] * step for _ in range(step)]
        for a in range(step):
            for b in range(a, step):
                spot = 8 + 8 * b + a
                pivot[a][b] = pivot[b][a] = jnp.broadcast_to(ref[spot : spot + 1, :], full)
        turned = symmetric_inverse(pivot)
        inside = (lane >= first) & (lane < first + step)
        rows = [jnp.where(lane == first + a, 1.0, jnp.where(inside, 0.0, line[a])) for a in range(step)]
        fresh = [dot_of(turned[a], rows) for a in range(step)]
        nxt = []
        for g, group in enumerate(groups):
            if g == home:
                value = fresh[0]
                for a in range(1, step):
                    value = jnp.where(place == a, fresh[a], value)
            else:
                value = jnp.where(inside, 0.0, group) - dot_of(cols_of(group), fresh)
            nxt.append(value)
        groups = nxt
    return jnp.concatenate(groups, axis=0)


def exact_dot(a, b, dims):
    return lax.dot_general(a, b, (dims, ((), ())), precision=lax.Precision.HIGHEST, preferred_element_type=F32)


def split2(x):
    high = x.astype(BF16)
    return high, (x - high.astype(F32)).astype(BF16)


CHUNK = 32
PAD = 136


def fold(x):
    total = None
    for k in range(x.shape[0] // 8):
        for half in range(2):
            part = x[8 * k : 8 * k + 8, 128 * half : 128 * half + 128]
            total = part if total is None else total + part
    return total


def walk_of(sizes):
    ys, xs, depth = sizes
    limit = ys // 2 + xs // 2 + depth // 2 - 2

    def hops(dy, dx):
        return min(dy, ys - dy) + min(dx, xs - dx)

    plane = sorted(((dy, dx) for dy in range(ys) for dx in range(xs)), key=lambda o: -hops(*o))
    walk, extra = [], 0
    for away in range(depth // 2, -1, -1):
        signs = 1 if away in (0, depth // 2) else 2
        far = [o for o in plane if hops(*o) + away >= limit]
        near = [o for o in plane if hops(*o) + away < limit and (away or o != (0, 0))]
        walk.append((signs, away, near, far, extra))
        extra += signs * len(far)
    return walk, extra


def kernel(
    sizes,
    obs_ref,
    shard_ref,
    out_ref,
    obs,
    own_shard,
    wide,
    turned_obs,
    packed,
    shards,
    lib,
    work_rows,
    inverse,
    gram2,
    inv3,
    proj,
    own_rims,
    est,
    part_a,
    part_b,
    rim_send,
    rim_left,
    rim_right,
    halo,
    ghost,
    sparse_var,
    sparse_dual,
    down_var,
    down_dual,
    down_arg,
    right_var,
    right_dual,
    right_arg,
    gram_mix,
    sums,
    pair,
    far,
    obs_sem,
    shard_sem,
    gather_sem,
    plane_sem,
    halo_sem,
    rim_sem,
    sum_sem,
):
    ys, xs, depth = sizes
    planes, half = ys * xs, depth // 2
    cols = planes * depth
    channels = 8 * cols
    row, col = lax.axis_index("row"), lax.axis_index("col")
    plane, z = lax.div(col, depth), lax.rem(col, depth)
    y, x = lax.div(plane, xs), lax.rem(plane, xs)
    parity = lax.rem(z, 2)
    flip = row == 1
    core_peer = (1 - row, col)
    walk, extra = walk_of(sizes)
    left = (row, lax.rem(col + cols - 1, cols))
    right = (row, lax.rem(col + 1, cols))

    def peer_at(dy, dx, dz):
        return (row, (lax.rem(y + dy, ys) * xs + lax.rem(x + dx, xs)) * depth + lax.rem(z + dz, depth))

    def z_peer(step):
        return peer_at(0, 0, step)

    def plane_peer(step):
        return peer_at(step // xs, step % xs, 0)

    obs_copy = pltpu.make_async_copy(obs_ref, obs, obs_sem)
    obs_copy.start()
    shard_copy = pltpu.make_async_copy(shard_ref, own_shard, shard_sem)
    shard_copy.start()
    barrier = pltpu.get_barrier_semaphore()
    peers = [z_peer(n) for n in range(1, depth)] + [plane_peer(n) for n in range(1, planes)] + [core_peer]
    for peer in peers:
        pl.semaphore_signal(barrier, inc=1, device_id=peer, device_id_type=MESH)
    shard_copy.wait()
    shard = own_shard[...].astype(F32)
    packed[...] = jnp.concatenate([shard[:, :128], shard[:, 128:]], axis=0).astype(BF16)
    mine = parity * (cols // 2) + plane * half + lax.div(z, 2)
    pl.semaphore_wait(barrier, len(peers))

    @pl.when(row == parity)
    def _():
        for step in range(1, depth):
            pltpu.make_async_remote_copy(
                src_ref=packed,
                dst_ref=shards.at[mine],
                send_sem=gather_sem.at[0],
                recv_sem=gather_sem.at[1],
                device_id=z_peer(step),
                device_id_type=MESH,
            ).start()
        shards[mine] = packed[...]

    obs_copy.wait()

    def widen(k, total):
        base = pl.multiple_of(k * 16, 16)
        part = obs[pl.ds(base, 16)].astype(F32)
        wide[pl.ds(pl.multiple_of(base * 8, 128), 128), :] = part.reshape(128, 128)
        return total + jnp.sum(part * part, axis=0)

    square = lax.fori_loop(0, channels // 16, widen, jnp.zeros((8, 128), F32))
    def turn_rows(i, carry):
        source = jnp.where(flip, 7 - i, i)
        part = wide[pl.ds(source, channels, stride=8), :]
        turned_obs[pl.ds(pl.multiple_of(i * 128, 128), 128), :] = part.T.astype(BF16)
        return carry

    lax.fori_loop(0, 3, turn_rows, 0)

    @pl.when(row == parity)
    def _():
        if half > 1:
            got = shards.at[pl.ds(0, half - 1)]
            pltpu.make_async_copy(got, got, gather_sem.at[1]).wait()

    @pl.when(row != parity)
    def _():
        got = shards.at[pl.ds(0, half)]
        pltpu.make_async_copy(got, got, gather_sem.at[1]).wait()

    def block_of(dy, dx):
        other = lax.rem(y + ys - dy, ys) * xs + lax.rem(x + xs - dx, xs)
        return shards.at[pl.ds(row * (cols // 2) + other * half, half)]

    def pass_over(block):
        pltpu.make_async_remote_copy(
            src_ref=block,
            dst_ref=block,
            send_sem=gather_sem.at[3],
            recv_sem=gather_sem.at[4],
            device_id=core_peer,
            device_id_type=MESH,
        ).start()

    block = block_of(0, 0)
    for step in range(1, planes):
        pltpu.make_async_remote_copy(
            src_ref=block,
            dst_ref=block,
            send_sem=gather_sem.at[2],
            recv_sem=plane_sem.at[step],
            device_id=plane_peer(step),
            device_id_type=MESH,
        ).start()
    pass_over(block)
    lax.fori_loop(3, 8, turn_rows, 0)
    nearest = sorted(range(1, planes), key=lambda n: min(n // xs, ys - n // xs) + min(n % xs, xs - n % xs))
    for step in nearest:
        got = block_of(step // xs, step % xs)
        pltpu.make_async_copy(got, got, plane_sem.at[step]).wait()
        pass_over(got)
    other_half = shards.at[pl.ds((1 - row) * (cols // 2), cols // 2)]
    pltpu.make_async_copy(other_half, other_half, gather_sem.at[4]).wait()

    @pl.when(row == parity)
    def _():
        sent = shards.at[pl.ds(0, depth - 1)]
        pltpu.make_async_copy(sent, sent, gather_sem.at[0]).wait()

    sent = shards.at[pl.ds(0, half * (planes - 1))]
    pltpu.make_async_copy(sent, sent, gather_sem.at[2]).wait()
    pltpu.make_async_copy(other_half, other_half, gather_sem.at[3]).wait()

    for two in range(cols // 2):
        one = shards[slot_of(2 * two, depth, cols)].astype(F32)
        other = shards[slot_of(2 * two + 1, depth, cols)].astype(F32)
        lib[16 * two : 16 * two + 16, 0:128] = jnp.concatenate([one[0:8], other[0:8]], axis=0).astype(BF16)
        lib[16 * two : 16 * two + 16, 128:256] = jnp.concatenate([one[8:16], other[8:16]], axis=0).astype(BF16)

    def rows_of(x):
        return pl.ds(pl.multiple_of(x * 128, 128), 128)

    def send_halo(turn, slot, field):
        copy = pltpu.make_async_remote_copy(
            src_ref=field.at[rows_of(7)],
            dst_ref=halo.at[turn, slot],
            send_sem=halo_sem.at[0, turn, slot],
            recv_sem=halo_sem.at[1, turn, slot],
            device_id=core_peer,
            device_id_type=MESH,
        )
        copy.start()
        return copy

    def send_rims(turn):
        used = 8 if turn == 0 else 16
        to_left = pltpu.make_async_remote_copy(
            src_ref=rim_send.at[turn, 0, pl.ds(0, used)],
            dst_ref=rim_right.at[turn, pl.ds(0, used)],
            send_sem=rim_sem.at[0, turn, 0],
            recv_sem=rim_sem.at[1, turn, 0],
            device_id=left,
            device_id_type=MESH,
        )
        to_right = pltpu.make_async_remote_copy(
            src_ref=rim_send.at[turn, 1, pl.ds(0, used)],
            dst_ref=rim_left.at[turn, pl.ds(0, used)],
            send_sem=rim_sem.at[0, turn, 1],
            recv_sem=rim_sem.at[1, turn, 1],
            device_id=right,
            device_id_type=MESH,
        )
        to_left.start()
        to_right.start()
        return [to_left, to_right]

    library = lib[...]
    gram = lax.dot_general(library, library, (((0,), (0,)), ((), ())), preferred_element_type=F32)
    high, low = split2(gram)
    gram2[0:256, :] = high
    gram2[256:512, :] = low
    same = lax.broadcasted_iota(jnp.int32, (256, 256), 0) == lax.broadcasted_iota(jnp.int32, (256, 256), 1)
    system = gram + jnp.where(same, 1.0 + PROX, 0.0)
    for i in range(8):
        value = jnp.dot(turned_obs[128 * i : 128 * i + 128, :], lib[...], preferred_element_type=F32)
        proj[128 * i : 128 * i + 128, :] = value
        rim_send[0, 0, i : i + 1, :] = value[0:1, :]
        rim_send[0, 1, i : i + 1, :] = value[127:128, :]

    first_inverse = eliminate(system[:128, :128], work_rows)
    rim_copies = send_rims(0)
    halo_copies = [send_halo(0, 0, proj)]
    lead = exact_dot(first_inverse, system[:128, 128:], ((1,), (0,)))
    last_inverse = eliminate(
        system[128:, 128:] - exact_dot(system[128:, :128], lead, ((1,), (0,))), work_rows
    )
    corner = -exact_dot(lead, last_inverse, ((1,), (0,)))
    inverse[0:128, 0:128] = first_inverse - exact_dot(corner, lead, ((1,), (1,)))
    inverse[0:128, 128:256] = corner
    inverse[128:256, 0:128] = -exact_dot(last_inverse, lead, ((1,), (1,)))
    inverse[128:256, 128:256] = last_inverse
    high, low = split2(inverse[...])
    inv3[0:256, :] = high
    inv3[256:512, :] = low
    inv3[512:768, :] = high

    def stacked(x):
        one, two = split2(x)
        return jnp.concatenate([one, one, two], axis=1)

    def solve(x):
        return jnp.dot(stacked(x), inv3[...], preferred_element_type=F32)

    def solve_turned(x):
        one, two = split2(x)
        dims = (((1,), (1,)), ((), ()))
        total = lax.dot_general(inv3[0:256, :], one, dims, preferred_element_type=F32)
        total = total + lax.dot_general(inv3[256:512, :], one, dims, preferred_element_type=F32)
        return total + lax.dot_general(inv3[0:256, :], two, dims, preferred_element_type=F32)

    def put_rims(turn, i, slot, value):
        rim_send[turn, 0, pl.ds(8 * slot + i, 1), :] = value[0:1, :]
        rim_send[turn, 1, pl.ds(8 * slot + i, 1), :] = value[127:128, :]

    for i in range(8):
        value = solve(proj[128 * i : 128 * i + 128, :])
        part_a[128 * i : 128 * i + 128, :] = value
        own_rims[0, i : i + 1, :] = value[0:1, :]
        own_rims[1, i : i + 1, :] = value[127:128, :]

    def send_pair(turn):
        pltpu.make_async_remote_copy(
            src_ref=sums.at[turn, 0],
            dst_ref=pair.at[turn],
            send_sem=sum_sem.at[0, turn, 0],
            recv_sem=sum_sem.at[1, turn, 0],
            device_id=core_peer,
            device_id_type=MESH,
        ).start()

    def send_line(turn, stage, slot, device):
        pltpu.make_async_remote_copy(
            src_ref=sums.at[turn, stage],
            dst_ref=far.at[turn, pl.ds(slot, 1)],
            send_sem=sum_sem.at[0, turn, 1],
            recv_sem=sum_sem.at[1, turn, 1],
            device_id=device,
            device_id_type=MESH,
        ).start()

    def send_far(turn):
        for signs, away, _, flat, base in walk:
            def one_sign(sign, carry):
                dz = sign * (depth - 2 * away) + away
                for n, (dy, dx) in enumerate(flat):
                    other, there = peer_at(dy, dx, dz)
                    send_line(turn, 0, col, (other, there))
                    send_line(turn, 0, cols + base + sign * len(flat) + n, (1 - other, there))
                return carry

            if flat:
                lax.fori_loop(0, signs, one_sign, 0)

    def send_near(turn):
        for signs, away, flat, _, _ in walk:
            def one_sign(sign, carry):
                dz = sign * (depth - 2 * away) + away
                for dy, dx in flat:
                    send_line(turn, 1, col, peer_at(dy, dx, dz))
                return carry

            if flat:
                lax.fori_loop(0, signs, one_sign, 0)

    def wait_pair(turn, which):
        pltpu.make_async_copy(pair.at[turn], pair.at[turn], sum_sem.at[which, turn, 0]).wait()

    def wait_far(turn, which):
        got = far.at[turn, pl.ds(0, cols - 1 + extra)]
        pltpu.make_async_copy(got, got, sum_sem.at[which, turn, 1]).wait()

    first_col = jnp.where(col == 0, 1.0, 0.0).astype(F32)
    last_col = jnp.where(col == cols - 1, 1.0, 0.0).astype(F32)
    lanes = lax.broadcasted_iota(jnp.int32, (1, 128), 1)
    penalty, rescale, carry_c, carry_s = 1.0, 0.0, 0.0, 0.0

    def scalar(x):
        return x if isinstance(x, float) else x[0, 0]

    for turn in range(ITERS):
        start = turn == 0
        old_c, old_s = carry_c, carry_s
        pc_v = penalty * old_c
        sigma_v = 1.0 - pc_v * old_s
        share_v = 1.0 / (1.0 + penalty)
        carry_s = 1.0 + old_c * old_s
        bound, cut = scalar(WEIGHT_TV / penalty), scalar(WEIGHT_SPARSE / penalty)
        pc, sigma, scale_c = scalar(pc_v), scalar(sigma_v), scalar(old_c)
        share, ratio, scale_s = scalar(share_v), scalar(penalty * share_v), scalar(carry_s)
        factor = scalar(rescale)
        for copy in rim_copies + halo_copies:
            copy.wait()

        def combined(a, b):
            return a if start else a + factor * b

        def place(i, carry):
            value = combined(part_a[rows_of(i), :], part_b[rows_of(i), :])
            est[i, 0:128, :] = value
            return carry

        lax.fori_loop(0, 8, place, 0)
        if start:
            est[8, 0:128, :] = solve(halo[0, 0])
            rims = solve(jnp.concatenate([rim_left[0, 0:8, :], rim_right[0, 0:8, :]], axis=0))
            from_left, from_right = rims[0:8], rims[8:16]
            own_first, own_last = own_rims[0], own_rims[1]
        else:
            est[8, 0:128, :] = combined(halo[turn, 0], halo[turn, 1])
            own_first = combined(rim_send[turn, 0, 0:8, :], rim_send[turn, 0, 8:16, :])
            own_last = combined(rim_send[turn, 1, 0:8, :], rim_send[turn, 1, 8:16, :])
            from_right = combined(rim_right[turn, 0:8, :], rim_right[turn, 8:16, :])
            from_left = combined(rim_left[turn, 0:8, :], rim_left[turn, 8:16, :])
        from_right = jnp.where(last_col > 0.0, own_last, from_right)
        from_left = jnp.where(first_col > 0.0, own_first, from_left)
        for i in range(8):
            est[i, 128:129, :] = from_right[i : i + 1, :]

        g_diff = own_first - from_left
        g_sum = g_diff if start else g_diff + factor * ghost[...]
        g_dual = jnp.clip(g_sum, -bound, bound)
        g_arg = g_diff - (g_sum - g_dual)
        ghost[...] = g_dual
        for i in range(8):
            right_arg[i, 7:8, :] = g_arg[i : i + 1, :]
            right_dual[i, 7:8, :] = g_dual[i : i + 1, :]

        def update(i, off, totals):
            at = pl.ds(off, CHUNK)
            shifted = pl.ds(off + 8, CHUNK)
            flat = pl.ds(pl.multiple_of(i * 128 + off, CHUNK), CHUNK)
            primal, dual, quad, cross, along = totals
            e = est[i, at, :]
            half = e.astype(BF16)
            gh = jnp.dot(jnp.concatenate([half, half], axis=1), gram2[...], preferred_element_type=F32)
            h = half.astype(F32)
            w = proj[flat, :]
            quad = quad + fold(h * gh)
            along = along + fold(h * w)
            if start:
                gram_mix[flat, :] = gh
            else:
                gy = gram_mix[flat, :]
                cross = cross + fold(h * gy)
                gram_mix[flat, :] = gh + scale_c * gy
            t = e if start else e + factor * sparse_dual[flat, :]
            fresh = jnp.maximum(t - cut, 0.0)
            gap = e - fresh
            primal = primal + fold(gap * gap)
            move = fresh if start else fresh - sparse_var[flat, :]
            dual = dual + fold(move * move)
            sparse_var[flat, :] = fresh
            sparse_dual[flat, :] = t - fresh
            d = est[i + 1, at, :] - e
            t = d if start else d + factor * down_dual[flat, :]
            clipped = jnp.clip(t, -bound, bound)
            fresh = t - clipped
            gap = d - fresh
            move = fresh if start else fresh - down_var[flat, :]
            weight = jnp.where((i == 7) & (row == 1), 0.0, 1.0).astype(F32)
            primal = primal + weight * fold(gap * gap)
            dual = dual + weight * fold(move * move)
            down_var[flat, :] = fresh
            down_dual[flat, :] = clipped
            down_arg[flat, :] = gap
            d = est[i, pl.ds(off + 1, CHUNK), :] - e
            t = d if start else d + factor * right_dual[i, shifted, :]
            clipped = jnp.clip(t, -bound, bound)
            fresh = t - clipped
            gap = d - fresh
            primal = primal + fold(gap * gap)
            move = fresh if start else fresh - right_var[flat, :]
            dual = dual + fold(move * move)
            right_var[flat, :] = fresh
            right_dual[i, shifted, :] = clipped
            right_arg[i, shifted, :] = gap
            return primal, dual, quad, cross, along

        def update_row(i, totals):
            for off in range(0, 128, CHUNK):
                totals = update(i, off, totals)
            return totals

        zero = jnp.zeros((8, 128), F32)
        primal, dual, quad, cross, along = lax.fori_loop(0, 8, update_row, (zero,) * 5)
        data = quad - 2.0 * along + square
        if not start:
            data = (quad - (2.0 * pc) * cross + (pc * pc) * old_quad) - (2.0 * sigma) * (along - pc * old_along)
            data = data + (sigma * sigma) * square
            quad = quad + (2.0 * scale_c) * cross + (scale_c * scale_c) * old_quad
            along = along + scale_c * old_along
        data = data * (share * share)
        old_quad, old_along = quad, along
        line_p = jnp.sum(primal + data, axis=0, keepdims=True)
        line_d = jnp.sum(dual, axis=0, keepdims=True)
        line_p = line_p + pltpu.roll(line_p, 64, 1)
        line_d = line_d + pltpu.roll(line_d, 64, 1)
        line = jnp.where(lanes < 64, line_p, line_d)
        sums[turn, 0] = line
        send_pair(turn)

        final = turn == ITERS - 1

        def rhs(i):
            flat = rows_of(i)
            above = rows_of(jnp.maximum(i - 1, 0))
            has_above = jnp.where(i > 0, 1.0, 0.0).astype(F32)
            w = proj[flat, :]
            we = gram_mix[flat, :] - scale_s * w
            at = pl.ds(8, 128)
            before = pl.ds(7, 128)
            adj_a = (has_above * down_arg[above, :] - down_arg[flat, :]) + (
                right_arg[i, before, :] - right_arg[i, at, :]
            )
            adj_b = (has_above * down_dual[above, :] - down_dual[flat, :]) + (
                right_dual[i, before, :] - right_dual[i, at, :]
            )
            a = w + ratio * we + sparse_var[flat, :] + PROX * est[i, 0:128, :] - adj_a
            b = -(share * we + sparse_dual[flat, :] + adj_b)
            return a, b

        def prepare(i, carry):
            a, b = rhs(i)
            a, b = solve(a), solve(b)
            part_a[rows_of(i), :] = a
            part_b[rows_of(i), :] = b
            put_rims(turn + 1, i, 0, a)
            put_rims(turn + 1, i, 1, b)
            return carry

        def prepare_final(i, carry):
            a, b = rhs(i)
            spot = jnp.where(flip, 7 - i, i)
            out_ref[pl.ds(spot, 256, stride=8), :] = solve_turned(a)
            wide[pl.ds(spot, 256, stride=8), :] = solve_turned(b)
            return carry

        work = prepare_final if final else prepare
        send_far(turn)
        wait_pair(turn, 1)
        line = line + pair[turn]
        sums[turn, 1] = line
        far[turn, pl.ds(col, 1), :] = line
        send_near(turn)
        lax.fori_loop(0, 8, work, 0)
        if not final:
            rim_copies = send_rims(turn + 1)
            halo_copies = [send_halo(turn + 1, 0, part_a), send_halo(turn + 1, 1, part_b)]
        wait_far(turn, 1)
        line = jnp.sum(far[turn, 0:cols, :], axis=0, keepdims=True)
        line = line + jnp.sum(far[turn, cols : cols + extra, :], axis=0, keepdims=True)
        total_p = jnp.sum(jnp.where(lanes < 64, line, 0.0), axis=1, keepdims=True)
        total_d = jnp.sum(jnp.where(lanes < 64, 0.0, line), axis=1, keepdims=True)
        root = jnp.sqrt(jnp.sqrt((total_p + 1.0) / (penalty * penalty * total_d + 1.0)))
        following = penalty * root
        rescale = penalty / following
        carry_c = rescale * share_v
        penalty = following

    factor = scalar(rescale)

    def finish(i, carry):
        at = pl.ds(pl.multiple_of(i * 256, 256), 256)
        out_ref[at, :] = out_ref[at, :] + factor * wide[at, :]
        return carry

    lax.fori_loop(0, 8, finish, 0)
    for turn in range(ITERS):
        wait_pair(turn, 0)
        wait_far(turn, 0)


def run(sizes, observed, shard):
    ys, xs, depth = sizes
    cols = ys * xs * depth
    planes = ys * xs
    extra = walk_of(sizes)[1]
    channels = 8 * cols
    field = pltpu.VMEM((1024, 256), F32)
    padded = pltpu.VMEM((8, PAD, 256), F32)
    rims = pltpu.VMEM((ITERS, 16, 256), F32)
    return pl.pallas_call(
        functools.partial(kernel, sizes),
        out_shape=jax.ShapeDtypeStruct((2048, 128), F32),
        in_specs=[pl.BlockSpec(memory_space=pltpu.HBM)] * 2,
        out_specs=VMEM,
        scratch_shapes=[
            pltpu.VMEM((channels, 8, 128), BF16),
            pltpu.VMEM((8, 256), BF16),
            pltpu.VMEM((max(channels * 8, 2048), 128), F32),
            pltpu.VMEM((1024, channels), BF16),
            pltpu.VMEM((16, 128), BF16),
            pltpu.VMEM((cols, 16, 128), BF16),
            pltpu.VMEM((channels, 256), BF16),
            pltpu.VMEM((72, 128), F32),
            pltpu.VMEM((256, 256), F32),
            pltpu.VMEM((512, 256), BF16),
            pltpu.VMEM((768, 256), BF16),
            field,
            pltpu.VMEM((2, 8, 256), F32),
            pltpu.VMEM((9, PAD, 256), F32),
            field,
            field,
            pltpu.VMEM((ITERS, 2, 16, 256), F32),
            rims,
            rims,
            pltpu.VMEM((ITERS, 2, 128, 256), F32),
            pltpu.VMEM((8, 256), F32),
            field,
            field,
            field,
            field,
            field,
            field,
            padded,
            padded,
            field,
            pltpu.VMEM((ITERS, 2, 1, 128), F32),
            pltpu.VMEM((ITERS, 1, 128), F32),
            pltpu.VMEM((ITERS, cols + 8 * pl.cdiv(extra, 8), 128), F32),
            pltpu.SemaphoreType.DMA(()),
            pltpu.SemaphoreType.DMA(()),
            pltpu.SemaphoreType.DMA((5,)),
            pltpu.SemaphoreType.DMA((planes,)),
            pltpu.SemaphoreType.DMA((2, ITERS, 2)),
            pltpu.SemaphoreType.DMA((2, ITERS, 2)),
            pltpu.SemaphoreType.DMA((2, ITERS, 2)),
        ],
        compiler_params=pltpu.CompilerParams(
            collective_id=0, has_side_effects=True, vmem_limit_bytes=52 * 2**20
        ),
        name="unmix",
    )(observed, shard)


def on_device(sizes, observed, library):
    return run(sizes, observed, library).reshape(256, 8, 128)


def solution(mesh):
    sizes = (4, 4, 8) if mesh.shape["col"] == 128 else (2, 2, 2)
    return jax.shard_map(
        functools.partial(on_device, sizes),
        mesh=mesh,
        in_specs=(P(None, "row", "col"), P("col", None)),
        out_specs=P(None, "row", "col"),
        check_vma=False,
    )
```

```python
import functools

import jax
import jax.numpy as jnp
from jax import lax
from jax.experimental import pallas as pl
from jax.experimental.pallas import tpu as pltpu
from jax.sharding import PartitionSpec as P

ITERS = 3
PROX = 8.0
WEIGHT_SPARSE = 0.3
WEIGHT_TV = 1.0
MESH = pl.DeviceIdType.MESH
F32 = jnp.float32
BF16 = jnp.bfloat16
VMEM = pl.BlockSpec(memory_space=pltpu.VMEM)


def slot_of(col, depth, cols):
    plane, z = col // depth, col % depth
    half = depth // 2
    return (z % 2) * (cols // 2) + plane * half + z // 2


def dot_of(x, y):
    t = [a * b for a, b in zip(x, y)]
    while len(t) > 1:
        t = [t[i] + t[i + 1] if i + 1 < len(t) else t[i] for i in range(0, len(t), 2)]
    return t[0]

def symmetric_inverse(m):
    n = len(m)
    if n == 1:
        return [[1.0 / m[0][0]]]
    if n == 2:
        scale = 1.0 / (m[0][0] * m[1][1] - m[0][1] * m[0][1])
        off = -m[0][1] * scale
        return [[m[1][1] * scale, off], [off, m[0][0] * scale]]
    h = n // 2
    a = symmetric_inverse([r[:h] for r in m[:h]])
    b = [r[h:] for r in m[:h]]
    bt = [list(c) for c in zip(*b)]
    t = [[dot_of(a[i], bt[j]) for j in range(h)] for i in range(h)]
    tt = [list(c) for c in zip(*t)]
    s = [[None] * h for _ in range(h)]
    for i in range(h):
        for j in range(i, h):
            s[i][j] = s[j][i] = m[h + i][h + j] - dot_of(bt[i], tt[j])
    s = symmetric_inverse(s)
    u = [[dot_of(t[i], s[j]) for j in range(h)] for i in range(h)]
    top = [[None] * h for _ in range(h)]
    for i in range(h):
        for j in range(i, h):
            top[i][j] = top[j][i] = a[i][j] + dot_of(u[i], t[j])
    out = [[None] * n for _ in range(n)]
    for i in range(h):
        for j in range(h):
            out[i][j] = top[i][j]
            out[h + i][h + j] = s[i][j]
            out[i][h + j] = -u[i][j]
            out[h + j][i] = -u[i][j]
    return out

def eliminate(matrix, ref):
    size, step = 128, 8
    groups = [matrix[8 * g : 8 * g + 8, :] for g in range(size // 8)]
    lane = lax.broadcasted_iota(jnp.int32, (8, size), 1)
    place = lax.broadcasted_iota(jnp.int32, (8, size), 0)
    full = (8, size)
    for home, first in enumerate(range(0, size, step)):

        def cols_of(g):
            return [jnp.broadcast_to(g[:, first + a : first + a + 1], full) for a in range(step)]

        home_cols = cols_of(groups[home])
        ref[0:8, :] = groups[home]
        for b in range(step):
            ref[8 + 8 * b : 16 + 8 * b, :] = home_cols[b]
        line = [jnp.broadcast_to(ref[a : a + 1, :], full) for a in range(step)]
        pivot = [[None] * step for _ in range(step)]
        for a in range(step):
            for b in range(a, step):
                spot = 8 + 8 * b + a
                pivot[a][b] = pivot[b][a] = jnp.broadcast_to(ref[spot : spot + 1, :], full)
        turned = symmetric_inverse(pivot)
        inside = (lane >= first) & (lane < first + step)
        rows = [jnp.where(lane == first + a, 1.0, jnp.where(inside, 0.0, line[a])) for a in range(step)]
        fresh = [dot_of(turned[a], rows) for a in range(step)]
        nxt = []
        for g, group in enumerate(groups):
            if g == home:
                value = fresh[0]
                for a in range(1, step):
                    value = jnp.where(place == a, fresh[a], value)
            else:
                value = jnp.where(inside, 0.0, group) - dot_of(cols_of(group), fresh)
            nxt.append(value)
        groups = nxt
    return jnp.concatenate(groups, axis=0)


def exact_dot(a, b, dims):
    return lax.dot_general(a, b, (dims, ((), ())), precision=lax.Precision.HIGHEST, preferred_element_type=F32)


def split2(x):
    high = x.astype(BF16)
    return high, (x - high.astype(F32)).astype(BF16)


CHUNK = 32
PAD = 136


def fold(x):
    total = None
    for k in range(x.shape[0] // 8):
        for half in range(2):
            part = x[8 * k : 8 * k + 8, 128 * half : 128 * half + 128]
            total = part if total is None else total + part
    return total


def walk_of(sizes):
    ys, xs, depth = sizes
    limit = ys // 2 + xs // 2 + depth // 2 - 2

    def hops(dy, dx):
        return min(dy, ys - dy) + min(dx, xs - dx)

    plane = sorted(((dy, dx) for dy in range(ys) for dx in range(xs)), key=lambda o: -hops(*o))
    walk, extra = [], 0
    for away in range(depth // 2, -1, -1):
        signs = 1 if away in (0, depth // 2) else 2
        far = [o for o in plane if hops(*o) + away >= limit]
        near = [o for o in plane if hops(*o) + away < limit and (away or o != (0, 0))]
        walk.append((signs, away, near, far, extra))
        extra += signs * len(far)
    return walk, extra


def kernel(
    sizes,
    obs_ref,
    shard_ref,
    out_ref,
    obs,
    own_shard,
    wide,
    turned_obs,
    packed,
    shards,
    lib,
    work_rows,
    inverse,
    gram2,
    inv3,
    proj,
    own_rims,
    est,
    part_a,
    part_b,
    rim_send,
    rim_left,
    rim_right,
    halo,
    ghost,
    sparse_var,
    sparse_dual,
    down_var,
    down_dual,
    down_arg,
    right_var,
    right_dual,
    right_arg,
    gram_mix,
    sums,
    pair,
    far,
    obs_sem,
    shard_sem,
    gather_sem,
    plane_sem,
    halo_sem,
    rim_sem,
    sum_sem,
):
    ys, xs, depth = sizes
    planes, half = ys * xs, depth // 2
    cols = planes * depth
    channels = 8 * cols
    row, col = lax.axis_index("row"), lax.axis_index("col")
    plane, z = lax.div(col, depth), lax.rem(col, depth)
    y, x = lax.div(plane, xs), lax.rem(plane, xs)
    parity = lax.rem(z, 2)
    flip = row == 1
    core_peer = (1 - row, col)
    walk, extra = walk_of(sizes)
    left = (row, lax.rem(col + cols - 1, cols))
    right = (row, lax.rem(col + 1, cols))

    def peer_at(dy, dx, dz):
        return (row, (lax.rem(y + dy, ys) * xs + lax.rem(x + dx, xs)) * depth + lax.rem(z + dz, depth))

    def z_peer(step):
        return peer_at(0, 0, step)

    def plane_peer(step):
        return peer_at(step // xs, step % xs, 0)

    obs_copy = pltpu.make_async_copy(obs_ref, obs, obs_sem)
    obs_copy.start()
    shard_copy = pltpu.make_async_copy(shard_ref, own_shard, shard_sem)
    shard_copy.start()
    barrier = pltpu.get_barrier_semaphore()
    peers = [z_peer(n) for n in range(1, depth)] + [plane_peer(n) for n in range(1, planes)] + [core_peer]
    for peer in peers:
        pl.semaphore_signal(barrier, inc=1, device_id=peer, device_id_type=MESH)
    shard_copy.wait()
    shard = own_shard[...].astype(F32)
    packed[...] = jnp.concatenate([shard[:, :128], shard[:, 128:]], axis=0).astype(BF16)
    mine = parity * (cols // 2) + plane * half + lax.div(z, 2)
    pl.semaphore_wait(barrier, len(peers))

    @pl.when(row == parity)
    def _():
        for step in range(1, depth):
            pltpu.make_async_remote_copy(
                src_ref=packed,
                dst_ref=shards.at[mine],
                send_sem=gather_sem.at[0],
                recv_sem=gather_sem.at[1],
                device_id=z_peer(step),
                device_id_type=MESH,
            ).start()
        shards[mine] = packed[...]

    obs_copy.wait()

    def widen(k, total):
        base = pl.multiple_of(k * 16, 16)
        part = obs[pl.ds(base, 16)].astype(F32)
        wide[pl.ds(pl.multiple_of(base * 8, 128), 128), :] = part.reshape(128, 128)
        return total + jnp.sum(part * part, axis=0)

    square = lax.fori_loop(0, channels // 16, widen, jnp.zeros((8, 128), F32))
    def turn_rows(i, carry):
        source = jnp.where(flip, 7 - i, i)
        part = wide[pl.ds(source, channels, stride=8), :]
        turned_obs[pl.ds(pl.multiple_of(i * 128, 128), 128), :] = part.T.astype(BF16)
        return carry

    lax.fori_loop(0, 3, turn_rows, 0)

    @pl.when(row == parity)
    def _():
        if half > 1:
            got = shards.at[pl.ds(0, half - 1)]
            pltpu.make_async_copy(got, got, gather_sem.at[1]).wait()

    @pl.when(row != parity)
    def _():
        got = shards.at[pl.ds(0, half)]
        pltpu.make_async_copy(got, got, gather_sem.at[1]).wait()

    def block_of(dy, dx):
        other = lax.rem(y + ys - dy, ys) * xs + lax.rem(x + xs - dx, xs)
        return shards.at[pl.ds(row * (cols // 2) + other * half, half)]

    def pass_over(block):
        pltpu.make_async_remote_copy(
            src_ref=block,
            dst_ref=block,
            send_sem=gather_sem.at[3],
            recv_sem=gather_sem.at[4],
            device_id=core_peer,
            device_id_type=MESH,
        ).start()

    block = block_of(0, 0)
    for step in range(1, planes):
        pltpu.make_async_remote_copy(
            src_ref=block,
            dst_ref=block,
            send_sem=gather_sem.at[2],
            recv_sem=plane_sem.at[step],
            device_id=plane_peer(step),
            device_id_type=MESH,
        ).start()
    pass_over(block)
    lax.fori_loop(3, 8, turn_rows, 0)
    nearest = sorted(range(1, planes), key=lambda n: min(n // xs, ys - n // xs) + min(n % xs, xs - n % xs))
    for step in nearest:
        got = block_of(step // xs, step % xs)
        pltpu.make_async_copy(got, got, plane_sem.at[step]).wait()
        pass_over(got)
    other_half = shards.at[pl.ds((1 - row) * (cols // 2), cols // 2)]
    pltpu.make_async_copy(other_half, other_half, gather_sem.at[4]).wait()

    @pl.when(row == parity)
    def _():
        sent = shards.at[pl.ds(0, depth - 1)]
        pltpu.make_async_copy(sent, sent, gather_sem.at[0]).wait()

    sent = shards.at[pl.ds(0, half * (planes - 1))]
    pltpu.make_async_copy(sent, sent, gather_sem.at[2]).wait()
    pltpu.make_async_copy(other_half, other_half, gather_sem.at[3]).wait()

    for two in range(cols // 2):
        one = shards[slot_of(2 * two, depth, cols)].astype(F32)
        other = shards[slot_of(2 * two + 1, depth, cols)].astype(F32)
        lib[16 * two : 16 * two + 16, 0:128] = jnp.concatenate([one[0:8], other[0:8]], axis=0).astype(BF16)
        lib[16 * two : 16 * two + 16, 128:256] = jnp.concatenate([one[8:16], other[8:16]], axis=0).astype(BF16)

    def rows_of(x):
        return pl.ds(pl.multiple_of(x * 128, 128), 128)

    def send_halo(turn, slot, field):
        copy = pltpu.make_async_remote_copy(
            src_ref=field.at[rows_of(7)],
            dst_ref=halo.at[turn, slot],
            send_sem=halo_sem.at[0, turn, slot],
            recv_sem=halo_sem.at[1, turn, slot],
            device_id=core_peer,
            device_id_type=MESH,
        )
        copy.start()
        return copy

    def send_rims(turn):
        used = 8 if turn == 0 else 16
        to_left = pltpu.make_async_remote_copy(
            src_ref=rim_send.at[turn, 0, pl.ds(0, used)],
            dst_ref=rim_right.at[turn, pl.ds(0, used)],
            send_sem=rim_sem.at[0, turn, 0],
            recv_sem=rim_sem.at[1, turn, 0],
            device_id=left,
            device_id_type=MESH,
        )
        to_right = pltpu.make_async_remote_copy(
            src_ref=rim_send.at[turn, 1, pl.ds(0, used)],
            dst_ref=rim_left.at[turn, pl.ds(0, used)],
            send_sem=rim_sem.at[0, turn, 1],
            recv_sem=rim_sem.at[1, turn, 1],
            device_id=right,
            device_id_type=MESH,
        )
        to_left.start()
        to_right.start()
        return [to_left, to_right]

    library = lib[...]
    gram = lax.dot_general(library, library, (((0,), (0,)), ((), ())), preferred_element_type=F32)
    high, low = split2(gram)
    gram2[0:256, :] = high
    gram2[256:512, :] = low
    same = lax.broadcasted_iota(jnp.int32, (256, 256), 0) == lax.broadcasted_iota(jnp.int32, (256, 256), 1)
    system = gram + jnp.where(same, 1.0 + PROX, 0.0)
    for i in range(8):
        value = jnp.dot(turned_obs[128 * i : 128 * i + 128, :], lib[...], preferred_element_type=F32)
        proj[128 * i : 128 * i + 128, :] = value
        rim_send[0, 0, i : i + 1, :] = value[0:1, :]
        rim_send[0, 1, i : i + 1, :] = value[127:128, :]

    first_inverse = eliminate(system[:128, :128], work_rows)
    rim_copies = send_rims(0)
    halo_copies = [send_halo(0, 0, proj)]
    lead = exact_dot(first_inverse, system[:128, 128:], ((1,), (0,)))
    last_inverse = eliminate(
        system[128:, 128:] - exact_dot(system[128:, :128], lead, ((1,), (0,))), work_rows
    )
    corner = -exact_dot(lead, last_inverse, ((1,), (0,)))
    inverse[0:128, 0:128] = first_inverse - exact_dot(corner, lead, ((1,), (1,)))
    inverse[0:128, 128:256] = corner
    inverse[128:256, 0:128] = -exact_dot(last_inverse, lead, ((1,), (1,)))
    inverse[128:256, 128:256] = last_inverse
    high, low = split2(inverse[...])
    inv3[0:256, :] = high
    inv3[256:512, :] = low
    inv3[512:768, :] = high

    def stacked(x):
        one, two = split2(x)
        return jnp.concatenate([one, one, two], axis=1)

    def solve(x):
        return jnp.dot(stacked(x), inv3[...], preferred_element_type=F32)

    def solve_turned(x):
        one, two = split2(x)
        dims = (((1,), (1,)), ((), ()))
        total = lax.dot_general(inv3[0:256, :], one, dims, preferred_element_type=F32)
        total = total + lax.dot_general(inv3[256:512, :], one, dims, preferred_element_type=F32)
        return total + lax.dot_general(inv3[0:256, :], two, dims, preferred_element_type=F32)

    for i in range(8):
        value = solve(proj[128 * i : 128 * i + 128, :])
        part_a[128 * i : 128 * i + 128, :] = value
        own_rims[0, i : i + 1, :] = value[0:1, :]
        own_rims[1, i : i + 1, :] = value[127:128, :]

    def send_pair(turn):
        pltpu.make_async_remote_copy(
            src_ref=sums.at[turn, 0],
            dst_ref=pair.at[turn],
            send_sem=sum_sem.at[0, turn, 0],
            recv_sem=sum_sem.at[1, turn, 0],
            device_id=core_peer,
            device_id_type=MESH,
        ).start()

    def send_line(turn, stage, slot, device):
        pltpu.make_async_remote_copy(
            src_ref=sums.at[turn, stage],
            dst_ref=far.at[turn, pl.ds(slot, 1)],
            send_sem=sum_sem.at[0, turn, 1],
            recv_sem=sum_sem.at[1, turn, 1],
            device_id=device,
            device_id_type=MESH,
        ).start()

    def send_far(turn):
        for signs, away, _, flat, base in walk:
            def one_sign(sign, carry):
                dz = sign * (depth - 2 * away) + away
                for n, (dy, dx) in enumerate(flat):
                    other, there = peer_at(dy, dx, dz)
                    send_line(turn, 0, col, (other, there))
                    send_line(turn, 0, cols + base + sign * len(flat) + n, (1 - other, there))
                return carry

            if flat:
                lax.fori_loop(0, signs, one_sign, 0)

    def send_near(turn):
        for signs, away, flat, _, _ in walk:
            def one_sign(sign, carry):
                dz = sign * (depth - 2 * away) + away
                for dy, dx in flat:
                    send_line(turn, 1, col, peer_at(dy, dx, dz))
                return carry

            if flat:
                lax.fori_loop(0, signs, one_sign, 0)

    def wait_pair(turn, which):
        pltpu.make_async_copy(pair.at[turn], pair.at[turn], sum_sem.at[which, turn, 0]).wait()

    def wait_far(turn, which):
        got = far.at[turn, pl.ds(0, cols - 1 + extra)]
        pltpu.make_async_copy(got, got, sum_sem.at[which, turn, 1]).wait()

    first_col = jnp.where(col == 0, 1.0, 0.0).astype(F32)
    last_col = jnp.where(col == cols - 1, 1.0, 0.0).astype(F32)
    lanes = lax.broadcasted_iota(jnp.int32, (1, 128), 1)
    penalty, rescale, carry_c, carry_s = 1.0, 0.0, 0.0, 0.0

    def scalar(x):
        return x if isinstance(x, float) else x[0, 0]

    for turn in range(ITERS):
        start = turn == 0
        old_c, old_s = carry_c, carry_s
        pc_v = penalty * old_c
        sigma_v = 1.0 - pc_v * old_s
        share_v = 1.0 / (1.0 + penalty)
        carry_s = 1.0 + old_c * old_s
        bound, cut = scalar(WEIGHT_TV / penalty), scalar(WEIGHT_SPARSE / penalty)
        pc, sigma, scale_c = scalar(pc_v), scalar(sigma_v), scalar(old_c)
        share, ratio, scale_s = scalar(share_v), scalar(penalty * share_v), scalar(carry_s)
        factor = scalar(rescale)
        for copy in rim_copies + halo_copies:
            copy.wait()

        def combined(a, b):
            return a if start else a + factor * b

        def place(i, carry):
            value = combined(part_a[rows_of(i), :], part_b[rows_of(i), :])
            est[i, 0:128, :] = value
            return carry

        lax.fori_loop(0, 8, place, 0)
        if start:
            est[8, 0:128, :] = solve(halo[0, 0])
            rims = solve(jnp.concatenate([rim_left[0, 0:8, :], rim_right[0, 0:8, :]], axis=0))
            from_left, from_right = rims[0:8], rims[8:16]
            own_first, own_last = own_rims[0], own_rims[1]
        else:
            est[8, 0:128, :] = combined(halo[turn, 0], halo[turn, 1])
            own_first = combined(rim_send[turn, 0, 0:8, :], rim_send[turn, 0, 8:16, :])
            own_last = combined(rim_send[turn, 1, 0:8, :], rim_send[turn, 1, 8:16, :])
            from_right = combined(rim_right[turn, 0:8, :], rim_right[turn, 8:16, :])
            from_left = combined(rim_left[turn, 0:8, :], rim_left[turn, 8:16, :])
        from_right = jnp.where(last_col > 0.0, own_last, from_right)
        from_left = jnp.where(first_col > 0.0, own_first, from_left)
        for i in range(8):
            est[i, 128:129, :] = from_right[i : i + 1, :]

        g_diff = own_first - from_left
        g_sum = g_diff if start else g_diff + factor * ghost[...]
        g_dual = jnp.clip(g_sum, -bound, bound)
        g_arg = g_diff - (g_sum - g_dual)
        ghost[...] = g_dual
        for i in range(8):
            right_arg[i, 7:8, :] = g_arg[i : i + 1, :]
            right_dual[i, 7:8, :] = g_dual[i : i + 1, :]

        def update(i, off, totals):
            at = pl.ds(off, CHUNK)
            shifted = pl.ds(off + 8, CHUNK)
            flat = pl.ds(pl.multiple_of(i * 128 + off, CHUNK), CHUNK)
            primal, dual, quad, cross, along = totals
            e = est[i, at, :]
            half = e.astype(BF16)
            gh = jnp.dot(jnp.concatenate([half, half], axis=1), gram2[...], preferred_element_type=F32)
            h = half.astype(F32)
            w = proj[flat, :]
            quad = quad + fold(h * gh)
            along = along + fold(h * w)
            if start:
                gram_mix[flat, :] = gh
            else:
                gy = gram_mix[flat, :]
                cross = cross + fold(h * gy)
                gram_mix[flat, :] = gh + scale_c * gy
            t = e if start else e + factor * sparse_dual[flat, :]
            fresh = jnp.maximum(t - cut, 0.0)
            gap = e - fresh
            primal = primal + fold(gap * gap)
            move = fresh if start else fresh - sparse_var[flat, :]
            dual = dual + fold(move * move)
            sparse_var[flat, :] = fresh
            sparse_dual[flat, :] = t - fresh
            d = est[i + 1, at, :] - e
            t = d if start else d + factor * down_dual[flat, :]
            clipped = jnp.clip(t, -bound, bound)
            fresh = t - clipped
            gap = d - fresh
            move = fresh if start else fresh - down_var[flat, :]
            weight = jnp.where((i == 7) & (row == 1), 0.0, 1.0).astype(F32)
            primal = primal + weight * fold(gap * gap)
            dual = dual + weight * fold(move * move)
            down_var[flat, :] = fresh
            down_dual[flat, :] = clipped
            down_arg[flat, :] = gap
            d = est[i, pl.ds(off + 1, CHUNK), :] - e
            t = d if start else d + factor * right_dual[i, shifted, :]
            clipped = jnp.clip(t, -bound, bound)
            fresh = t - clipped
            gap = d - fresh
            primal = primal + fold(gap * gap)
            move = fresh if start else fresh - right_var[flat, :]
            dual = dual + fold(move * move)
            right_var[flat, :] = fresh
            right_dual[i, shifted, :] = clipped
            right_arg[i, shifted, :] = gap
            return primal, dual, quad, cross, along

        def update_row(i, totals):
            for off in range(0, 128, CHUNK):
                totals = update(i, off, totals)
            return totals

        zero = jnp.zeros((8, 128), F32)
        primal, dual, quad, cross, along = lax.fori_loop(0, 8, update_row, (zero,) * 5)
        data = quad - 2.0 * along + square
        if not start:
            data = (quad - (2.0 * pc) * cross + (pc * pc) * old_quad) - (2.0 * sigma) * (along - pc * old_along)
            data = data + (sigma * sigma) * square
            quad = quad + (2.0 * scale_c) * cross + (scale_c * scale_c) * old_quad
            along = along + scale_c * old_along
        data = data * (share * share)
        old_quad, old_along = quad, along
        line_p = jnp.sum(primal + data, axis=0, keepdims=True)
        line_d = jnp.sum(dual, axis=0, keepdims=True)
        line_p = line_p + pltpu.roll(line_p, 64, 1)
        line_d = line_d + pltpu.roll(line_d, 64, 1)
        line = jnp.where(lanes < 64, line_p, line_d)
        sums[turn, 0] = line
        send_pair(turn)

        final = turn == ITERS - 1

        def rhs(i):
            flat = rows_of(i)
            above = rows_of(jnp.maximum(i - 1, 0))
            has_above = jnp.where(i > 0, 1.0, 0.0).astype(F32)
            w = proj[flat, :]
            we = gram_mix[flat, :] - scale_s * w
            at = pl.ds(8, 128)
            before = pl.ds(7, 128)
            adj_a = (has_above * down_arg[above, :] - down_arg[flat, :]) + (
                right_arg[i, before, :] - right_arg[i, at, :]
            )
            adj_b = (has_above * down_dual[above, :] - down_dual[flat, :]) + (
                right_dual[i, before, :] - right_dual[i, at, :]
            )
            a = w + ratio * we + sparse_var[flat, :] + PROX * est[i, 0:128, :] - adj_a
            b = -(share * we + sparse_dual[flat, :] + adj_b)
            return a, b

        def rim_rhs(j):
            def flat(field):
                return jnp.concatenate([field[128 * i + j : 128 * i + j + 1, :] for i in range(8)], axis=0)

            def deep(field, k):
                return jnp.concatenate([field[i, k : k + 1, :] for i in range(8)], axis=0)

            def adjoint(down, side):
                rows = flat(down)
                above = jnp.concatenate([jnp.zeros((1, 256), F32), rows[0:7, :]], axis=0)
                return (above - rows) + (deep(side, 7 + j) - deep(side, 8 + j))

            w = flat(proj)
            we = flat(gram_mix) - scale_s * w
            a = w + ratio * we + flat(sparse_var) + PROX * deep(est, j) - adjoint(down_arg, right_arg)
            b = -(share * we + flat(sparse_dual) + adjoint(down_dual, right_dual))
            return [a, b]

        def prepare(n, carry):
            i = 7 - n
            a, b = rhs(i)
            a, b = solve(a), solve(b)
            part_a[rows_of(i), :] = a
            part_b[rows_of(i), :] = b
            return carry

        def prepare_final(i, carry):
            a, b = rhs(i)
            spot = jnp.where(flip, 7 - i, i)
            out_ref[pl.ds(spot, 256, stride=8), :] = solve_turned(a)
            wide[pl.ds(spot, 256, stride=8), :] = solve_turned(b)
            return carry

        work = prepare_final if final else prepare
        send_far(turn)
        wait_pair(turn, 1)
        line = line + pair[turn]
        sums[turn, 1] = line
        far[turn, pl.ds(col, 1), :] = line
        if not final:
            solved = solve(jnp.concatenate(rim_rhs(0) + rim_rhs(127), axis=0))
            rim_send[turn + 1, 0] = solved[0:16, :]
            rim_send[turn + 1, 1] = solved[16:32, :]
            rim_copies = send_rims(turn + 1)
        send_near(turn)
        work(0, 0)
        if not final:
            halo_copies = [send_halo(turn + 1, 0, part_a), send_halo(turn + 1, 1, part_b)]
        lax.fori_loop(1, 8, work, 0)
        wait_far(turn, 1)
        line = jnp.sum(far[turn, 0:cols, :], axis=0, keepdims=True)
        line = line + jnp.sum(far[turn, cols : cols + extra, :], axis=0, keepdims=True)
        total_p = jnp.sum(jnp.where(lanes < 64, line, 0.0), axis=1, keepdims=True)
        total_d = jnp.sum(jnp.where(lanes < 64, 0.0, line), axis=1, keepdims=True)
        root = jnp.sqrt(jnp.sqrt((total_p + 1.0) / (penalty * penalty * total_d + 1.0)))
        following = penalty * root
        rescale = penalty / following
        carry_c = rescale * share_v
        penalty = following

    factor = scalar(rescale)

    def finish(i, carry):
        at = pl.ds(pl.multiple_of(i * 256, 256), 256)
        out_ref[at, :] = out_ref[at, :] + factor * wide[at, :]
        return carry

    lax.fori_loop(0, 8, finish, 0)
    for turn in range(ITERS):
        wait_pair(turn, 0)
        wait_far(turn, 0)


def run(sizes, observed, shard):
    ys, xs, depth = sizes
    cols = ys * xs * depth
    planes = ys * xs
    extra = walk_of(sizes)[1]
    channels = 8 * cols
    field = pltpu.VMEM((1024, 256), F32)
    padded = pltpu.VMEM((8, PAD, 256), F32)
    rims = pltpu.VMEM((ITERS, 16, 256), F32)
    return pl.pallas_call(
        functools.partial(kernel, sizes),
        out_shape=jax.ShapeDtypeStruct((2048, 128), F32),
        in_specs=[pl.BlockSpec(memory_space=pltpu.HBM)] * 2,
        out_specs=VMEM,
        scratch_shapes=[
            pltpu.VMEM((channels, 8, 128), BF16),
            pltpu.VMEM((8, 256), BF16),
            pltpu.VMEM((max(channels * 8, 2048), 128), F32),
            pltpu.VMEM((1024, channels), BF16),
            pltpu.VMEM((16, 128), BF16),
            pltpu.VMEM((cols, 16, 128), BF16),
            pltpu.VMEM((channels, 256), BF16),
            pltpu.VMEM((72, 128), F32),
            pltpu.VMEM((256, 256), F32),
            pltpu.VMEM((512, 256), BF16),
            pltpu.VMEM((768, 256), BF16),
            field,
            pltpu.VMEM((2, 8, 256), F32),
            pltpu.VMEM((9, PAD, 256), F32),
            field,
            field,
            pltpu.VMEM((ITERS, 2, 16, 256), F32),
            rims,
            rims,
            pltpu.VMEM((ITERS, 2, 128, 256), F32),
            pltpu.VMEM((8, 256), F32),
            field,
            field,
            field,
            field,
            field,
            field,
            padded,
            padded,
            field,
            pltpu.VMEM((ITERS, 2, 1, 128), F32),
            pltpu.VMEM((ITERS, 1, 128), F32),
            pltpu.VMEM((ITERS, cols + 8 * pl.cdiv(extra, 8), 128), F32),
            pltpu.SemaphoreType.DMA(()),
            pltpu.SemaphoreType.DMA(()),
            pltpu.SemaphoreType.DMA((5,)),
            pltpu.SemaphoreType.DMA((planes,)),
            pltpu.SemaphoreType.DMA((2, ITERS, 2)),
            pltpu.SemaphoreType.DMA((2, ITERS, 2)),
            pltpu.SemaphoreType.DMA((2, ITERS, 2)),
        ],
        compiler_params=pltpu.CompilerParams(
            collective_id=0, has_side_effects=True, vmem_limit_bytes=52 * 2**20
        ),
        name="unmix",
    )(observed, shard)


def on_device(sizes, observed, library):
    return run(sizes, observed, library).reshape(256, 8, 128)


def solution(mesh):
    sizes = (4, 4, 8) if mesh.shape["col"] == 128 else (2, 2, 2)
    return jax.shard_map(
        functools.partial(on_device, sizes),
        mesh=mesh,
        in_specs=(P(None, "row", "col"), P("col", None)),
        out_specs=P(None, "row", "col"),
        check_vma=False,
    )
```

```python
import functools

import jax
import jax.numpy as jnp
from jax import lax
from jax.experimental import pallas as pl
from jax.experimental.pallas import tpu as pltpu
from jax.sharding import PartitionSpec as P

ITERS = 3
PROX = 8.0
WEIGHT_SPARSE = 0.3
WEIGHT_TV = 1.0
MESH = pl.DeviceIdType.MESH
F32 = jnp.float32
BF16 = jnp.bfloat16
VMEM = pl.BlockSpec(memory_space=pltpu.VMEM)


def slot_of(col, depth, cols):
    plane, z = col // depth, col % depth
    half = depth // 2
    return (z % 2) * (cols // 2) + plane * half + z // 2


def dot_of(x, y):
    t = [a * b for a, b in zip(x, y)]
    while len(t) > 1:
        t = [t[i] + t[i + 1] if i + 1 < len(t) else t[i] for i in range(0, len(t), 2)]
    return t[0]

def symmetric_inverse(m):
    n = len(m)
    if n == 1:
        return [[1.0 / m[0][0]]]
    if n == 2:
        scale = 1.0 / (m[0][0] * m[1][1] - m[0][1] * m[0][1])
        off = -m[0][1] * scale
        return [[m[1][1] * scale, off], [off, m[0][0] * scale]]
    h = n // 2
    a = symmetric_inverse([r[:h] for r in m[:h]])
    b = [r[h:] for r in m[:h]]
    bt = [list(c) for c in zip(*b)]
    t = [[dot_of(a[i], bt[j]) for j in range(h)] for i in range(h)]
    tt = [list(c) for c in zip(*t)]
    s = [[None] * h for _ in range(h)]
    for i in range(h):
        for j in range(i, h):
            s[i][j] = s[j][i] = m[h + i][h + j] - dot_of(bt[i], tt[j])
    s = symmetric_inverse(s)
    u = [[dot_of(t[i], s[j]) for j in range(h)] for i in range(h)]
    top = [[None] * h for _ in range(h)]
    for i in range(h):
        for j in range(i, h):
            top[i][j] = top[j][i] = a[i][j] + dot_of(u[i], t[j])
    out = [[None] * n for _ in range(n)]
    for i in range(h):
        for j in range(h):
            out[i][j] = top[i][j]
            out[h + i][h + j] = s[i][j]
            out[i][h + j] = -u[i][j]
            out[h + j][i] = -u[i][j]
    return out

def eliminate(matrix, ref):
    size, step = 128, 8
    groups = [matrix[8 * g : 8 * g + 8, :] for g in range(size // 8)]
    lane = lax.broadcasted_iota(jnp.int32, (8, size), 1)
    place = lax.broadcasted_iota(jnp.int32, (8, size), 0)
    full = (8, size)
    for home, first in enumerate(range(0, size, step)):

        def cols_of(g):
            return [jnp.broadcast_to(g[:, first + a : first + a + 1], full) for a in range(step)]

        home_cols = cols_of(groups[home])
        ref[0:8, :] = groups[home]
        for b in range(step):
            ref[8 + 8 * b : 16 + 8 * b, :] = home_cols[b]
        line = [jnp.broadcast_to(ref[a : a + 1, :], full) for a in range(step)]
        pivot = [[None] * step for _ in range(step)]
        for a in range(step):
            for b in range(a, step):
                spot = 8 + 8 * b + a
                pivot[a][b] = pivot[b][a] = jnp.broadcast_to(ref[spot : spot + 1, :], full)
        turned = symmetric_inverse(pivot)
        inside = (lane >= first) & (lane < first + step)
        rows = [jnp.where(lane == first + a, 1.0, jnp.where(inside, 0.0, line[a])) for a in range(step)]
        fresh = [dot_of(turned[a], rows) for a in range(step)]
        nxt = []
        for g, group in enumerate(groups):
            if g == home:
                value = fresh[0]
                for a in range(1, step):
                    value = jnp.where(place == a, fresh[a], value)
            else:
                value = jnp.where(inside, 0.0, group) - dot_of(cols_of(group), fresh)
            nxt.append(value)
        groups = nxt
    return jnp.concatenate(groups, axis=0)


def exact_dot(a, b, dims):
    return lax.dot_general(a, b, (dims, ((), ())), precision=lax.Precision.HIGHEST, preferred_element_type=F32)


def split2(x):
    high = x.astype(BF16)
    return high, (x - high.astype(F32)).astype(BF16)


CHUNK = 32
PAD = 136


def fold(x):
    total = None
    for k in range(x.shape[0] // 8):
        for half in range(2):
            part = x[8 * k : 8 * k + 8, 128 * half : 128 * half + 128]
            total = part if total is None else total + part
    return total


def walk_of(sizes):
    ys, xs, depth = sizes
    limit = ys // 2 + xs // 2 + depth // 2 - 2

    def hops(dy, dx):
        return min(dy, ys - dy) + min(dx, xs - dx)

    plane = sorted(((dy, dx) for dy in range(ys) for dx in range(xs)), key=lambda o: -hops(*o))
    walk, extra = [], 0
    for away in range(depth // 2, -1, -1):
        signs = 1 if away in (0, depth // 2) else 2
        far = [o for o in plane if hops(*o) + away >= limit]
        near = [o for o in plane if hops(*o) + away < limit and (away or o != (0, 0))]
        walk.append((signs, away, near, far, extra))
        extra += signs * len(far)
    return walk, extra


def kernel(
    sizes,
    obs_ref,
    shard_ref,
    out_ref,
    obs,
    own_shard,
    wide,
    turned_obs,
    packed,
    shards,
    lib,
    work_rows,
    inverse,
    gram2,
    inv3,
    inv_wide,
    proj,
    own_rims,
    est,
    part_a,
    part_b,
    rim_send,
    rim_left,
    rim_right,
    halo,
    ghost,
    sparse_var,
    sparse_dual,
    down_var,
    down_dual,
    down_arg,
    right_var,
    right_dual,
    right_arg,
    gram_mix,
    sums,
    pair,
    far,
    obs_sem,
    shard_sem,
    gather_sem,
    plane_sem,
    halo_sem,
    rim_sem,
    sum_sem,
):
    ys, xs, depth = sizes
    planes, half = ys * xs, depth // 2
    cols = planes * depth
    channels = 8 * cols
    row, col = lax.axis_index("row"), lax.axis_index("col")
    plane, z = lax.div(col, depth), lax.rem(col, depth)
    y, x = lax.div(plane, xs), lax.rem(plane, xs)
    parity = lax.rem(z, 2)
    flip = row == 1
    core_peer = (1 - row, col)
    walk, extra = walk_of(sizes)
    left = (row, lax.rem(col + cols - 1, cols))
    right = (row, lax.rem(col + 1, cols))

    columns = [
        [(lax.rem(y + dy, ys) * xs + lax.rem(x + dx, xs)) * depth for dx in range(xs)] for dy in range(ys)
    ]

    def peer_at(dy, dx, dz):
        return (row, columns[dy][dx] + lax.rem(z + dz, depth))

    def z_peer(step):
        return peer_at(0, 0, step)

    def plane_peer(step):
        return peer_at(step // xs, step % xs, 0)

    obs_copy = pltpu.make_async_copy(obs_ref, obs, obs_sem)
    obs_copy.start()
    shard_copy = pltpu.make_async_copy(shard_ref, own_shard, shard_sem)
    shard_copy.start()
    barrier = pltpu.get_barrier_semaphore()
    peers = [z_peer(n) for n in range(1, depth)] + [plane_peer(n) for n in range(1, planes)] + [core_peer]
    for peer in peers:
        pl.semaphore_signal(barrier, inc=1, device_id=peer, device_id_type=MESH)
    shard_copy.wait()
    shard = own_shard[...].astype(F32)
    packed[...] = jnp.concatenate([shard[:, :128], shard[:, 128:]], axis=0).astype(BF16)
    mine = parity * (cols // 2) + plane * half + lax.div(z, 2)
    pl.semaphore_wait(barrier, len(peers))

    @pl.when(row == parity)
    def _():
        for step in range(1, depth):
            pltpu.make_async_remote_copy(
                src_ref=packed,
                dst_ref=shards.at[mine],
                send_sem=gather_sem.at[0],
                recv_sem=gather_sem.at[1],
                device_id=z_peer(step),
                device_id_type=MESH,
            ).start()
        shards[mine] = packed[...]

    obs_copy.wait()

    def widen(k, total):
        base = pl.multiple_of(k * 16, 16)
        part = obs[pl.ds(base, 16)].astype(F32)
        wide[pl.ds(pl.multiple_of(base * 8, 128), 128), :] = part.reshape(128, 128)
        return total + jnp.sum(part * part, axis=0)

    square = lax.fori_loop(0, channels // 16, widen, jnp.zeros((8, 128), F32))
    def turn_rows(i, carry):
        source = jnp.where(flip, 7 - i, i)
        part = wide[pl.ds(source, channels, stride=8), :]
        turned_obs[pl.ds(pl.multiple_of(i * 128, 128), 128), :] = part.T.astype(BF16)
        return carry

    lax.fori_loop(0, 3, turn_rows, 0)

    @pl.when(row == parity)
    def _():
        if half > 1:
            got = shards.at[pl.ds(0, half - 1)]
            pltpu.make_async_copy(got, got, gather_sem.at[1]).wait()

    @pl.when(row != parity)
    def _():
        got = shards.at[pl.ds(0, half)]
        pltpu.make_async_copy(got, got, gather_sem.at[1]).wait()

    def block_of(dy, dx):
        other = lax.rem(y + ys - dy, ys) * xs + lax.rem(x + xs - dx, xs)
        return shards.at[pl.ds(row * (cols // 2) + other * half, half)]

    def pass_over(block):
        pltpu.make_async_remote_copy(
            src_ref=block,
            dst_ref=block,
            send_sem=gather_sem.at[3],
            recv_sem=gather_sem.at[4],
            device_id=core_peer,
            device_id_type=MESH,
        ).start()

    block = block_of(0, 0)
    for step in range(1, planes):
        pltpu.make_async_remote_copy(
            src_ref=block,
            dst_ref=block,
            send_sem=gather_sem.at[2],
            recv_sem=plane_sem.at[step],
            device_id=plane_peer(step),
            device_id_type=MESH,
        ).start()
    pass_over(block)
    lax.fori_loop(3, 8, turn_rows, 0)
    nearest = sorted(range(1, planes), key=lambda n: min(n // xs, ys - n // xs) + min(n % xs, xs - n % xs))
    for step in nearest:
        got = block_of(step // xs, step % xs)
        pltpu.make_async_copy(got, got, plane_sem.at[step]).wait()
        pass_over(got)
    other_half = shards.at[pl.ds((1 - row) * (cols // 2), cols // 2)]
    pltpu.make_async_copy(other_half, other_half, gather_sem.at[4]).wait()

    @pl.when(row == parity)
    def _():
        sent = shards.at[pl.ds(0, depth - 1)]
        pltpu.make_async_copy(sent, sent, gather_sem.at[0]).wait()

    sent = shards.at[pl.ds(0, half * (planes - 1))]
    pltpu.make_async_copy(sent, sent, gather_sem.at[2]).wait()
    pltpu.make_async_copy(other_half, other_half, gather_sem.at[3]).wait()

    for two in range(cols // 2):
        one = shards[slot_of(2 * two, depth, cols)].astype(F32)
        other = shards[slot_of(2 * two + 1, depth, cols)].astype(F32)
        lib[16 * two : 16 * two + 16, 0:128] = jnp.concatenate([one[0:8], other[0:8]], axis=0).astype(BF16)
        lib[16 * two : 16 * two + 16, 128:256] = jnp.concatenate([one[8:16], other[8:16]], axis=0).astype(BF16)

    def rows_of(x):
        return pl.ds(pl.multiple_of(x * 128, 128), 128)

    def send_halo(turn, slot, field):
        copy = pltpu.make_async_remote_copy(
            src_ref=field.at[rows_of(7)],
            dst_ref=halo.at[turn, slot],
            send_sem=halo_sem.at[0, turn, slot],
            recv_sem=halo_sem.at[1, turn, slot],
            device_id=core_peer,
            device_id_type=MESH,
        )
        copy.start()
        return copy

    def send_rims(turn):
        used = 8 if turn == 0 else 16
        to_left = pltpu.make_async_remote_copy(
            src_ref=rim_send.at[turn, 0, pl.ds(0, used)],
            dst_ref=rim_right.at[turn, pl.ds(0, used)],
            send_sem=rim_sem.at[0, turn, 0],
            recv_sem=rim_sem.at[1, turn, 0],
            device_id=left,
            device_id_type=MESH,
        )
        to_right = pltpu.make_async_remote_copy(
            src_ref=rim_send.at[turn, 1, pl.ds(0, used)],
            dst_ref=rim_left.at[turn, pl.ds(0, used)],
            send_sem=rim_sem.at[0, turn, 1],
            recv_sem=rim_sem.at[1, turn, 1],
            device_id=right,
            device_id_type=MESH,
        )
        to_left.start()
        to_right.start()
        return [to_left, to_right]

    library = lib[...]
    gram = lax.dot_general(library, library, (((0,), (0,)), ((), ())), preferred_element_type=F32)
    high, low = split2(gram)
    gram2[0:256, :] = high
    gram2[256:512, :] = low
    same = lax.broadcasted_iota(jnp.int32, (256, 256), 0) == lax.broadcasted_iota(jnp.int32, (256, 256), 1)
    system = gram + jnp.where(same, 1.0 + PROX, 0.0)
    for i in range(8):
        value = jnp.dot(turned_obs[128 * i : 128 * i + 128, :], lib[...], preferred_element_type=F32)
        proj[128 * i : 128 * i + 128, :] = value
        rim_send[0, 0, i : i + 1, :] = value[0:1, :]
        rim_send[0, 1, i : i + 1, :] = value[127:128, :]

    first_inverse = eliminate(system[:128, :128], work_rows)
    rim_copies = send_rims(0)
    halo_copies = [send_halo(0, 0, proj)]
    lead = exact_dot(first_inverse, system[:128, 128:], ((1,), (0,)))
    last_inverse = eliminate(
        system[128:, 128:] - exact_dot(system[128:, :128], lead, ((1,), (0,))), work_rows
    )
    corner = -exact_dot(lead, last_inverse, ((1,), (0,)))
    inverse[0:128, 0:128] = first_inverse - exact_dot(corner, lead, ((1,), (1,)))
    inverse[0:128, 128:256] = corner
    inverse[128:256, 0:128] = -exact_dot(last_inverse, lead, ((1,), (1,)))
    inverse[128:256, 128:256] = last_inverse
    high, low = split2(inverse[...])
    inv3[0:256, :] = high
    inv3[256:512, :] = low
    inv3[512:768, :] = high
    inv_wide[:, 0:256] = high
    inv_wide[:, 256:512] = low
    inv_wide[:, 512:768] = high

    def stacked(x):
        one, two = split2(x)
        return jnp.concatenate([one, one, two], axis=1)

    def solve(x):
        return jnp.dot(stacked(x), inv3[...], preferred_element_type=F32)

    def solve_turned(x):
        return lax.dot_general(inv_wide[...], stacked(x), (((1,), (1,)), ((), ())), preferred_element_type=F32)

    for i in range(8):
        value = solve(proj[128 * i : 128 * i + 128, :])
        part_a[128 * i : 128 * i + 128, :] = value
        own_rims[0, i : i + 1, :] = value[0:1, :]
        own_rims[1, i : i + 1, :] = value[127:128, :]

    def send_pair(turn):
        pltpu.make_async_remote_copy(
            src_ref=sums.at[turn, 0],
            dst_ref=pair.at[turn],
            send_sem=sum_sem.at[0, turn, 0],
            recv_sem=sum_sem.at[1, turn, 0],
            device_id=core_peer,
            device_id_type=MESH,
        ).start()

    def send_line(turn, stage, slot, device):
        pltpu.make_async_remote_copy(
            src_ref=sums.at[turn, stage],
            dst_ref=far.at[turn, pl.ds(slot, 1)],
            send_sem=sum_sem.at[0, turn, 1],
            recv_sem=sum_sem.at[1, turn, 1],
            device_id=device,
            device_id_type=MESH,
        ).start()

    def send_far(turn):
        for signs, away, _, flat, base in walk:
            def one_sign(sign, carry):
                dz = sign * (depth - 2 * away) + away
                for n, (dy, dx) in enumerate(flat):
                    other, there = peer_at(dy, dx, dz)
                    send_line(turn, 0, col, (other, there))
                    send_line(turn, 0, cols + base + sign * len(flat) + n, (1 - other, there))
                return carry

            if flat:
                lax.fori_loop(0, signs, one_sign, 0)

    def send_near(turn):
        for signs, away, flat, _, _ in walk:
            def one_sign(sign, carry):
                dz = sign * (depth - 2 * away) + away
                for dy, dx in flat:
                    send_line(turn, 1, col, peer_at(dy, dx, dz))
                return carry

            if flat:
                lax.fori_loop(0, signs, one_sign, 0)

    def wait_pair(turn, which):
        pltpu.make_async_copy(pair.at[turn], pair.at[turn], sum_sem.at[which, turn, 0]).wait()

    def wait_far(turn, which):
        got = far.at[turn, pl.ds(0, cols - 1 + extra)]
        pltpu.make_async_copy(got, got, sum_sem.at[which, turn, 1]).wait()

    first_col = jnp.where(col == 0, 1.0, 0.0).astype(F32)
    last_col = jnp.where(col == cols - 1, 1.0, 0.0).astype(F32)
    lanes = lax.broadcasted_iota(jnp.int32, (1, 128), 1)
    penalty, rescale, carry_c, carry_s = 1.0, 0.0, 0.0, 0.0

    def scalar(x):
        return x if isinstance(x, float) else x[0, 0]

    for turn in range(ITERS):
        start = turn == 0
        old_c, old_s = carry_c, carry_s
        pc_v = penalty * old_c
        sigma_v = 1.0 - pc_v * old_s
        share_v = 1.0 / (1.0 + penalty)
        carry_s = 1.0 + old_c * old_s
        bound, cut = scalar(WEIGHT_TV / penalty), scalar(WEIGHT_SPARSE / penalty)
        pc, sigma, scale_c = scalar(pc_v), scalar(sigma_v), scalar(old_c)
        share, ratio, scale_s = scalar(share_v), scalar(penalty * share_v), scalar(carry_s)
        factor = scalar(rescale)
        for copy in rim_copies + halo_copies:
            copy.wait()

        def combined(a, b):
            return a if start else a + factor * b

        def place(i, carry):
            value = combined(part_a[rows_of(i), :], part_b[rows_of(i), :])
            est[i, 0:128, :] = value
            return carry

        lax.fori_loop(0, 8, place, 0)
        if start:
            est[8, 0:128, :] = solve(halo[0, 0])
            rims = solve(jnp.concatenate([rim_left[0, 0:8, :], rim_right[0, 0:8, :]], axis=0))
            from_left, from_right = rims[0:8], rims[8:16]
            own_first, own_last = own_rims[0], own_rims[1]
        else:
            est[8, 0:128, :] = combined(halo[turn, 0], halo[turn, 1])
            own_first = combined(rim_send[turn, 0, 0:8, :], rim_send[turn, 0, 8:16, :])
            own_last = combined(rim_send[turn, 1, 0:8, :], rim_send[turn, 1, 8:16, :])
            from_right = combined(rim_right[turn, 0:8, :], rim_right[turn, 8:16, :])
            from_left = combined(rim_left[turn, 0:8, :], rim_left[turn, 8:16, :])
        from_right = jnp.where(last_col > 0.0, own_last, from_right)
        from_left = jnp.where(first_col > 0.0, own_first, from_left)
        for i in range(8):
            est[i, 128:129, :] = from_right[i : i + 1, :]

        g_diff = own_first - from_left
        g_sum = g_diff if start else g_diff + factor * ghost[...]
        g_dual = jnp.clip(g_sum, -bound, bound)
        g_arg = g_diff - (g_sum - g_dual)
        ghost[...] = g_dual
        for i in range(8):
            right_arg[i, 7:8, :] = g_arg[i : i + 1, :]
            right_dual[i, 7:8, :] = g_dual[i : i + 1, :]

        def update(i, off, half_row, gh_row, totals):
            at = pl.ds(off, CHUNK)
            shifted = pl.ds(off + 8, CHUNK)
            flat = pl.ds(pl.multiple_of(i * 128 + off, CHUNK), CHUNK)
            primal, dual, quad, cross, along = totals
            e = est[i, at, :]
            gh = gh_row[off : off + CHUNK, :]
            h = half_row[off : off + CHUNK, :].astype(F32)
            w = proj[flat, :]
            quad = quad + fold(h * gh)
            along = along + fold(h * w)
            if start:
                gram_mix[flat, :] = gh
            else:
                gy = gram_mix[flat, :]
                cross = cross + fold(h * gy)
                gram_mix[flat, :] = gh + scale_c * gy
            t = e if start else e + factor * sparse_dual[flat, :]
            fresh = jnp.maximum(t - cut, 0.0)
            gap = e - fresh
            primal = primal + fold(gap * gap)
            move = fresh if start else fresh - sparse_var[flat, :]
            dual = dual + fold(move * move)
            sparse_var[flat, :] = fresh
            sparse_dual[flat, :] = t - fresh
            d = est[i + 1, at, :] - e
            t = d if start else d + factor * down_dual[flat, :]
            clipped = jnp.clip(t, -bound, bound)
            fresh = t - clipped
            gap = d - fresh
            move = fresh if start else fresh - down_var[flat, :]
            weight = jnp.where((i == 7) & (row == 1), 0.0, 1.0).astype(F32)
            primal = primal + weight * fold(gap * gap)
            dual = dual + weight * fold(move * move)
            down_var[flat, :] = fresh
            down_dual[flat, :] = clipped
            down_arg[flat, :] = gap
            d = est[i, pl.ds(off + 1, CHUNK), :] - e
            t = d if start else d + factor * right_dual[i, shifted, :]
            clipped = jnp.clip(t, -bound, bound)
            fresh = t - clipped
            gap = d - fresh
            primal = primal + fold(gap * gap)
            move = fresh if start else fresh - right_var[flat, :]
            dual = dual + fold(move * move)
            right_var[flat, :] = fresh
            right_dual[i, shifted, :] = clipped
            right_arg[i, shifted, :] = gap
            return primal, dual, quad, cross, along

        def update_row(i, totals):
            half_row = est[i, 0:128, :].astype(BF16)
            gh_row = jnp.dot(
                jnp.concatenate([half_row, half_row], axis=1), gram2[...], preferred_element_type=F32
            )
            for off in range(0, 128, CHUNK):
                totals = update(i, off, half_row, gh_row, totals)
            return totals

        zero = jnp.zeros((8, 128), F32)
        primal, dual, quad, cross, along = lax.fori_loop(0, 8, update_row, (zero,) * 5)
        data = quad - 2.0 * along + square
        if not start:
            data = (quad - (2.0 * pc) * cross + (pc * pc) * old_quad) - (2.0 * sigma) * (along - pc * old_along)
            data = data + (sigma * sigma) * square
            quad = quad + (2.0 * scale_c) * cross + (scale_c * scale_c) * old_quad
            along = along + scale_c * old_along
        data = data * (share * share)
        old_quad, old_along = quad, along
        line_p = jnp.sum(primal + data, axis=0, keepdims=True)
        line_d = jnp.sum(dual, axis=0, keepdims=True)
        line_p = line_p + pltpu.roll(line_p, 64, 1)
        line_d = line_d + pltpu.roll(line_d, 64, 1)
        line = jnp.where(lanes < 64, line_p, line_d)
        sums[turn, 0] = line
        send_pair(turn)

        final = turn == ITERS - 1

        def rhs(i):
            flat = rows_of(i)
            above = rows_of(jnp.maximum(i - 1, 0))
            has_above = jnp.where(i > 0, 1.0, 0.0).astype(F32)
            w = proj[flat, :]
            we = gram_mix[flat, :] - scale_s * w
            at = pl.ds(8, 128)
            before = pl.ds(7, 128)
            adj_a = (has_above * down_arg[above, :] - down_arg[flat, :]) + (
                right_arg[i, before, :] - right_arg[i, at, :]
            )
            adj_b = (has_above * down_dual[above, :] - down_dual[flat, :]) + (
                right_dual[i, before, :] - right_dual[i, at, :]
            )
            a = w + ratio * we + sparse_var[flat, :] + PROX * est[i, 0:128, :] - adj_a
            b = -(share * we + sparse_dual[flat, :] + adj_b)
            return a, b

        def rim_rhs(j):
            def flat(field):
                return jnp.concatenate([field[128 * i + j : 128 * i + j + 1, :] for i in range(8)], axis=0)

            def deep(field, k):
                return jnp.concatenate([field[i, k : k + 1, :] for i in range(8)], axis=0)

            def adjoint(down, side):
                rows = flat(down)
                above = jnp.concatenate([jnp.zeros((1, 256), F32), rows[0:7, :]], axis=0)
                return (above - rows) + (deep(side, 7 + j) - deep(side, 8 + j))

            w = flat(proj)
            we = flat(gram_mix) - scale_s * w
            a = w + ratio * we + flat(sparse_var) + PROX * deep(est, j) - adjoint(down_arg, right_arg)
            b = -(share * we + flat(sparse_dual) + adjoint(down_dual, right_dual))
            return [a, b]

        def prepare(n, carry):
            i = 7 - n
            a, b = rhs(i)
            both = solve(jnp.concatenate([a, b], axis=0))
            part_a[rows_of(i), :] = both[0:128, :]
            part_b[rows_of(i), :] = both[128:256, :]
            return carry

        def prepare_final(i, carry):
            a, b = rhs(i)
            spot = jnp.where(flip, 7 - i, i)
            both = solve_turned(jnp.concatenate([a, b], axis=0))
            out_ref[pl.ds(spot, 256, stride=8), :] = both[:, 0:128]
            wide[pl.ds(spot, 256, stride=8), :] = both[:, 128:256]
            return carry

        work = prepare_final if final else prepare
        send_far(turn)
        wait_pair(turn, 1)
        line = line + pair[turn]
        sums[turn, 1] = line
        far[turn, pl.ds(col, 1), :] = line
        if not final:
            solved = solve(jnp.concatenate(rim_rhs(0) + rim_rhs(127), axis=0))
            rim_send[turn + 1, 0] = solved[0:16, :]
            rim_send[turn + 1, 1] = solved[16:32, :]
            rim_copies = send_rims(turn + 1)
        send_near(turn)
        work(0, 0)
        if not final:
            halo_copies = [send_halo(turn + 1, 0, part_a), send_halo(turn + 1, 1, part_b)]
        lax.fori_loop(1, 8, work, 0)
        wait_far(turn, 1)
        line = jnp.sum(far[turn, 0:cols, :], axis=0, keepdims=True)
        line = line + jnp.sum(far[turn, cols : cols + extra, :], axis=0, keepdims=True)
        total_p = jnp.sum(jnp.where(lanes < 64, line, 0.0), axis=1, keepdims=True)
        total_d = jnp.sum(jnp.where(lanes < 64, 0.0, line), axis=1, keepdims=True)
        root = jnp.sqrt(jnp.sqrt((total_p + 1.0) / (penalty * penalty * total_d + 1.0)))
        following = penalty * root
        rescale = penalty / following
        carry_c = rescale * share_v
        penalty = following

    factor = scalar(rescale)

    def finish(i, carry):
        at = pl.ds(pl.multiple_of(i * 256, 256), 256)
        out_ref[at, :] = out_ref[at, :] + factor * wide[at, :]
        return carry

    lax.fori_loop(0, 8, finish, 0)
    for turn in range(ITERS):
        wait_pair(turn, 0)
        wait_far(turn, 0)


def run(sizes, observed, shard):
    ys, xs, depth = sizes
    cols = ys * xs * depth
    planes = ys * xs
    extra = walk_of(sizes)[1]
    channels = 8 * cols
    field = pltpu.VMEM((1024, 256), F32)
    padded = pltpu.VMEM((8, PAD, 256), F32)
    rims = pltpu.VMEM((ITERS, 16, 256), F32)
    return pl.pallas_call(
        functools.partial(kernel, sizes),
        out_shape=jax.ShapeDtypeStruct((2048, 128), F32),
        in_specs=[pl.BlockSpec(memory_space=pltpu.HBM)] * 2,
        out_specs=VMEM,
        scratch_shapes=[
            pltpu.VMEM((channels, 8, 128), BF16),
            pltpu.VMEM((8, 256), BF16),
            pltpu.VMEM((max(channels * 8, 2048), 128), F32),
            pltpu.VMEM((1024, channels), BF16),
            pltpu.VMEM((16, 128), BF16),
            pltpu.VMEM((cols, 16, 128), BF16),
            pltpu.VMEM((channels, 256), BF16),
            pltpu.VMEM((72, 128), F32),
            pltpu.VMEM((256, 256), F32),
            pltpu.VMEM((512, 256), BF16),
            pltpu.VMEM((768, 256), BF16),
            pltpu.VMEM((256, 768), BF16),
            field,
            pltpu.VMEM((2, 8, 256), F32),
            pltpu.VMEM((9, PAD, 256), F32),
            field,
            field,
            pltpu.VMEM((ITERS, 2, 16, 256), F32),
            rims,
            rims,
            pltpu.VMEM((ITERS, 2, 128, 256), F32),
            pltpu.VMEM((8, 256), F32),
            field,
            field,
            field,
            field,
            field,
            field,
            padded,
            padded,
            field,
            pltpu.VMEM((ITERS, 2, 1, 128), F32),
            pltpu.VMEM((ITERS, 1, 128), F32),
            pltpu.VMEM((ITERS, cols + 8 * pl.cdiv(extra, 8), 128), F32),
            pltpu.SemaphoreType.DMA(()),
            pltpu.SemaphoreType.DMA(()),
            pltpu.SemaphoreType.DMA((5,)),
            pltpu.SemaphoreType.DMA((planes,)),
            pltpu.SemaphoreType.DMA((2, ITERS, 2)),
            pltpu.SemaphoreType.DMA((2, ITERS, 2)),
            pltpu.SemaphoreType.DMA((2, ITERS, 2)),
        ],
        compiler_params=pltpu.CompilerParams(
            collective_id=0, has_side_effects=True, vmem_limit_bytes=52 * 2**20
        ),
        name="unmix",
    )(observed, shard)


def on_device(sizes, observed, library):
    return run(sizes, observed, library).reshape(256, 8, 128)


def solution(mesh):
    sizes = (4, 4, 8) if mesh.shape["col"] == 128 else (2, 2, 2)
    return jax.shard_map(
        functools.partial(on_device, sizes),
        mesh=mesh,
        in_specs=(P(None, "row", "col"), P("col", None)),
        out_specs=P(None, "row", "col"),
        check_vma=False,
    )
```

```python
import functools

import jax
import jax.numpy as jnp
from jax import lax
from jax.experimental import pallas as pl
from jax.experimental.pallas import tpu as pltpu
from jax.sharding import PartitionSpec as P

ITERS = 3
PROX = 8.0
WEIGHT_SPARSE = 0.3
WEIGHT_TV = 1.0
MESH = pl.DeviceIdType.MESH
F32 = jnp.float32
BF16 = jnp.bfloat16
VMEM = pl.BlockSpec(memory_space=pltpu.VMEM)


def slot_of(col, depth, cols):
    plane, z = col // depth, col % depth
    half = depth // 2
    return (z % 2) * (cols // 2) + plane * half + z // 2


def dot_of(x, y):
    t = [a * b for a, b in zip(x, y)]
    while len(t) > 1:
        t = [t[i] + t[i + 1] if i + 1 < len(t) else t[i] for i in range(0, len(t), 2)]
    return t[0]

def symmetric_inverse(m):
    n = len(m)
    if n == 1:
        return [[1.0 / m[0][0]]]
    if n == 2:
        scale = 1.0 / (m[0][0] * m[1][1] - m[0][1] * m[0][1])
        off = -m[0][1] * scale
        return [[m[1][1] * scale, off], [off, m[0][0] * scale]]
    h = n // 2
    a = symmetric_inverse([r[:h] for r in m[:h]])
    b = [r[h:] for r in m[:h]]
    bt = [list(c) for c in zip(*b)]
    t = [[dot_of(a[i], bt[j]) for j in range(h)] for i in range(h)]
    tt = [list(c) for c in zip(*t)]
    s = [[None] * h for _ in range(h)]
    for i in range(h):
        for j in range(i, h):
            s[i][j] = s[j][i] = m[h + i][h + j] - dot_of(bt[i], tt[j])
    s = symmetric_inverse(s)
    u = [[dot_of(t[i], s[j]) for j in range(h)] for i in range(h)]
    top = [[None] * h for _ in range(h)]
    for i in range(h):
        for j in range(i, h):
            top[i][j] = top[j][i] = a[i][j] + dot_of(u[i], t[j])
    out = [[None] * n for _ in range(n)]
    for i in range(h):
        for j in range(h):
            out[i][j] = top[i][j]
            out[h + i][h + j] = s[i][j]
            out[i][h + j] = -u[i][j]
            out[h + j][i] = -u[i][j]
    return out

def eliminate(matrix, ref):
    size, step = 128, 8
    groups = [matrix[8 * g : 8 * g + 8, :] for g in range(size // 8)]
    lane = lax.broadcasted_iota(jnp.int32, (8, size), 1)
    place = lax.broadcasted_iota(jnp.int32, (8, size), 0)
    full = (8, size)
    for home, first in enumerate(range(0, size, step)):

        def cols_of(g):
            return [jnp.broadcast_to(g[:, first + a : first + a + 1], full) for a in range(step)]

        home_cols = cols_of(groups[home])
        ref[0:8, :] = groups[home]
        for b in range(step):
            ref[8 + 8 * b : 16 + 8 * b, :] = home_cols[b]
        line = [jnp.broadcast_to(ref[a : a + 1, :], full) for a in range(step)]
        pivot = [[None] * step for _ in range(step)]
        for a in range(step):
            for b in range(a, step):
                spot = 8 + 8 * b + a
                pivot[a][b] = pivot[b][a] = jnp.broadcast_to(ref[spot : spot + 1, :], full)
        turned = symmetric_inverse(pivot)
        inside = (lane >= first) & (lane < first + step)
        rows = [jnp.where(lane == first + a, 1.0, jnp.where(inside, 0.0, line[a])) for a in range(step)]
        fresh = [dot_of(turned[a], rows) for a in range(step)]
        nxt = []
        for g, group in enumerate(groups):
            if g == home:
                value = fresh[0]
                for a in range(1, step):
                    value = jnp.where(place == a, fresh[a], value)
            else:
                value = jnp.where(inside, 0.0, group) - dot_of(cols_of(group), fresh)
            nxt.append(value)
        groups = nxt
    return jnp.concatenate(groups, axis=0)


def exact_dot(a, b, dims):
    return lax.dot_general(a, b, (dims, ((), ())), precision=lax.Precision.HIGHEST, preferred_element_type=F32)


def split2(x):
    high = x.astype(BF16)
    return high, (x - high.astype(F32)).astype(BF16)


CHUNK = 16
PAD = 136


def fold(x):
    total = None
    for k in range(x.shape[0] // 8):
        for half in range(2):
            part = x[8 * k : 8 * k + 8, 128 * half : 128 * half + 128]
            total = part if total is None else total + part
    return total


def walk_of(sizes):
    ys, xs, depth = sizes
    limit = ys // 2 + xs // 2 + depth // 2 - 2

    def hops(dy, dx):
        return min(dy, ys - dy) + min(dx, xs - dx)

    plane = sorted(((dy, dx) for dy in range(ys) for dx in range(xs)), key=lambda o: -hops(*o))
    walk, extra = [], 0
    for away in range(depth // 2, -1, -1):
        signs = 1 if away in (0, depth // 2) else 2
        far = [o for o in plane if hops(*o) + away >= limit]
        near = [o for o in plane if hops(*o) + away < limit and (away or o != (0, 0))]
        walk.append((signs, away, near, far, extra))
        extra += signs * len(far)
    return walk, extra


def kernel(
    sizes,
    obs_ref,
    shard_ref,
    out_ref,
    obs,
    own_shard,
    wide,
    turned_obs,
    packed,
    shards,
    lib,
    work_rows,
    inverse,
    gram2,
    inv3,
    inv_wide,
    proj,
    own_rims,
    est,
    part_a,
    part_b,
    rim_send,
    rim_left,
    rim_right,
    halo,
    ghost,
    sparse_var,
    sparse_dual,
    down_var,
    down_dual,
    down_arg,
    right_var,
    right_dual,
    right_arg,
    gram_mix,
    sums,
    pair,
    far,
    obs_sem,
    shard_sem,
    gather_sem,
    plane_sem,
    halo_sem,
    rim_sem,
    sum_sem,
):
    ys, xs, depth = sizes
    planes, half = ys * xs, depth // 2
    cols = planes * depth
    channels = 8 * cols
    row, col = lax.axis_index("row"), lax.axis_index("col")
    plane, z = lax.div(col, depth), lax.rem(col, depth)
    y, x = lax.div(plane, xs), lax.rem(plane, xs)
    parity = lax.rem(z, 2)
    flip = row == 1
    core_peer = (1 - row, col)
    walk, extra = walk_of(sizes)
    left = (row, lax.rem(col + cols - 1, cols))
    right = (row, lax.rem(col + 1, cols))

    columns = [
        [(lax.rem(y + dy, ys) * xs + lax.rem(x + dx, xs)) * depth for dx in range(xs)] for dy in range(ys)
    ]

    def peer_at(dy, dx, dz):
        return (row, columns[dy][dx] + lax.rem(z + dz, depth))

    def z_peer(step):
        return peer_at(0, 0, step)

    def plane_peer(step):
        return peer_at(step // xs, step % xs, 0)

    obs_copy = pltpu.make_async_copy(obs_ref, obs, obs_sem)
    obs_copy.start()
    shard_copy = pltpu.make_async_copy(shard_ref, own_shard, shard_sem)
    shard_copy.start()
    barrier = pltpu.get_barrier_semaphore()
    peers = [z_peer(n) for n in range(1, depth)] + [plane_peer(n) for n in range(1, planes)] + [core_peer]
    for peer in peers:
        pl.semaphore_signal(barrier, inc=1, device_id=peer, device_id_type=MESH)
    shard_copy.wait()
    shard = own_shard[...].astype(F32)
    packed[...] = jnp.concatenate([shard[:, :128], shard[:, 128:]], axis=0).astype(BF16)
    mine = parity * (cols // 2) + plane * half + lax.div(z, 2)
    pl.semaphore_wait(barrier, len(peers))

    @pl.when(row == parity)
    def _():
        for step in range(1, depth):
            pltpu.make_async_remote_copy(
                src_ref=packed,
                dst_ref=shards.at[mine],
                send_sem=gather_sem.at[0],
                recv_sem=gather_sem.at[1],
                device_id=z_peer(step),
                device_id_type=MESH,
            ).start()
        shards[mine] = packed[...]

    obs_copy.wait()

    def widen(k, total):
        base = pl.multiple_of(k * 16, 16)
        part = obs[pl.ds(base, 16)].astype(F32)
        wide[pl.ds(pl.multiple_of(base * 8, 128), 128), :] = part.reshape(128, 128)
        return total + jnp.sum(part * part, axis=0)

    square = lax.fori_loop(0, channels // 16, widen, jnp.zeros((8, 128), F32))
    def turn_rows(i, carry):
        source = jnp.where(flip, 7 - i, i)
        part = wide[pl.ds(source, channels, stride=8), :]
        turned_obs[pl.ds(pl.multiple_of(i * 128, 128), 128), :] = part.T.astype(BF16)
        return carry

    lax.fori_loop(0, 3, turn_rows, 0)

    @pl.when(row == parity)
    def _():
        if half > 1:
            got = shards.at[pl.ds(0, half - 1)]
            pltpu.make_async_copy(got, got, gather_sem.at[1]).wait()

    @pl.when(row != parity)
    def _():
        got = shards.at[pl.ds(0, half)]
        pltpu.make_async_copy(got, got, gather_sem.at[1]).wait()

    def block_of(dy, dx):
        other = lax.rem(y + ys - dy, ys) * xs + lax.rem(x + xs - dx, xs)
        return shards.at[pl.ds(row * (cols // 2) + other * half, half)]

    def pass_over(block):
        pltpu.make_async_remote_copy(
            src_ref=block,
            dst_ref=block,
            send_sem=gather_sem.at[3],
            recv_sem=gather_sem.at[4],
            device_id=core_peer,
            device_id_type=MESH,
        ).start()

    block = block_of(0, 0)
    for step in range(1, planes):
        pltpu.make_async_remote_copy(
            src_ref=block,
            dst_ref=block,
            send_sem=gather_sem.at[2],
            recv_sem=plane_sem.at[step],
            device_id=plane_peer(step),
            device_id_type=MESH,
        ).start()
    pass_over(block)
    lax.fori_loop(3, 8, turn_rows, 0)
    nearest = sorted(range(1, planes), key=lambda n: min(n // xs, ys - n // xs) + min(n % xs, xs - n % xs))
    for step in nearest:
        got = block_of(step // xs, step % xs)
        pltpu.make_async_copy(got, got, plane_sem.at[step]).wait()
        pass_over(got)
    other_half = shards.at[pl.ds((1 - row) * (cols // 2), cols // 2)]
    pltpu.make_async_copy(other_half, other_half, gather_sem.at[4]).wait()

    @pl.when(row == parity)
    def _():
        sent = shards.at[pl.ds(0, depth - 1)]
        pltpu.make_async_copy(sent, sent, gather_sem.at[0]).wait()

    sent = shards.at[pl.ds(0, half * (planes - 1))]
    pltpu.make_async_copy(sent, sent, gather_sem.at[2]).wait()
    pltpu.make_async_copy(other_half, other_half, gather_sem.at[3]).wait()

    for two in range(cols // 2):
        one = shards[slot_of(2 * two, depth, cols)].astype(F32)
        other = shards[slot_of(2 * two + 1, depth, cols)].astype(F32)
        lib[16 * two : 16 * two + 16, 0:128] = jnp.concatenate([one[0:8], other[0:8]], axis=0).astype(BF16)
        lib[16 * two : 16 * two + 16, 128:256] = jnp.concatenate([one[8:16], other[8:16]], axis=0).astype(BF16)

    def rows_of(x):
        return pl.ds(pl.multiple_of(x * 128, 128), 128)

    def send_halo(turn, slot, field):
        copy = pltpu.make_async_remote_copy(
            src_ref=field.at[rows_of(7)],
            dst_ref=halo.at[turn, slot],
            send_sem=halo_sem.at[0, turn, slot],
            recv_sem=halo_sem.at[1, turn, slot],
            device_id=core_peer,
            device_id_type=MESH,
        )
        copy.start()
        return copy

    def send_rims(turn):
        used = 8 if turn == 0 else 16
        to_left = pltpu.make_async_remote_copy(
            src_ref=rim_send.at[turn, 0, pl.ds(0, used)],
            dst_ref=rim_right.at[turn, pl.ds(0, used)],
            send_sem=rim_sem.at[0, turn, 0],
            recv_sem=rim_sem.at[1, turn, 0],
            device_id=left,
            device_id_type=MESH,
        )
        to_right = pltpu.make_async_remote_copy(
            src_ref=rim_send.at[turn, 1, pl.ds(0, used)],
            dst_ref=rim_left.at[turn, pl.ds(0, used)],
            send_sem=rim_sem.at[0, turn, 1],
            recv_sem=rim_sem.at[1, turn, 1],
            device_id=right,
            device_id_type=MESH,
        )
        to_left.start()
        to_right.start()
        return [to_left, to_right]

    library = lib[...]
    gram = lax.dot_general(library, library, (((0,), (0,)), ((), ())), preferred_element_type=F32)
    high, low = split2(gram)
    gram2[0:256, :] = high
    gram2[256:512, :] = low
    same = lax.broadcasted_iota(jnp.int32, (256, 256), 0) == lax.broadcasted_iota(jnp.int32, (256, 256), 1)
    system = gram + jnp.where(same, 1.0 + PROX, 0.0)
    for i in range(8):
        value = jnp.dot(turned_obs[128 * i : 128 * i + 128, :], lib[...], preferred_element_type=F32)
        proj[128 * i : 128 * i + 128, :] = value
        rim_send[0, 0, i : i + 1, :] = value[0:1, :]
        rim_send[0, 1, i : i + 1, :] = value[127:128, :]

    first_inverse = eliminate(system[:128, :128], work_rows)
    rim_copies = send_rims(0)
    halo_copies = [send_halo(0, 0, proj)]
    lead = exact_dot(first_inverse, system[:128, 128:], ((1,), (0,)))
    last_inverse = eliminate(
        system[128:, 128:] - exact_dot(system[128:, :128], lead, ((1,), (0,))), work_rows
    )
    corner = -exact_dot(lead, last_inverse, ((1,), (0,)))
    inverse[0:128, 0:128] = first_inverse - exact_dot(corner, lead, ((1,), (1,)))
    inverse[0:128, 128:256] = corner
    inverse[128:256, 0:128] = -exact_dot(last_inverse, lead, ((1,), (1,)))
    inverse[128:256, 128:256] = last_inverse
    high, low = split2(inverse[...])
    inv3[0:256, :] = high
    inv3[256:512, :] = low
    inv3[512:768, :] = high
    inv_wide[:, 0:256] = high
    inv_wide[:, 256:512] = low
    inv_wide[:, 512:768] = high

    def stacked(x):
        one, two = split2(x)
        return jnp.concatenate([one, one, two], axis=1)

    def solve(x):
        return jnp.dot(stacked(x), inv3[...], preferred_element_type=F32)

    def solve_turned(x):
        return lax.dot_general(inv_wide[...], stacked(x), (((1,), (1,)), ((), ())), preferred_element_type=F32)

    for i in range(8):
        value = solve(proj[128 * i : 128 * i + 128, :])
        part_a[128 * i : 128 * i + 128, :] = value
        own_rims[0, i : i + 1, :] = value[0:1, :]
        own_rims[1, i : i + 1, :] = value[127:128, :]

    def send_pair(turn):
        pltpu.make_async_remote_copy(
            src_ref=sums.at[turn, 0],
            dst_ref=pair.at[turn],
            send_sem=sum_sem.at[0, turn, 0],
            recv_sem=sum_sem.at[1, turn, 0],
            device_id=core_peer,
            device_id_type=MESH,
        ).start()

    def send_line(turn, stage, slot, device):
        pltpu.make_async_remote_copy(
            src_ref=sums.at[turn, stage],
            dst_ref=far.at[turn, pl.ds(slot, 1)],
            send_sem=sum_sem.at[0, turn, 1],
            recv_sem=sum_sem.at[1, turn, 1],
            device_id=device,
            device_id_type=MESH,
        ).start()

    def send_far(turn):
        for signs, away, _, flat, base in walk:
            def one_sign(sign, carry):
                dz = sign * (depth - 2 * away) + away
                for n, (dy, dx) in enumerate(flat):
                    other, there = peer_at(dy, dx, dz)
                    send_line(turn, 0, col, (other, there))
                    send_line(turn, 0, cols + base + sign * len(flat) + n, (1 - other, there))
                return carry

            if flat:
                lax.fori_loop(0, signs, one_sign, 0)

    def send_near(turn):
        for signs, away, flat, _, _ in walk:
            def one_sign(sign, carry):
                dz = sign * (depth - 2 * away) + away
                for dy, dx in flat:
                    send_line(turn, 1, col, peer_at(dy, dx, dz))
                return carry

            if flat:
                lax.fori_loop(0, signs, one_sign, 0)

    def wait_pair(turn, which):
        pltpu.make_async_copy(pair.at[turn], pair.at[turn], sum_sem.at[which, turn, 0]).wait()

    def wait_far(turn, which):
        got = far.at[turn, pl.ds(0, cols - 1 + extra)]
        pltpu.make_async_copy(got, got, sum_sem.at[which, turn, 1]).wait()

    first_col = jnp.where(col == 0, 1.0, 0.0).astype(F32)
    last_col = jnp.where(col == cols - 1, 1.0, 0.0).astype(F32)
    lanes = lax.broadcasted_iota(jnp.int32, (1, 128), 1)
    penalty, rescale, carry_c, carry_s = 1.0, 0.0, 0.0, 0.0

    def scalar(x):
        return x if isinstance(x, float) else x[0, 0]

    for turn in range(ITERS):
        start = turn == 0
        old_c, old_s = carry_c, carry_s
        pc_v = penalty * old_c
        sigma_v = 1.0 - pc_v * old_s
        share_v = 1.0 / (1.0 + penalty)
        carry_s = 1.0 + old_c * old_s
        bound, cut = scalar(WEIGHT_TV / penalty), scalar(WEIGHT_SPARSE / penalty)
        pc, sigma, scale_c = scalar(pc_v), scalar(sigma_v), scalar(old_c)
        share, ratio, scale_s = scalar(share_v), scalar(penalty * share_v), scalar(carry_s)
        factor = scalar(rescale)
        for copy in rim_copies + halo_copies:
            copy.wait()

        def combined(a, b):
            return a if start else a + factor * b

        def place(i, carry):
            value = combined(part_a[rows_of(i), :], part_b[rows_of(i), :])
            est[i, 0:128, :] = value
            return carry

        lax.fori_loop(0, 8, place, 0)
        if start:
            est[8, 0:128, :] = solve(halo[0, 0])
            rims = solve(jnp.concatenate([rim_left[0, 0:8, :], rim_right[0, 0:8, :]], axis=0))
            from_left, from_right = rims[0:8], rims[8:16]
            own_first, own_last = own_rims[0], own_rims[1]
        else:
            est[8, 0:128, :] = combined(halo[turn, 0], halo[turn, 1])
            own_first = combined(rim_send[turn, 0, 0:8, :], rim_send[turn, 0, 8:16, :])
            own_last = combined(rim_send[turn, 1, 0:8, :], rim_send[turn, 1, 8:16, :])
            from_right = combined(rim_right[turn, 0:8, :], rim_right[turn, 8:16, :])
            from_left = combined(rim_left[turn, 0:8, :], rim_left[turn, 8:16, :])
        from_right = jnp.where(last_col > 0.0, own_last, from_right)
        from_left = jnp.where(first_col > 0.0, own_first, from_left)
        for i in range(8):
            est[i, 128:129, :] = from_right[i : i + 1, :]

        g_diff = own_first - from_left
        g_sum = g_diff if start else g_diff + factor * ghost[...]
        g_dual = jnp.clip(g_sum, -bound, bound)
        g_arg = g_diff - (g_sum - g_dual)
        ghost[...] = g_dual
        for i in range(8):
            right_arg[i, 7:8, :] = g_arg[i : i + 1, :]
            right_dual[i, 7:8, :] = g_dual[i : i + 1, :]

        def update(i, off, half_row, gh_row, totals):
            at = pl.ds(off, CHUNK)
            shifted = pl.ds(off + 8, CHUNK)
            flat = pl.ds(pl.multiple_of(i * 128 + off, CHUNK), CHUNK)
            primal, dual, quad, cross, along = totals
            e = est[i, at, :]
            gh = gh_row[off : off + CHUNK, :]
            h = half_row[off : off + CHUNK, :].astype(F32)
            w = proj[flat, :]
            quad = quad + fold(h * gh)
            along = along + fold(h * w)
            if start:
                gram_mix[flat, :] = gh
            else:
                gy = gram_mix[flat, :]
                cross = cross + fold(h * gy)
                gram_mix[flat, :] = gh + scale_c * gy
            t = e if start else e + factor * sparse_dual[flat, :]
            fresh = jnp.maximum(t - cut, 0.0)
            gap = e - fresh
            primal = primal + fold(gap * gap)
            move = fresh if start else fresh - sparse_var[flat, :]
            dual = dual + fold(move * move)
            sparse_var[flat, :] = fresh
            sparse_dual[flat, :] = t - fresh
            d = est[i + 1, at, :] - e
            t = d if start else d + factor * down_dual[flat, :]
            clipped = jnp.clip(t, -bound, bound)
            fresh = t - clipped
            gap = d - fresh
            move = fresh if start else fresh - down_var[flat, :]
            weight = jnp.where((i == 7) & (row == 1), 0.0, 1.0).astype(F32)
            primal = primal + weight * fold(gap * gap)
            dual = dual + weight * fold(move * move)
            down_var[flat, :] = fresh
            down_dual[flat, :] = clipped
            down_arg[flat, :] = gap
            d = est[i, pl.ds(off + 1, CHUNK), :] - e
            t = d if start else d + factor * right_dual[i, shifted, :]
            clipped = jnp.clip(t, -bound, bound)
            fresh = t - clipped
            gap = d - fresh
            primal = primal + fold(gap * gap)
            move = fresh if start else fresh - right_var[flat, :]
            dual = dual + fold(move * move)
            right_var[flat, :] = fresh
            right_dual[i, shifted, :] = clipped
            right_arg[i, shifted, :] = gap
            return primal, dual, quad, cross, along

        def update_row(i, totals):
            half_row = est[i, 0:128, :].astype(BF16)
            gh_row = jnp.dot(
                jnp.concatenate([half_row, half_row], axis=1), gram2[...], preferred_element_type=F32
            )
            for off in range(0, 128, CHUNK):
                totals = update(i, off, half_row, gh_row, totals)
            return totals

        zero = jnp.zeros((8, 128), F32)
        primal, dual, quad, cross, along = lax.fori_loop(0, 8, update_row, (zero,) * 5)
        data = quad - 2.0 * along + square
        if not start:
            data = (quad - (2.0 * pc) * cross + (pc * pc) * old_quad) - (2.0 * sigma) * (along - pc * old_along)
            data = data + (sigma * sigma) * square
            quad = quad + (2.0 * scale_c) * cross + (scale_c * scale_c) * old_quad
            along = along + scale_c * old_along
        data = data * (share * share)
        old_quad, old_along = quad, along
        line_p = jnp.sum(primal + data, axis=0, keepdims=True)
        line_d = jnp.sum(dual, axis=0, keepdims=True)
        line_p = line_p + pltpu.roll(line_p, 64, 1)
        line_d = line_d + pltpu.roll(line_d, 64, 1)
        line = jnp.where(lanes < 64, line_p, line_d)
        sums[turn, 0] = line
        send_pair(turn)

        final = turn == ITERS - 1

        def rhs(i):
            flat = rows_of(i)
            above = rows_of(jnp.maximum(i - 1, 0))
            has_above = jnp.where(i > 0, 1.0, 0.0).astype(F32)
            w = proj[flat, :]
            we = gram_mix[flat, :] - scale_s * w
            at = pl.ds(8, 128)
            before = pl.ds(7, 128)
            adj_a = (has_above * down_arg[above, :] - down_arg[flat, :]) + (
                right_arg[i, before, :] - right_arg[i, at, :]
            )
            adj_b = (has_above * down_dual[above, :] - down_dual[flat, :]) + (
                right_dual[i, before, :] - right_dual[i, at, :]
            )
            a = w + ratio * we + sparse_var[flat, :] + PROX * est[i, 0:128, :] - adj_a
            b = -(share * we + sparse_dual[flat, :] + adj_b)
            return a, b

        def rim_rhs(j):
            def flat(field):
                return jnp.concatenate([field[128 * i + j : 128 * i + j + 1, :] for i in range(8)], axis=0)

            def deep(field, k):
                return jnp.concatenate([field[i, k : k + 1, :] for i in range(8)], axis=0)

            def adjoint(down, side):
                rows = flat(down)
                above = jnp.concatenate([jnp.zeros((1, 256), F32), rows[0:7, :]], axis=0)
                return (above - rows) + (deep(side, 7 + j) - deep(side, 8 + j))

            w = flat(proj)
            we = flat(gram_mix) - scale_s * w
            a = w + ratio * we + flat(sparse_var) + PROX * deep(est, j) - adjoint(down_arg, right_arg)
            b = -(share * we + flat(sparse_dual) + adjoint(down_dual, right_dual))
            return [a, b]

        def prepare(n, carry):
            i = 7 - n
            a, b = rhs(i)
            both = solve(jnp.concatenate([a, b], axis=0))
            part_a[rows_of(i), :] = both[0:128, :]
            part_b[rows_of(i), :] = both[128:256, :]
            return carry

        def prepare_final(i, carry):
            a, b = rhs(i)
            spot = jnp.where(flip, 7 - i, i)
            both = solve_turned(jnp.concatenate([a, b], axis=0))
            out_ref[pl.ds(spot, 256, stride=8), :] = both[:, 0:128]
            wide[pl.ds(spot, 256, stride=8), :] = both[:, 128:256]
            return carry

        work = prepare_final if final else prepare
        send_far(turn)
        wait_pair(turn, 1)
        line = line + pair[turn]
        sums[turn, 1] = line
        far[turn, pl.ds(col, 1), :] = line
        if not final:
            solved = solve(jnp.concatenate(rim_rhs(0) + rim_rhs(127), axis=0))
            rim_send[turn + 1, 0] = solved[0:16, :]
            rim_send[turn + 1, 1] = solved[16:32, :]
            rim_copies = send_rims(turn + 1)
        send_near(turn)
        work(0, 0)
        if not final:
            halo_copies = [send_halo(turn + 1, 0, part_a), send_halo(turn + 1, 1, part_b)]
        lax.fori_loop(1, 8, work, 0)
        wait_far(turn, 1)
        line = jnp.sum(far[turn, 0:cols, :], axis=0, keepdims=True)
        line = line + jnp.sum(far[turn, cols : cols + extra, :], axis=0, keepdims=True)
        total_p = jnp.sum(jnp.where(lanes < 64, line, 0.0), axis=1, keepdims=True)
        total_d = jnp.sum(jnp.where(lanes < 64, 0.0, line), axis=1, keepdims=True)
        root = jnp.sqrt(jnp.sqrt((total_p + 1.0) / (penalty * penalty * total_d + 1.0)))
        following = penalty * root
        rescale = penalty / following
        carry_c = rescale * share_v
        penalty = following

    factor = scalar(rescale)

    def finish(i, carry):
        at = pl.ds(pl.multiple_of(i * 256, 256), 256)
        out_ref[at, :] = out_ref[at, :] + factor * wide[at, :]
        return carry

    lax.fori_loop(0, 8, finish, 0)
    for turn in range(ITERS):
        wait_pair(turn, 0)
        wait_far(turn, 0)


def run(sizes, observed, shard):
    ys, xs, depth = sizes
    cols = ys * xs * depth
    planes = ys * xs
    extra = walk_of(sizes)[1]
    channels = 8 * cols
    field = pltpu.VMEM((1024, 256), F32)
    padded = pltpu.VMEM((8, PAD, 256), F32)
    rims = pltpu.VMEM((ITERS, 16, 256), F32)
    return pl.pallas_call(
        functools.partial(kernel, sizes),
        out_shape=jax.ShapeDtypeStruct((2048, 128), F32),
        in_specs=[pl.BlockSpec(memory_space=pltpu.HBM)] * 2,
        out_specs=VMEM,
        scratch_shapes=[
            pltpu.VMEM((channels, 8, 128), BF16),
            pltpu.VMEM((8, 256), BF16),
            pltpu.VMEM((max(channels * 8, 2048), 128), F32),
            pltpu.VMEM((1024, channels), BF16),
            pltpu.VMEM((16, 128), BF16),
            pltpu.VMEM((cols, 16, 128), BF16),
            pltpu.VMEM((channels, 256), BF16),
            pltpu.VMEM((72, 128), F32),
            pltpu.VMEM((256, 256), F32),
            pltpu.VMEM((512, 256), BF16),
            pltpu.VMEM((768, 256), BF16),
            pltpu.VMEM((256, 768), BF16),
            field,
            pltpu.VMEM((2, 8, 256), F32),
            pltpu.VMEM((9, PAD, 256), F32),
            field,
            field,
            pltpu.VMEM((ITERS, 2, 16, 256), F32),
            rims,
            rims,
            pltpu.VMEM((ITERS, 2, 128, 256), F32),
            pltpu.VMEM((8, 256), F32),
            field,
            field,
            field,
            field,
            field,
            field,
            padded,
            padded,
            field,
            pltpu.VMEM((ITERS, 2, 1, 128), F32),
            pltpu.VMEM((ITERS, 1, 128), F32),
            pltpu.VMEM((ITERS, cols + 8 * pl.cdiv(extra, 8), 128), F32),
            pltpu.SemaphoreType.DMA(()),
            pltpu.SemaphoreType.DMA(()),
            pltpu.SemaphoreType.DMA((5,)),
            pltpu.SemaphoreType.DMA((planes,)),
            pltpu.SemaphoreType.DMA((2, ITERS, 2)),
            pltpu.SemaphoreType.DMA((2, ITERS, 2)),
            pltpu.SemaphoreType.DMA((2, ITERS, 2)),
        ],
        compiler_params=pltpu.CompilerParams(
            collective_id=0, has_side_effects=True, vmem_limit_bytes=52 * 2**20
        ),
        name="unmix",
    )(observed, shard)


def on_device(sizes, observed, library):
    return run(sizes, observed, library).reshape(256, 8, 128)


def solution(mesh):
    sizes = (4, 4, 8) if mesh.shape["col"] == 128 else (2, 2, 2)
    return jax.shard_map(
        functools.partial(on_device, sizes),
        mesh=mesh,
        in_specs=(P(None, "row", "col"), P("col", None)),
        out_specs=P(None, "row", "col"),
        check_vma=False,
    )
```
